32 devices in a mesh: cfg: 1, gz: 32 (over z, y, x, core).
Axes of the slice: x: 2, y: 2, z: 4, core: 2. Of those that a mesh axis runs over, the one named last changes fastest.
Arguments:
- adjoint: float32 [128, 2, 3, 8, 128], P(('cfg', 'gz')), may hold values from -6 to 6
- flowed: float32 [128, 3, 4, 2, 3, 3, 128], P(('cfg', 'gz')), may hold values from -2.5 to 2.5
- source_slice: int32 [1], P('cfg'), may hold values from 12 to 19
- band_width: int32 [1], P('cfg'), may hold values from 8 to 15
- flow_steps: int32 [1], P('cfg'), may hold values from 1 to 4
Outputs:
- pulled_back: float32 [128, 2, 3, 8, 128], P(('cfg', 'gz'))
The draws below stay inside these ranges and needn't reach their ends.
All inputs are finite; a program needn't handle non-finite values.
Results may differ from the reference program's by a relative error of at most 0.00002.
Values sent between devices are 32-bit elements; how exact they have to be, the bound alone decides.
No kernel may reach another device: no remote copies, remote signals or barrier semaphores. Data moves between devices by JAX's collectives and lax.ppermute only.
A program may use at most 64 MiB of HBM per device.

```python
import jax
import jax.numpy as jnp

BAND = 32
LX = 8
NROWS = 128
VECTORS = 8
SITES = 128


def level_of(own_key, shape, split, least, high):
    gain, own = 1.0, jax.random.fold_in(own_key, 6)
    for position, shards_of in split:
        steps = jnp.exp(jax.random.uniform(jax.random.fold_in(own, position), (shards_of,), jnp.float32, least / len(split), high / len(split)))
        gain = gain * jnp.repeat(steps, shape[position] // shards_of).reshape([-1 if axis == position else 1 for axis in range(len(shape))])
    return gain


def scatter_about(stream_key, dims, deviation, limit, shards=(), held_as=jnp.bfloat16):
    gain = level_of(stream_key, dims, shards, -0.22, 0.18) if shards else 1.0
    array = jax.random.normal(stream_key, dims, jnp.float32) * deviation * gain
    return jnp.minimum(jnp.maximum(array, -limit), limit).astype(held_as)


def setup_inputs(seed: int = 0, part: int = 0) -> dict:
    splits = jax.random.split(jax.random.key(seed), 6)
    part_splits = jax.random.split(jax.random.fold_in(splits[5], part), 6)
    adjoint = scatter_about(part_splits[0], (NROWS, 2, 3, VECTORS, SITES), 1.0, 6.0, ((0, 32),), jnp.float32)
    flowed = scatter_about(part_splits[1], (NROWS, 3, 4, 2, 3, 3, SITES), 6 ** -0.5, 2.5, ((0, 32),), jnp.float32)
    source_slice = jax.random.randint(part_splits[2], (1,), BAND // 2 - 4, BAND // 2 + 4).astype(jnp.int32)
    band_width = jax.random.randint(part_splits[3], (1,), BAND // 4, BAND // 2).astype(jnp.int32)
    flow_steps = jax.random.randint(part_splits[4], (1,), 1, 5).astype(jnp.int32)
    return dict(adjoint=adjoint, flowed=flowed, source_slice=source_slice, band_width=band_width, flow_steps=flow_steps)


def multiply(matrix, spinor, dagger):
    real_u = matrix[:, 0]
    imag_u = matrix[:, 1]
    real_v = spinor[:, 0]
    imag_v = spinor[:, 1]
    real_rows = []
    imag_rows = []
    for row_a in range(3):
        real_sum = None
        imag_sum = None
        for col_b in range(3):
            if dagger:
                entry_re = real_u[:, col_b, row_a][:, None, :]
                entry_im = -imag_u[:, col_b, row_a][:, None, :]
            else:
                entry_re = real_u[:, row_a, col_b][:, None, :]
                entry_im = imag_u[:, row_a, col_b][:, None, :]
            term_re = entry_re * real_v[:, col_b] - entry_im * imag_v[:, col_b]
            term_im = entry_re * imag_v[:, col_b] + entry_im * real_v[:, col_b]
            real_sum = term_re if real_sum is None else real_sum + term_re
            imag_sum = term_im if imag_sum is None else imag_sum + term_im
        real_rows.append(real_sum)
        imag_rows.append(imag_sum)
    return jnp.stack([jnp.stack(real_rows, axis=1), jnp.stack(imag_rows, axis=1)], axis=1)


def planar_terms(spinor, set_links):
    column_pos = jnp.arange(spinor.shape[-1], dtype=jnp.int32) % LX
    at_last = column_pos == LX - 1
    at_first = column_pos == 0
    ahead_x = multiply(set_links[:, 0], jnp.where(at_last, jnp.roll(spinor, LX - 1, -1), jnp.roll(spinor, -1, -1)), False)
    hop_x = multiply(set_links[:, 0], spinor, True)
    behind_x = jnp.where(at_first, jnp.roll(hop_x, -(LX - 1), -1), jnp.roll(hop_x, 1, -1))
    ahead_y = multiply(set_links[:, 1], jnp.roll(spinor, -LX, -1), False)
    behind_y = jnp.roll(multiply(set_links[:, 1], spinor, True), LX, -1)
    return ahead_x + behind_x + ahead_y + behind_y


def laplace(spinor, set_links, inside, not_last, not_first, step_size):
    summed = planar_terms(spinor, set_links)
    ahead_z = multiply(set_links[:, 2], jnp.roll(spinor, -BAND, 0), False)
    behind_z = jnp.roll(multiply(set_links[:, 2], spinor, True), BAND, 0)
    ahead_t = multiply(set_links[:, 3], jnp.roll(spinor, -1, 0), False) * not_last
    behind_t = jnp.roll(multiply(set_links[:, 3], spinor, True), 1, 0) * not_first
    summed = summed + ahead_z + behind_z + ahead_t + behind_t - 8.0 * spinor
    return inside * (step_size * summed)


def reference(adjoint, flowed, source_slice, band_width, flow_steps):
    slice_pos = jnp.arange(adjoint.shape[0], dtype=jnp.int32) % BAND
    shape_rows = (adjoint.shape[0], 1, 1, 1, 1)
    distance = (slice_pos - source_slice[0]).astype(jnp.float32) / band_width[0].astype(jnp.float32)
    inside = (1.0 / (1.0 + distance * distance)).reshape(shape_rows)
    not_last = (slice_pos != BAND - 1).astype(jnp.float32).reshape(shape_rows)
    not_first = (slice_pos != 0).astype(jnp.float32).reshape(shape_rows)
    step_size = 0.25 / flow_steps[0].astype(jnp.float32)

    def apply(spinor, link_set):
        return laplace(spinor, flowed[:, link_set], inside, not_last, not_first, step_size)

    start = inside * adjoint
    third = 0.75 * apply(start, 2)
    second = start + (8.0 / 9.0) * apply(third, 1)
    return second + third + apply(0.25 * second - (2.0 / 9.0) * third, 0)
```

```python
import functools

import jax
import jax.numpy as jnp
from jax import lax
from jax.experimental import pallas as pl
from jax.experimental.pallas import tpu as pltpu
from jax.sharding import PartitionSpec as P

BAND = 32
LX = 8
SETS = 3
MUS = 4
ENTRIES = 18


def load_field(ref, row):
    return [[ref[row, c, a] for a in range(3)] for c in range(2)]


def store_field(ref, row, field):
    for c in range(2):
        for a in range(3):
            ref[row, c, a] = field[c][a]


def combine(function, *fields):
    return [[function(*(f[c][a] for f in fields)) for a in range(3)] for c in range(2)]


def entry(links_ref, row, link_set, mu, a, b, c, shape):
    index = ((row * SETS + link_set) * MUS + mu) * ENTRIES + (a * 3 + b) * 2 + c
    return jnp.broadcast_to(links_ref[pl.ds(index, 1), :], shape)


def transport(links_ref, row, link_set, mu, ahead, here):
    forward = [[None] * 3, [None] * 3]
    backward = [[None] * 3, [None] * 3]
    shape = (ahead if ahead is not None else here)[0][0].shape

    def add(total, c, a, value):
        total[c][a] = value if total[c][a] is None else total[c][a] + value

    for a in range(3):
        for b in range(3):
            real = entry(links_ref, row, link_set, mu, a, b, 0, shape)
            imag = entry(links_ref, row, link_set, mu, a, b, 1, shape)
            if ahead is not None:
                add(forward, 0, a, real * ahead[0][b] - imag * ahead[1][b])
                add(forward, 1, a, real * ahead[1][b] + imag * ahead[0][b])
            if here is not None:
                add(backward, 0, b, real * here[0][a] + imag * here[1][a])
                add(backward, 1, b, real * here[1][a] - imag * here[0][a])
    return forward, backward


def roll(plane, by):
    return pltpu.roll(plane, by % plane.shape[-1], plane.ndim - 1)


def taper(scalars, row):
    source, width, steps, first = (scalars[i] for i in range(4))
    ones = jnp.ones((8, 128), jnp.float32)
    slice_pos = lax.rem(first + row, BAND)
    distance = ones * (slice_pos - source).astype(jnp.float32) / (ones * width.astype(jnp.float32))
    inside = 1.0 / (1.0 + distance * distance)
    eps = 0.25 / (ones * steps.astype(jnp.float32))
    return inside, eps


def send_parts(links_ref, link_set, row, rows, field, up_ref, first_ref, last_ref):
    _, up = transport(links_ref, row, link_set, 2, None, field)
    store_field(up_ref, row, up)

    @pl.when(row == 0)
    def _():
        store_field(first_ref, 0, field)

    @pl.when(row == rows - 1)
    def _():
        _, later = transport(links_ref, row, link_set, 3, None, field)
        store_field(last_ref, 0, later)


def begin_kernel(rows, scalars, adjoint_ref, links_ref, start_ref, up_ref, first_ref, last_ref):
    def one(row, carry):
        inside, _ = taper(scalars, row)
        start = combine(lambda v: inside * v, load_field(adjoint_ref, row))
        store_field(start_ref, row, start)
        send_parts(links_ref, 2, row, rows, start, up_ref, first_ref, last_ref)
        return carry

    lax.fori_loop(0, rows, one, 0)


def local_kernel(rows, link_set, field_ref, links_ref, sum_ref):
    shape = field_ref.shape[-2:]
    x_pos = lax.broadcasted_iota(jnp.int32, shape, 1) % LX
    at_last = x_pos == LX - 1
    at_first = x_pos == 0

    def one(row, carry):
        here = load_field(field_ref, row)
        ahead = combine(lambda v: jnp.where(at_last, roll(v, LX - 1), roll(v, -1)), here)
        ahead_x, hop = transport(links_ref, row, link_set, 0, ahead, here)
        total = combine(
            lambda v, f, h: f + jnp.where(at_first, roll(h, 1 - LX), roll(h, 1)) - 8.0 * v, here, ahead_x, hop
        )
        ahead = combine(lambda v: roll(v, -LX), here)
        ahead_y, hop = transport(links_ref, row, link_set, 1, ahead, here)
        total = combine(lambda s, f, h: s + f + roll(h, LX), total, ahead_y, hop)
        store_field(sum_ref, row, total)
        return carry

    lax.fori_loop(0, rows, one, 0)

    def between(row, carry):
        ahead_t, hop = transport(
            links_ref, row, link_set, 3, load_field(field_ref, row + 1), load_field(field_ref, row)
        )
        store_field(sum_ref, row, combine(lambda s, f: s + f, load_field(sum_ref, row), ahead_t))
        store_field(sum_ref, row + 1, combine(lambda s, h: s + h, load_field(sum_ref, row + 1), hop))
        return carry

    lax.fori_loop(0, rows - 1, between, 0)


def arrived_sum(links_ref, link_set, row, rows, sum_ref, above_ref, below_ref, later_ref, earlier_ref):
    ahead_z, _ = transport(links_ref, row, link_set, 2, load_field(above_ref, row), None)
    total = combine(lambda s, f, h: s + f + h, load_field(sum_ref, row), ahead_z, load_field(below_ref, row))
    is_first = jnp.where(row == 0, 1.0, 0.0)
    is_last = jnp.where(row == rows - 1, 1.0, 0.0)
    ahead_t, _ = transport(links_ref, row, link_set, 3, load_field(later_ref, 0), None)
    return combine(lambda s, f, h: s + is_last * f + is_first * h, total, ahead_t, load_field(earlier_ref, 0))


def third_kernel(
    rows, scalars, links_ref, sum_ref, above_ref, below_ref, later_ref, earlier_ref,
    third_ref, up_ref, first_ref, last_ref,
):
    def one(row, carry):
        inside, eps = taper(scalars, row)
        total = arrived_sum(links_ref, 2, row, rows, sum_ref, above_ref, below_ref, later_ref, earlier_ref)
        third = combine(lambda s: 0.75 * (inside * (eps * s)), total)
        store_field(third_ref, row, third)
        send_parts(links_ref, 1, row, rows, third, up_ref, first_ref, last_ref)
        return carry

    lax.fori_loop(0, rows, one, 0)


def second_kernel(
    rows, scalars, links_ref, sum_ref, above_ref, below_ref, later_ref, earlier_ref, start_ref, third_ref,
    mixed_ref, up_ref, first_ref, last_ref, base_ref,
):
    def one(row, carry):
        inside, eps = taper(scalars, row)
        total = arrived_sum(links_ref, 1, row, rows, sum_ref, above_ref, below_ref, later_ref, earlier_ref)
        third = load_field(third_ref, row)
        second = combine(lambda v, s: v + (8.0 / 9.0) * (inside * (eps * s)), load_field(start_ref, row), total)
        mixed = combine(lambda p, q: 0.25 * p - (2.0 / 9.0) * q, second, third)
        store_field(mixed_ref, row, mixed)
        store_field(base_ref, row, combine(lambda p, q: p + q, second, third))
        send_parts(links_ref, 0, row, rows, mixed, up_ref, first_ref, last_ref)
        return carry

    lax.fori_loop(0, rows, one, 0)


def last_kernel(
    rows, scalars, links_ref, sum_ref, above_ref, below_ref, later_ref, earlier_ref, base_ref, out_ref
):
    def one(row, carry):
        inside, eps = taper(scalars, row)
        total = arrived_sum(links_ref, 0, row, rows, sum_ref, above_ref, below_ref, later_ref, earlier_ref)
        store_field(out_ref, row, combine(lambda p, s: p + inside * (eps * s), load_field(base_ref, row), total))
        return carry

    lax.fori_loop(0, rows, one, 0)


def call(kernel, name, n_scalars, operands, out_shapes, matvecs):
    vmem = pl.BlockSpec(memory_space=pltpu.VMEM)
    smem = pl.BlockSpec(memory_space=pltpu.SMEM)
    return pl.pallas_call(
        kernel,
        name=name,
        out_shape=out_shapes,
        in_specs=[smem] * n_scalars + [vmem] * (len(operands) - n_scalars),
        out_specs=jax.tree.map(lambda _: vmem, out_shapes),
        cost_estimate=pl.CostEstimate(flops=matvecs * 72 * 1024, bytes_accessed=4096 * 18 * matvecs, transcendentals=0),
        compiler_params=pltpu.CompilerParams(vmem_limit_bytes=16 * 2**20),
    )(*operands)


def body(adjoint, flowed, source_slice, band_width, flow_steps):
    rows = adjoint.shape[0]
    per_plane = BAND // rows
    count = lax.axis_size("gz")
    me = lax.axis_index("gz")
    links = jnp.transpose(flowed, (0, 1, 2, 4, 5, 3, 6)).reshape(-1, flowed.shape[-1])
    scalars = jnp.concatenate(
        [source_slice, band_width, flow_steps, (me * rows).astype(jnp.int32).reshape(1)]
    )
    whole = jax.ShapeDtypeStruct(adjoint.shape, jnp.float32)
    one_row = jax.ShapeDtypeStruct((1,) + adjoint.shape[1:], jnp.float32)

    up_pairs = [(i, (i + per_plane) % count) for i in range(count)]
    down_pairs = [(j, i) for i, j in up_pairs]
    later_pairs = [(i, i + 1) for i in range(count) if (i + 1) % per_plane]
    earlier_pairs = [(j, i) for i, j in later_pairs]

    def exchange(field, up, first, last):
        later = lax.ppermute(first, "gz", earlier_pairs)
        earlier = lax.ppermute(last, "gz", later_pairs)
        above = lax.ppermute(field, "gz", down_pairs)
        below = lax.ppermute(up, "gz", up_pairs)
        return above, below, later, earlier

    def local(field, link_set):
        return call(
            functools.partial(local_kernel, rows, link_set), f"local_{link_set}", 0, (field, links), whole, 22
        )

    start, up, first, last = call(
        functools.partial(begin_kernel, rows), "begin", 1, (scalars, adjoint, links),
        (whole, whole, one_row, one_row), 5,
    )
    arrived = exchange(start, up, first, last)
    third, up, first, last = call(
        functools.partial(third_kernel, rows), "third", 1, (scalars, links, local(start, 2)) + arrived,
        (whole, whole, one_row, one_row), 10,
    )
    arrived = exchange(third, up, first, last)
    mixed, up, first, last, base = call(
        functools.partial(second_kernel, rows), "second", 1,
        (scalars, links, local(third, 1)) + arrived + (start, third),
        (whole, whole, one_row, one_row, whole), 10,
    )
    arrived = exchange(mixed, up, first, last)
    return call(
        functools.partial(last_kernel, rows), "last", 1, (scalars, links, local(mixed, 0)) + arrived + (base,),
        whole, 5,
    )


def solution(mesh):
    in_specs = (
        P(("cfg", "gz"), None, None, None, None),
        P(("cfg", "gz"), None, None, None, None, None, None),
        P("cfg"),
        P("cfg"),
        P("cfg"),
    )
    out_specs = P(("cfg", "gz"), None, None, None, None)
    return jax.shard_map(body, mesh=mesh, in_specs=in_specs, out_specs=out_specs, check_vma=False)
```

```python
import functools

import jax
import jax.numpy as jnp
from jax import lax
from jax.experimental import pallas as pl
from jax.experimental.pallas import tpu as pltpu
from jax.sharding import PartitionSpec as P

BAND = 32
LX = 8
SETS = 3
MUS = 4
ENTRIES = 18


def load_field(ref, row):
    return [[ref[row, c, a] for a in range(3)] for c in range(2)]


def store_field(ref, row, field):
    for c in range(2):
        for a in range(3):
            ref[row, c, a] = field[c][a]


def combine(function, *fields):
    return [[function(*(f[c][a] for f in fields)) for a in range(3)] for c in range(2)]


def entry(links_ref, row, link_set, mu, a, b, c, shape):
    index = ((row * SETS + link_set) * MUS + mu) * ENTRIES + (a * 3 + b) * 2 + c
    return jnp.broadcast_to(links_ref[pl.ds(index, 1), :], shape)


def transport(links_ref, row, link_set, mu, ahead, here):
    forward = [[None] * 3, [None] * 3]
    backward = [[None] * 3, [None] * 3]
    shape = (ahead if ahead is not None else here)[0][0].shape

    def add(total, c, a, value):
        total[c][a] = value if total[c][a] is None else total[c][a] + value

    for a in range(3):
        for b in range(3):
            real = entry(links_ref, row, link_set, mu, a, b, 0, shape)
            imag = entry(links_ref, row, link_set, mu, a, b, 1, shape)
            if ahead is not None:
                add(forward, 0, a, real * ahead[0][b] - imag * ahead[1][b])
                add(forward, 1, a, real * ahead[1][b] + imag * ahead[0][b])
            if here is not None:
                add(backward, 0, b, real * here[0][a] + imag * here[1][a])
                add(backward, 1, b, real * here[1][a] - imag * here[0][a])
    return forward, backward


def roll(plane, by):
    return pltpu.roll(plane, by % plane.shape[-1], plane.ndim - 1)


def taper(scalars, row):
    source, width, steps, first = (scalars[i] for i in range(4))
    ones = jnp.ones((8, 128), jnp.float32)
    slice_pos = lax.rem(first + row, BAND)
    distance = ones * (slice_pos - source).astype(jnp.float32) / (ones * width.astype(jnp.float32))
    inside = 1.0 / (1.0 + distance * distance)
    eps = 0.25 / (ones * steps.astype(jnp.float32))
    return inside, eps


def edge_parts(links_ref, link_set, row, rows, field, first_ref, last_ref):
    @pl.when(row == 0)
    def _():
        store_field(first_ref, 0, field)

    @pl.when(row == rows - 1)
    def _():
        _, later = transport(links_ref, row, link_set, 3, None, field)
        store_field(last_ref, 0, later)


def begin_kernel(rows, scalars, adjoint_ref, links_ref, start_ref, first_ref, last_ref):
    def one(row, carry):
        inside, _ = taper(scalars, row)
        start = combine(lambda v: inside * v, load_field(adjoint_ref, row))
        store_field(start_ref, row, start)
        edge_parts(links_ref, 2, row, rows, start, first_ref, last_ref)
        return carry

    lax.fori_loop(0, rows, one, 0)


def middle_kernel(rows, link_set, scalars, field_ref, links_ref, later_ref, earlier_ref, up_ref, down_ref, edge_ref):
    def one(row, carry):
        field = load_field(field_ref, row)
        store_field(down_ref, row, field)
        _, up = transport(links_ref, row, link_set, 2, None, field)
        store_field(up_ref, row, up)
        return carry

    lax.fori_loop(0, rows, one, 0)
    first_pos = lax.rem(scalars[3], BAND)
    not_first = jnp.where(first_pos != 0, 1.0, 0.0)
    not_last = jnp.where(first_pos != BAND - rows, 1.0, 0.0)
    store_field(edge_ref, 0, combine(lambda h: not_first * h, load_field(earlier_ref, 0)))
    ahead_t, _ = transport(links_ref, rows - 1, link_set, 3, load_field(later_ref, 0), None)
    store_field(edge_ref, 1, combine(lambda f: not_last * f, ahead_t))


def local_kernel(rows, link_set, field_ref, links_ref, sum_ref):
    shape = field_ref.shape[-2:]
    x_pos = lax.broadcasted_iota(jnp.int32, shape, 1) % LX
    at_last = x_pos == LX - 1
    at_first = x_pos == 0

    def one(row, carry):
        here = load_field(field_ref, row)
        ahead = combine(lambda v: jnp.where(at_last, roll(v, LX - 1), roll(v, -1)), here)
        ahead_x, hop = transport(links_ref, row, link_set, 0, ahead, here)
        total = combine(
            lambda v, f, h: f + jnp.where(at_first, roll(h, 1 - LX), roll(h, 1)) - 8.0 * v, here, ahead_x, hop
        )
        ahead = combine(lambda v: roll(v, -LX), here)
        ahead_y, hop = transport(links_ref, row, link_set, 1, ahead, here)
        total = combine(lambda s, f, h: s + f + roll(h, LX), total, ahead_y, hop)
        store_field(sum_ref, row, total)
        return carry

    lax.fori_loop(0, rows, one, 0)

    def between(row, carry):
        ahead_t, hop = transport(
            links_ref, row, link_set, 3, load_field(field_ref, row + 1), load_field(field_ref, row)
        )
        store_field(sum_ref, row, combine(lambda s, f: s + f, load_field(sum_ref, row), ahead_t))
        store_field(sum_ref, row + 1, combine(lambda s, h: s + h, load_field(sum_ref, row + 1), hop))
        return carry

    lax.fori_loop(0, rows - 1, between, 0)


def arrived_sum(links_ref, link_set, row, rows, sum_ref, edge_ref, above_ref, below_ref):
    ahead_z, _ = transport(links_ref, row, link_set, 2, load_field(above_ref, row), None)
    total = combine(lambda s, f, h: s + f + h, load_field(sum_ref, row), ahead_z, load_field(below_ref, row))
    is_first = jnp.where(row == 0, 1.0, 0.0)
    is_last = jnp.where(row == rows - 1, 1.0, 0.0)
    return combine(
        lambda s, h, f: s + is_first * h + is_last * f, total, load_field(edge_ref, 0), load_field(edge_ref, 1)
    )


def third_kernel(
    rows, scalars, links_ref, sum_ref, edge_ref, above_ref, below_ref, third_ref, first_ref, last_ref
):
    def one(row, carry):
        inside, eps = taper(scalars, row)
        total = arrived_sum(links_ref, 2, row, rows, sum_ref, edge_ref, above_ref, below_ref)
        third = combine(lambda s: 0.75 * (inside * (eps * s)), total)
        store_field(third_ref, row, third)
        edge_parts(links_ref, 1, row, rows, third, first_ref, last_ref)
        return carry

    lax.fori_loop(0, rows, one, 0)


def second_kernel(
    rows, scalars, links_ref, sum_ref, edge_ref, above_ref, below_ref, start_ref, third_ref,
    mixed_ref, first_ref, last_ref, base_ref,
):
    def one(row, carry):
        inside, eps = taper(scalars, row)
        total = arrived_sum(links_ref, 1, row, rows, sum_ref, edge_ref, above_ref, below_ref)
        third = load_field(third_ref, row)
        second = combine(lambda v, s: v + (8.0 / 9.0) * (inside * (eps * s)), load_field(start_ref, row), total)
        mixed = combine(lambda p, q: 0.25 * p - (2.0 / 9.0) * q, second, third)
        store_field(mixed_ref, row, mixed)
        store_field(base_ref, row, combine(lambda p, q: p + q, second, third))
        edge_parts(links_ref, 0, row, rows, mixed, first_ref, last_ref)
        return carry

    lax.fori_loop(0, rows, one, 0)


def last_kernel(rows, scalars, links_ref, sum_ref, edge_ref, above_ref, below_ref, base_ref, out_ref):
    def one(row, carry):
        inside, eps = taper(scalars, row)
        total = arrived_sum(links_ref, 0, row, rows, sum_ref, edge_ref, above_ref, below_ref)
        store_field(out_ref, row, combine(lambda p, s: p + inside * (eps * s), load_field(base_ref, row), total))
        return carry

    lax.fori_loop(0, rows, one, 0)


def call(kernel, name, n_scalars, operands, out_shapes, matvecs):
    vmem = pl.BlockSpec(memory_space=pltpu.VMEM)
    smem = pl.BlockSpec(memory_space=pltpu.SMEM)
    return pl.pallas_call(
        kernel,
        name=name,
        out_shape=out_shapes,
        in_specs=[smem] * n_scalars + [vmem] * (len(operands) - n_scalars),
        out_specs=jax.tree.map(lambda _: vmem, out_shapes),
        cost_estimate=pl.CostEstimate(flops=matvecs * 72 * 1024, bytes_accessed=4096 * 18 * matvecs, transcendentals=0),
        compiler_params=pltpu.CompilerParams(vmem_limit_bytes=16 * 2**20),
    )(*operands)


def body(adjoint, flowed, source_slice, band_width, flow_steps):
    rows = adjoint.shape[0]
    per_plane = BAND // rows
    count = lax.axis_size("gz")
    me = lax.axis_index("gz")
    links = jnp.transpose(flowed, (0, 1, 2, 4, 5, 3, 6)).reshape(-1, flowed.shape[-1])
    scalars = jnp.concatenate(
        [source_slice, band_width, flow_steps, (me * rows).astype(jnp.int32).reshape(1)]
    )
    whole = jax.ShapeDtypeStruct(adjoint.shape, jnp.float32)
    one_row = jax.ShapeDtypeStruct((1,) + adjoint.shape[1:], jnp.float32)
    two_rows = jax.ShapeDtypeStruct((2,) + adjoint.shape[1:], jnp.float32)

    up_pairs = [(i, (i + per_plane) % count) for i in range(count)]
    down_pairs = [(j, i) for i, j in up_pairs]
    later_pairs = [(i, i - i % per_plane + (i + 1) % per_plane) for i in range(count)]
    earlier_pairs = [(j, i) for i, j in later_pairs]

    def gathered(link_set, field, first, last):
        later = lax.ppermute(first, "gz", earlier_pairs)
        earlier = lax.ppermute(last, "gz", later_pairs)
        up, down, edge = call(
            functools.partial(middle_kernel, rows, link_set), f"middle_{link_set}", 1,
            (scalars, field, links, later, earlier), (whole, whole, two_rows), 5,
        )
        above = lax.ppermute(down, "gz", down_pairs)
        below = lax.ppermute(up, "gz", up_pairs)
        total = call(
            functools.partial(local_kernel, rows, link_set), f"local_{link_set}", 0, (field, links), whole, 22
        )
        return total, edge, above, below

    start, first, last = call(
        functools.partial(begin_kernel, rows), "begin", 1, (scalars, adjoint, links), (whole, one_row, one_row), 1
    )
    third, first, last = call(
        functools.partial(third_kernel, rows), "third", 1, (scalars, links) + gathered(2, start, first, last),
        (whole, one_row, one_row), 5,
    )
    mixed, first, last, base = call(
        functools.partial(second_kernel, rows), "second", 1,
        (scalars, links) + gathered(1, third, first, last) + (start, third),
        (whole, one_row, one_row, whole), 5,
    )
    return call(
        functools.partial(last_kernel, rows), "last", 1,
        (scalars, links) + gathered(0, mixed, first, last) + (base,), whole, 4,
    )


def solution(mesh):
    in_specs = (
        P(("cfg", "gz"), None, None, None, None),
        P(("cfg", "gz"), None, None, None, None, None, None),
        P("cfg"),
        P("cfg"),
        P("cfg"),
    )
    out_specs = P(("cfg", "gz"), None, None, None, None)
    return jax.shard_map(body, mesh=mesh, in_specs=in_specs, out_specs=out_specs, check_vma=False)
```

```python
import functools

import jax
import jax.numpy as jnp
from jax import lax
from jax.experimental import pallas as pl
from jax.experimental.pallas import tpu as pltpu
from jax.sharding import PartitionSpec as P

BAND = 32
LX = 8
SETS = 3
MUS = 4
ENTRIES = 18


def load_field(ref, row):
    return [[ref[row, c, a] for a in range(3)] for c in range(2)]


def store_field(ref, row, field):
    for c in range(2):
        for a in range(3):
            ref[row, c, a] = field[c][a]


def combine(function, *fields):
    return [[function(*(f[c][a] for f in fields)) for a in range(3)] for c in range(2)]


def entry(links_ref, row, link_set, mu, a, b, c, shape, mus=MUS):
    index = ((row * SETS + link_set) * mus + mu) * ENTRIES + (a * 3 + b) * 2 + c
    return jnp.broadcast_to(links_ref[pl.ds(index, 1), :], shape)


def transport(links_ref, row, link_set, mu, ahead, here, mus=MUS):
    forward = [[None] * 3, [None] * 3]
    backward = [[None] * 3, [None] * 3]
    shape = (ahead if ahead is not None else here)[0][0].shape

    def add(total, c, a, value):
        total[c][a] = value if total[c][a] is None else total[c][a] + value

    for a in range(3):
        for b in range(3):
            real = entry(links_ref, row, link_set, mu, a, b, 0, shape, mus)
            imag = entry(links_ref, row, link_set, mu, a, b, 1, shape, mus)
            if ahead is not None:
                add(forward, 0, a, real * ahead[0][b] - imag * ahead[1][b])
                add(forward, 1, a, real * ahead[1][b] + imag * ahead[0][b])
            if here is not None:
                add(backward, 0, b, real * here[0][a] + imag * here[1][a])
                add(backward, 1, b, real * here[1][a] - imag * here[0][a])
    return forward, backward


def roll(plane, by):
    return pltpu.roll(plane, by % plane.shape[-1], plane.ndim - 1)


def taper(scalars, row):
    source, width, steps, first = (scalars[i] for i in range(4))
    ones = jnp.ones((8, 128), jnp.float32)
    slice_pos = lax.rem(first + row, BAND)
    distance = ones * (slice_pos - source).astype(jnp.float32) / (ones * width.astype(jnp.float32))
    inside = 1.0 / (1.0 + distance * distance)
    eps = 0.25 / (ones * steps.astype(jnp.float32))
    return inside, eps


def edge_parts(links_ref, link_set, row, rows, field, first_ref, last_ref):
    @pl.when(row == 0)
    def _():
        store_field(first_ref, 0, field)

    @pl.when(row == rows - 1)
    def _():
        _, later = transport(links_ref, row, link_set, 3, None, field)
        store_field(last_ref, 0, later)


def begin_kernel(rows, scalars, adjoint_ref, links_ref, start_ref, first_ref, last_ref):
    def one(row, carry):
        inside, _ = taper(scalars, row)
        start = combine(lambda v: inside * v, load_field(adjoint_ref, row))
        store_field(start_ref, row, start)
        edge_parts(links_ref, 2, row, rows, start, first_ref, last_ref)
        return carry

    lax.fori_loop(0, rows, one, 0)


def local_kernel(rows, link_set, field_ref, links_ref, sum_ref):
    shape = field_ref.shape[-2:]
    x_pos = lax.broadcasted_iota(jnp.int32, shape, 1) % LX
    at_last = x_pos == LX - 1
    at_first = x_pos == 0

    def one(row, carry):
        here = load_field(field_ref, row)
        ahead = combine(lambda v: jnp.where(at_last, roll(v, LX - 1), roll(v, -1)), here)
        ahead_x, hop = transport(links_ref, row, link_set, 0, ahead, here)
        total = combine(
            lambda v, f, h: f + jnp.where(at_first, roll(h, 1 - LX), roll(h, 1)) - 8.0 * v, here, ahead_x, hop
        )
        ahead = combine(lambda v: roll(v, -LX), here)
        ahead_y, hop = transport(links_ref, row, link_set, 1, ahead, here)
        total = combine(lambda s, f, h: s + f + roll(h, LX), total, ahead_y, hop)
        store_field(sum_ref, row, total)
        return carry

    lax.fori_loop(0, rows, one, 0)

    def between(row, carry):
        ahead_t, hop = transport(
            links_ref, row, link_set, 3, load_field(field_ref, row + 1), load_field(field_ref, row)
        )
        store_field(sum_ref, row, combine(lambda s, f: s + f, load_field(sum_ref, row), ahead_t))
        store_field(sum_ref, row + 1, combine(lambda s, h: s + h, load_field(sum_ref, row + 1), hop))
        return carry

    lax.fori_loop(0, rows - 1, between, 0)


def arrived_sum(
    links_ref, link_set, row, rows, scalars, planes, sum_ref, lower_links_ref, gathered_ref, later_ref, earlier_ref
):
    first_pos = lax.rem(scalars[3], BAND)
    plane = scalars[3] // BAND
    above = lax.rem(plane + 1, planes)
    below = lax.rem(plane + planes - 1, planes)
    ahead_z, _ = transport(links_ref, row, link_set, 2, load_field(gathered_ref.at[above], row), None)
    _, behind_z = transport(lower_links_ref, row, link_set, 0, None, load_field(gathered_ref.at[below], row), 1)
    total = combine(lambda s, f, h: s + f + h, load_field(sum_ref, row), ahead_z, behind_z)
    is_first = jnp.where((row == 0) & (first_pos != 0), 1.0, 0.0)
    is_last = jnp.where((row == rows - 1) & (first_pos != BAND - rows), 1.0, 0.0)
    ahead_t, _ = transport(links_ref, row, link_set, 3, load_field(later_ref, 0), None)
    return combine(lambda s, f, h: s + is_last * f + is_first * h, total, ahead_t, load_field(earlier_ref, 0))


def third_kernel(
    rows, planes, scalars, links_ref, sum_ref, lower_links_ref, gathered_ref, later_ref, earlier_ref,
    third_ref, first_ref, last_ref,
):
    def one(row, carry):
        inside, eps = taper(scalars, row)
        total = arrived_sum(
            links_ref, 2, row, rows, scalars, planes, sum_ref, lower_links_ref, gathered_ref, later_ref, earlier_ref
        )
        third = combine(lambda s: 0.75 * (inside * (eps * s)), total)
        store_field(third_ref, row, third)
        edge_parts(links_ref, 1, row, rows, third, first_ref, last_ref)
        return carry

    lax.fori_loop(0, rows, one, 0)


def second_kernel(
    rows, planes, scalars, links_ref, sum_ref, lower_links_ref, gathered_ref, later_ref, earlier_ref, start_ref,
    third_ref, mixed_ref, first_ref, last_ref, base_ref,
):
    def one(row, carry):
        inside, eps = taper(scalars, row)
        total = arrived_sum(
            links_ref, 1, row, rows, scalars, planes, sum_ref, lower_links_ref, gathered_ref, later_ref, earlier_ref
        )
        third = load_field(third_ref, row)
        second = combine(lambda v, s: v + (8.0 / 9.0) * (inside * (eps * s)), load_field(start_ref, row), total)
        mixed = combine(lambda p, q: 0.25 * p - (2.0 / 9.0) * q, second, third)
        store_field(mixed_ref, row, mixed)
        store_field(base_ref, row, combine(lambda p, q: p + q, second, third))
        edge_parts(links_ref, 0, row, rows, mixed, first_ref, last_ref)
        return carry

    lax.fori_loop(0, rows, one, 0)


def last_kernel(
    rows, planes, scalars, links_ref, sum_ref, lower_links_ref, gathered_ref, later_ref, earlier_ref, base_ref, out_ref
):
    def one(row, carry):
        inside, eps = taper(scalars, row)
        total = arrived_sum(
            links_ref, 0, row, rows, scalars, planes, sum_ref, lower_links_ref, gathered_ref, later_ref, earlier_ref
        )
        store_field(out_ref, row, combine(lambda p, s: p + inside * (eps * s), load_field(base_ref, row), total))
        return carry

    lax.fori_loop(0, rows, one, 0)


def call(kernel, name, n_scalars, operands, out_shapes, matvecs):
    vmem = pl.BlockSpec(memory_space=pltpu.VMEM)
    smem = pl.BlockSpec(memory_space=pltpu.SMEM)
    return pl.pallas_call(
        kernel,
        name=name,
        out_shape=out_shapes,
        in_specs=[smem] * n_scalars + [vmem] * (len(operands) - n_scalars),
        out_specs=jax.tree.map(lambda _: vmem, out_shapes),
        cost_estimate=pl.CostEstimate(flops=matvecs * 72 * 1024, bytes_accessed=4096 * 18 * matvecs, transcendentals=0),
        compiler_params=pltpu.CompilerParams(vmem_limit_bytes=16 * 2**20),
    )(*operands)


def body(adjoint, flowed, source_slice, band_width, flow_steps):
    rows = adjoint.shape[0]
    per_plane = BAND // rows
    count = lax.axis_size("gz")
    me = lax.axis_index("gz")
    planes = count // per_plane
    by_entry = jnp.transpose(flowed, (0, 1, 2, 4, 5, 3, 6))
    links = by_entry.reshape(-1, flowed.shape[-1])
    scalars = jnp.concatenate(
        [source_slice, band_width, flow_steps, (me * rows).astype(jnp.int32).reshape(1)]
    )
    whole = jax.ShapeDtypeStruct(adjoint.shape, jnp.float32)
    one_row = jax.ShapeDtypeStruct((1,) + adjoint.shape[1:], jnp.float32)

    up_pairs = [(i, (i + per_plane) % count) for i in range(count)]
    later_pairs = [(i, i - i % per_plane + (i + 1) % per_plane) for i in range(count)]
    earlier_pairs = [(j, i) for i, j in later_pairs]
    z_lines = [[t + z * per_plane for z in range(planes)] for t in range(per_plane)]
    lower_links = lax.ppermute(by_entry[:, :, 2], "gz", up_pairs).reshape(-1, flowed.shape[-1])

    def arrivals(link_set, field, first, last):
        gathered = lax.all_gather(field, "gz", axis_index_groups=z_lines)
        later = lax.ppermute(first, "gz", earlier_pairs)
        earlier = lax.ppermute(last, "gz", later_pairs)
        total = call(
            functools.partial(local_kernel, rows, link_set), f"local_{link_set}", 0, (field, links), whole, 22
        )
        return total, lower_links, gathered, later, earlier

    start, first, last = call(
        functools.partial(begin_kernel, rows), "begin", 1, (scalars, adjoint, links), (whole, one_row, one_row), 1
    )
    third, first, last = call(
        functools.partial(third_kernel, rows, planes), "third", 1, (scalars, links) + arrivals(2, start, first, last),
        (whole, one_row, one_row), 13,
    )
    mixed, first, last, base = call(
        functools.partial(second_kernel, rows, planes), "second", 1,
        (scalars, links) + arrivals(1, third, first, last) + (start, third),
        (whole, one_row, one_row, whole), 13,
    )
    return call(
        functools.partial(last_kernel, rows, planes), "last", 1,
        (scalars, links) + arrivals(0, mixed, first, last) + (base,), whole, 12,
    )


def solution(mesh):
    in_specs = (
        P(("cfg", "gz"), None, None, None, None),
        P(("cfg", "gz"), None, None, None, None, None, None),
        P("cfg"),
        P("cfg"),
        P("cfg"),
    )
    out_specs = P(("cfg", "gz"), None, None, None, None)
    return jax.shard_map(body, mesh=mesh, in_specs=in_specs, out_specs=out_specs, check_vma=False)
```

```python
import functools

import jax
import jax.numpy as jnp
from jax import lax
from jax.experimental import pallas as pl
from jax.experimental.pallas import tpu as pltpu
from jax.sharding import PartitionSpec as P

BAND = 32
LX = 8
SETS = 3
MUS = 4
ENTRIES = 18


def load_field(ref, row):
    return [[ref[row, c, a] for a in range(3)] for c in range(2)]


def store_field(ref, row, field):
    for c in range(2):
        for a in range(3):
            ref[row, c, a] = field[c][a]


def combine(function, *fields):
    return [[function(*(f[c][a] for f in fields)) for a in range(3)] for c in range(2)]


def entry(links_ref, row, link_set, mu, a, b, c, shape):
    index = ((row * SETS + link_set) * MUS + mu) * ENTRIES + (a * 3 + b) * 2 + c
    return jnp.broadcast_to(links_ref[pl.ds(index, 1), :], shape)


def transport(links_ref, row, link_set, mu, ahead, here):
    forward = [[None] * 3, [None] * 3]
    backward = [[None] * 3, [None] * 3]
    shape = (ahead if ahead is not None else here)[0][0].shape

    def add(total, c, a, value):
        total[c][a] = value if total[c][a] is None else total[c][a] + value

    for a in range(3):
        for b in range(3):
            real = entry(links_ref, row, link_set, mu, a, b, 0, shape)
            imag = entry(links_ref, row, link_set, mu, a, b, 1, shape)
            if ahead is not None:
                add(forward, 0, a, real * ahead[0][b] - imag * ahead[1][b])
                add(forward, 1, a, real * ahead[1][b] + imag * ahead[0][b])
            if here is not None:
                add(backward, 0, b, real * here[0][a] + imag * here[1][a])
                add(backward, 1, b, real * here[1][a] - imag * here[0][a])
    return forward, backward


def roll(plane, by):
    return pltpu.roll(plane, by % plane.shape[-1], plane.ndim - 1)


def place(scalars, rows):
    first_pos = lax.rem(scalars[3], BAND)
    return first_pos, lax.rem(first_pos // rows, 2) == 1


def taper(scalars, row):
    ones = jnp.ones((8, 128), jnp.float32)
    slice_pos = lax.rem(scalars[3] + row, BAND)
    distance = ones * (slice_pos - scalars[0]).astype(jnp.float32) / (ones * scalars[1].astype(jnp.float32))
    inside = 1.0 / (1.0 + distance * distance)
    eps = 0.25 / (ones * scalars[2].astype(jnp.float32))
    return inside, eps


def store_edges(scalars, links_ref, link_set, rows, field_ref, outer_ref, inner_ref):
    _, is_odd = place(scalars, rows)
    first = load_field(field_ref, 0)
    _, last = transport(links_ref, rows - 1, link_set, 3, None, load_field(field_ref, rows - 1))
    store_field(outer_ref, 0, combine(lambda p, q: jnp.where(is_odd, q, p), first, last))
    store_field(inner_ref, 0, combine(lambda p, q: jnp.where(is_odd, p, q), first, last))


def store_up(links_ref, link_set, row, field, up_ref):
    _, up = transport(links_ref, row, link_set, 2, None, field)
    store_field(up_ref, row, up)


def begin_kernel(rows, scalars, adjoint_ref, links_ref, start_ref, up_ref, outer_ref, inner_ref):
    for row in range(rows):
        inside, _ = taper(scalars, row)
        start = combine(lambda v: inside * v, load_field(adjoint_ref, row))
        store_field(start_ref, row, start)
        store_up(links_ref, 2, row, start, up_ref)
    store_edges(scalars, links_ref, 2, rows, start_ref, outer_ref, inner_ref)


def local_kernel(rows, link_set, field_ref, links_ref, sum_ref):
    shape = field_ref.shape[-2:]
    x_pos = lax.broadcasted_iota(jnp.int32, shape, 1) % LX
    at_last = x_pos == LX - 1
    at_first = x_pos == 0

    def one(row, carry):
        here = load_field(field_ref, row)
        ahead = combine(lambda v: jnp.where(at_last, roll(v, LX - 1), roll(v, -1)), here)
        ahead_x, hop = transport(links_ref, row, link_set, 0, ahead, here)
        total = combine(
            lambda v, f, h: f + jnp.where(at_first, roll(h, 1 - LX), roll(h, 1)) - 8.0 * v, here, ahead_x, hop
        )
        ahead = combine(lambda v: roll(v, -LX), here)
        ahead_y, hop = transport(links_ref, row, link_set, 1, ahead, here)
        total = combine(lambda s, f, h: s + f + roll(h, LX), total, ahead_y, hop)
        store_field(sum_ref, row, total)
        return carry

    lax.fori_loop(0, rows, one, 0)

    def between(row, carry):
        ahead_t, hop = transport(
            links_ref, row, link_set, 3, load_field(field_ref, row + 1), load_field(field_ref, row)
        )
        store_field(sum_ref, row, combine(lambda s, f: s + f, load_field(sum_ref, row), ahead_t))
        store_field(sum_ref, row + 1, combine(lambda s, h: s + h, load_field(sum_ref, row + 1), hop))
        return carry

    lax.fori_loop(0, rows - 1, between, 0)


def arrived_sum(scalars, links_ref, link_set, row, rows, arrivals, scale=None):
    sum_ref, above_ref, below_ref, outer_ref, inner_ref = arrivals
    first_pos, is_odd = place(scalars, rows)
    above = load_field(above_ref, row)
    if scale is not None:
        above = combine(lambda v: scale * v, above)
    ahead_z, _ = transport(links_ref, row, link_set, 2, above, None)
    total = combine(lambda s, f, h: s + f + h, load_field(sum_ref, row), ahead_z, load_field(below_ref, row))
    outer, inner = load_field(outer_ref, 0), load_field(inner_ref, 0)
    if row == 0:
        exists = jnp.where(first_pos != 0, 1.0, 0.0)
        total = combine(lambda s, p, q: s + exists * jnp.where(is_odd, q, p), total, outer, inner)
    if row == rows - 1:
        exists = jnp.where(first_pos != BAND - rows, 1.0, 0.0)
        later = combine(lambda p, q: exists * jnp.where(is_odd, p, q), outer, inner)
        ahead_t, _ = transport(links_ref, row, link_set, 3, later, None)
        total = combine(lambda s, f: s + f, total, ahead_t)
    return total


def third_kernel(rows, scalars, links_ref, *refs):
    arrivals, (third_ref, up_ref, outer_ref, inner_ref) = refs[:5], refs[5:]
    for row in range(rows):
        inside, eps = taper(scalars, row)
        total = arrived_sum(scalars, links_ref, 2, row, rows, arrivals, inside)
        third = combine(lambda s: 0.75 * (inside * (eps * s)), total)
        store_field(third_ref, row, third)
        store_up(links_ref, 1, row, third, up_ref)
    store_edges(scalars, links_ref, 1, rows, third_ref, outer_ref, inner_ref)


def second_kernel(rows, scalars, links_ref, *refs):
    arrivals, (start_ref, third_ref, mixed_ref, up_ref, outer_ref, inner_ref, base_ref) = refs[:5], refs[5:]
    for row in range(rows):
        inside, eps = taper(scalars, row)
        total = arrived_sum(scalars, links_ref, 1, row, rows, arrivals)
        third = load_field(third_ref, row)
        second = combine(lambda v, s: v + (8.0 / 9.0) * (inside * (eps * s)), load_field(start_ref, row), total)
        mixed = combine(lambda p, q: 0.25 * p - (2.0 / 9.0) * q, second, third)
        store_field(mixed_ref, row, mixed)
        store_field(base_ref, row, combine(lambda p, q: p + q, second, third))
        store_up(links_ref, 0, row, mixed, up_ref)
    store_edges(scalars, links_ref, 0, rows, mixed_ref, outer_ref, inner_ref)


def last_kernel(rows, scalars, links_ref, *refs):
    arrivals, (base_ref, out_ref) = refs[:5], refs[5:]
    for row in range(rows):
        inside, eps = taper(scalars, row)
        total = arrived_sum(scalars, links_ref, 0, row, rows, arrivals)
        store_field(out_ref, row, combine(lambda p, s: p + inside * (eps * s), load_field(base_ref, row), total))


def call(kernel, name, n_scalars, operands, out_shapes, matvecs):
    vmem = pl.BlockSpec(memory_space=pltpu.VMEM)
    smem = pl.BlockSpec(memory_space=pltpu.SMEM)
    return pl.pallas_call(
        kernel,
        name=name,
        out_shape=out_shapes,
        in_specs=[smem] * n_scalars + [vmem] * (len(operands) - n_scalars),
        out_specs=jax.tree.map(lambda _: vmem, out_shapes),
        cost_estimate=pl.CostEstimate(flops=matvecs * 72 * 1024, bytes_accessed=4096 * 18 * matvecs, transcendentals=0),
        compiler_params=pltpu.CompilerParams(vmem_limit_bytes=16 * 2**20),
    )(*operands)


def body(adjoint, flowed, source_slice, band_width, flow_steps):
    rows = adjoint.shape[0]
    per_plane = BAND // rows
    count = lax.axis_size("gz")
    me = lax.axis_index("gz")
    links = jnp.transpose(flowed, (0, 1, 2, 4, 5, 3, 6)).reshape(-1, flowed.shape[-1])
    scalars = jnp.concatenate(
        [source_slice, band_width, flow_steps, (me * rows).astype(jnp.int32).reshape(1)]
    )
    whole = jax.ShapeDtypeStruct(adjoint.shape, jnp.float32)
    one_row = jax.ShapeDtypeStruct((1,) + adjoint.shape[1:], jnp.float32)

    up_pairs = [(i, (i + per_plane) % count) for i in range(count)]
    down_pairs = [(j, i) for i, j in up_pairs]

    def in_plane(i, by):
        return i - i % per_plane + (i + by) % per_plane

    outer_pairs = [(i, in_plane(i, 1 if i % 2 else -1)) for i in range(count)]
    inner_pairs = [(i, in_plane(i, -1 if i % 2 else 1)) for i in range(count)]

    def local(field, link_set):
        return call(
            functools.partial(local_kernel, rows, link_set), f"local_{link_set}", 0, (field, links), whole, 22
        )

    def arrivals(link_set, field, sent_down, up, outer, inner):
        above = lax.ppermute(sent_down, "gz", down_pairs)
        below = lax.ppermute(up, "gz", up_pairs)
        outer = lax.ppermute(outer, "gz", outer_pairs)
        inner = lax.ppermute(inner, "gz", inner_pairs)
        return local(field, link_set), above, below, outer, inner

    start, up, outer, inner = call(
        functools.partial(begin_kernel, rows), "begin", 1, (scalars, adjoint, links),
        (whole, whole, one_row, one_row), 5,
    )
    third, up, outer, inner = call(
        functools.partial(third_kernel, rows), "third", 1,
        (scalars, links) + arrivals(2, start, adjoint, up, outer, inner), (whole, whole, one_row, one_row), 10,
    )
    mixed, up, outer, inner, base = call(
        functools.partial(second_kernel, rows), "second", 1,
        (scalars, links) + arrivals(1, third, third, up, outer, inner) + (start, third),
        (whole, whole, one_row, one_row, whole), 10,
    )
    return call(
        functools.partial(last_kernel, rows), "last", 1,
        (scalars, links) + arrivals(0, mixed, mixed, up, outer, inner) + (base,), whole, 5,
    )


def solution(mesh):
    in_specs = (
        P(("cfg", "gz"), None, None, None, None),
        P(("cfg", "gz"), None, None, None, None, None, None),
        P("cfg"),
        P("cfg"),
        P("cfg"),
    )
    out_specs = P(("cfg", "gz"), None, None, None, None)
    return jax.shard_map(body, mesh=mesh, in_specs=in_specs, out_specs=out_specs, check_vma=False)
```

```python
import functools

import jax
import jax.numpy as jnp
from jax import lax
from jax.experimental import pallas as pl
from jax.experimental.pallas import tpu as pltpu
from jax.sharding import PartitionSpec as P

BAND = 32
LX = 8
SETS = 3
MUS = 4
ENTRIES = 18


def load_field(ref, row):
    return [[ref[row, c, a] for a in range(3)] for c in range(2)]


def store_field(ref, row, field):
    for c in range(2):
        for a in range(3):
            ref[row, c, a] = field[c][a]


def combine(function, *fields):
    return [[function(*(f[c][a] for f in fields)) for a in range(3)] for c in range(2)]


def links_at(links_ref, row, link_set, mu):
    return links_ref, ((row * SETS + link_set) * MUS + mu) * ENTRIES


def entry(matrices, a, b, c, shape):
    ref, base = matrices
    return jnp.broadcast_to(ref[pl.ds(base + (a * 3 + b) * 2 + c, 1), :], shape)


def transport(matrices, ahead, here):
    forward = [[None] * 3, [None] * 3]
    backward = [[None] * 3, [None] * 3]
    shape = (ahead if ahead is not None else here)[0][0].shape

    def add(total, c, a, value):
        total[c][a] = value if total[c][a] is None else total[c][a] + value

    for a in range(3):
        for b in range(3):
            real = entry(matrices, a, b, 0, shape)
            imag = entry(matrices, a, b, 1, shape)
            if ahead is not None:
                add(forward, 0, a, real * ahead[0][b] - imag * ahead[1][b])
                add(forward, 1, a, real * ahead[1][b] + imag * ahead[0][b])
            if here is not None:
                add(backward, 0, b, real * here[0][a] + imag * here[1][a])
                add(backward, 1, b, real * here[1][a] - imag * here[0][a])
    return forward, backward


def roll(plane, by):
    return pltpu.roll(plane, by % plane.shape[-1], plane.ndim - 1)


def place(rows):
    first = lax.axis_index("gz") * rows
    plane, first_pos = first // BAND, lax.rem(first, BAND)
    return plane, first_pos, lax.rem(plane, 2) == 1, lax.rem(first_pos // rows, 2) == 1


def taper(first_pos, row, source, width):
    ones = jnp.ones((8, 128), jnp.float32)
    distance = ones * (first_pos + row - source).astype(jnp.float32) / (ones * width.astype(jnp.float32))
    return 1.0 / (1.0 + distance * distance)


def store_z(rows, matrices, row, field, far_ref, near_ref):
    _, _, odd_plane, _ = place(rows)
    _, up = transport(matrices, None, field)
    store_field(far_ref, row, combine(lambda v, h: jnp.where(odd_plane, h, v), field, up))
    store_field(near_ref, row, combine(lambda v, h: jnp.where(odd_plane, v, h), field, up))


def store_t(rows, matrices, field_ref, outer_ref, inner_ref):
    _, _, _, odd_block = place(rows)
    first = load_field(field_ref, 0)
    _, last = transport(matrices, None, load_field(field_ref, rows - 1))
    store_field(outer_ref, 0, combine(lambda p, q: jnp.where(odd_block, q, p), first, last))
    store_field(inner_ref, 0, combine(lambda p, q: jnp.where(odd_block, p, q), first, last))


def begin_kernel(
    rows, source_hbm, width_hbm, steps_hbm, adjoint_hbm, links_hbm,
    start_ref, far_ref, near_ref, outer_ref, inner_ref, coefs_ref,
    source_ref, width_ref, steps_ref, adjoint_ref, links_ref, sems,
):
    row_entries = SETS * MUS * ENTRIES
    z_first = (2 * MUS + 2) * ENTRIES
    aligned = z_first // 8 * 8
    pairs = [(source_hbm, source_ref), (width_hbm, width_ref), (steps_hbm, steps_ref), (adjoint_hbm, adjoint_ref)]
    for row in range(rows):
        part = links_hbm.at[pl.ds(row * row_entries + aligned, row_entries - aligned), :]
        pairs.append((part, links_ref.at[row]))
    copies = [pltpu.make_async_copy(p, q, sems.at[i]) for i, (p, q) in enumerate(pairs)]
    for copy in copies:
        copy.start()
    for copy in copies:
        copy.wait()
    _, first_pos, _, _ = place(rows)
    for row in range(rows):
        inside = taper(first_pos, row, source_ref[0], width_ref[0])
        coefs_ref[row] = inside
        start = combine(lambda v: inside * v, load_field(adjoint_ref, row))
        store_field(start_ref, row, start)
        store_z(rows, (links_ref.at[row], z_first - aligned), row, start, far_ref, near_ref)
    coefs_ref[rows] = 0.25 / (jnp.ones((8, 128), jnp.float32) * steps_ref[0].astype(jnp.float32))
    store_t(rows, (links_ref.at[rows - 1], z_first + ENTRIES - aligned), start_ref, outer_ref, inner_ref)


def local_kernel(rows, link_set, field_ref, links_ref, sum_ref):
    shape = field_ref.shape[-2:]
    x_pos = lax.broadcasted_iota(jnp.int32, shape, 1) % LX
    at_last = x_pos == LX - 1
    at_first = x_pos == 0

    def one(row, carry):
        here = load_field(field_ref, row)
        ahead = combine(lambda v: jnp.where(at_last, roll(v, LX - 1), roll(v, -1)), here)
        ahead_x, hop = transport(links_at(links_ref, row, link_set, 0), ahead, here)
        total = combine(
            lambda v, f, h: f + jnp.where(at_first, roll(h, 1 - LX), roll(h, 1)) - 8.0 * v, here, ahead_x, hop
        )
        ahead = combine(lambda v: roll(v, -LX), here)
        ahead_y, hop = transport(links_at(links_ref, row, link_set, 1), ahead, here)
        total = combine(lambda s, f, h: s + f + roll(h, LX), total, ahead_y, hop)
        store_field(sum_ref, row, total)
        return carry

    lax.fori_loop(0, rows, one, 0)

    def between(row, carry):
        ahead_t, hop = transport(
            links_at(links_ref, row, link_set, 3), load_field(field_ref, row + 1), load_field(field_ref, row)
        )
        store_field(sum_ref, row, combine(lambda s, f: s + f, load_field(sum_ref, row), ahead_t))
        store_field(sum_ref, row + 1, combine(lambda s, h: s + h, load_field(sum_ref, row + 1), hop))
        return carry

    lax.fori_loop(0, rows - 1, between, 0)


def arrived_sum(links_ref, link_set, row, rows, arrivals):
    sum_ref, far_ref, near_ref, outer_ref, inner_ref = arrivals
    _, first_pos, odd_plane, odd_block = place(rows)
    far, near = load_field(far_ref, row), load_field(near_ref, row)
    above = combine(lambda p, q: jnp.where(odd_plane, p, q), far, near)
    ahead_z, _ = transport(links_at(links_ref, row, link_set, 2), above, None)
    total = combine(
        lambda s, f, p, q: s + f + jnp.where(odd_plane, q, p), load_field(sum_ref, row), ahead_z, far, near
    )
    outer, inner = load_field(outer_ref, 0), load_field(inner_ref, 0)
    if row == 0:
        exists = jnp.where(first_pos != 0, 1.0, 0.0)
        total = combine(lambda s, p, q: s + exists * jnp.where(odd_block, q, p), total, outer, inner)
    if row == rows - 1:
        exists = jnp.where(first_pos != BAND - rows, 1.0, 0.0)
        later = combine(lambda p, q: exists * jnp.where(odd_block, p, q), outer, inner)
        ahead_t, _ = transport(links_at(links_ref, row, link_set, 3), later, None)
        total = combine(lambda s, f: s + f, total, ahead_t)
    return total


def third_kernel(rows, coefs_ref, links_ref, *refs):
    arrivals, (third_ref, far_ref, near_ref, outer_ref, inner_ref) = refs[:5], refs[5:]
    for row in range(rows):
        inside, eps = coefs_ref[row], coefs_ref[rows]
        total = arrived_sum(links_ref, 2, row, rows, arrivals)
        third = combine(lambda s: 0.75 * (inside * (eps * s)), total)
        store_field(third_ref, row, third)
        store_z(rows, links_at(links_ref, row, 1, 2), row, third, far_ref, near_ref)
    store_t(rows, links_at(links_ref, rows - 1, 1, 3), third_ref, outer_ref, inner_ref)


def second_kernel(rows, coefs_ref, links_ref, *refs):
    arrivals, (start_ref, third_ref, mixed_ref, far_ref, near_ref, outer_ref, inner_ref, base_ref) = refs[:5], refs[5:]
    for row in range(rows):
        inside, eps = coefs_ref[row], coefs_ref[rows]
        total = arrived_sum(links_ref, 1, row, rows, arrivals)
        third = load_field(third_ref, row)
        second = combine(lambda v, s: v + (8.0 / 9.0) * (inside * (eps * s)), load_field(start_ref, row), total)
        mixed = combine(lambda p, q: 0.25 * p - (2.0 / 9.0) * q, second, third)
        store_field(mixed_ref, row, mixed)
        store_field(base_ref, row, combine(lambda p, q: p + q, second, third))
        store_z(rows, links_at(links_ref, row, 0, 2), row, mixed, far_ref, near_ref)
    store_t(rows, links_at(links_ref, rows - 1, 0, 3), mixed_ref, outer_ref, inner_ref)


def last_kernel(rows, coefs_ref, links_ref, *refs):
    arrivals, (base_ref, out_ref) = refs[:5], refs[5:]
    for row in range(rows):
        inside, eps = coefs_ref[row], coefs_ref[rows]
        total = arrived_sum(links_ref, 0, row, rows, arrivals)
        store_field(out_ref, row, combine(lambda p, s: p + inside * (eps * s), load_field(base_ref, row), total))


def call(kernel, name, operands, out_shapes, matvecs, space=pltpu.VMEM, scratch=()):
    vmem = pl.BlockSpec(memory_space=pltpu.VMEM)
    return pl.pallas_call(
        kernel,
        name=name,
        out_shape=out_shapes,
        in_specs=[pl.BlockSpec(memory_space=space)] * len(operands),
        out_specs=jax.tree.map(lambda _: vmem, out_shapes),
        scratch_shapes=scratch,
        cost_estimate=pl.CostEstimate(flops=matvecs * 72 * 1024, bytes_accessed=4096 * 18 * matvecs, transcendentals=0),
        compiler_params=pltpu.CompilerParams(vmem_limit_bytes=16 * 2**20),
    )(*operands)


def body(adjoint, flowed, source_slice, band_width, flow_steps):
    rows = adjoint.shape[0]
    per_plane = BAND // rows
    count = lax.axis_size("gz")
    links = jnp.transpose(flowed, (0, 1, 2, 4, 5, 3, 6)).reshape(-1, flowed.shape[-1])
    whole = jax.ShapeDtypeStruct(adjoint.shape, jnp.float32)
    one_row = jax.ShapeDtypeStruct((1,) + adjoint.shape[1:], jnp.float32)
    coefs = jax.ShapeDtypeStruct((rows + 1,) + adjoint.shape[3:], jnp.float32)

    def in_plane(i, by):
        return i - i % per_plane + (i + by) % per_plane

    def in_line(i, by):
        return (i + by * per_plane) % count

    far_pairs = [(i, in_line(i, 1 if i // per_plane % 2 else -1)) for i in range(count)]
    near_pairs = [(i, in_line(i, -1 if i // per_plane % 2 else 1)) for i in range(count)]
    outer_pairs = [(i, in_plane(i, 1 if i % 2 else -1)) for i in range(count)]
    inner_pairs = [(i, in_plane(i, -1 if i % 2 else 1)) for i in range(count)]

    def arrivals(link_set, field, far, near, outer, inner):
        far = lax.ppermute(far, "gz", far_pairs)
        near = lax.ppermute(near, "gz", near_pairs)
        outer = lax.ppermute(outer, "gz", outer_pairs)
        inner = lax.ppermute(inner, "gz", inner_pairs)
        total = call(functools.partial(local_kernel, rows, link_set), f"local_{link_set}", (field, links), whole, 22)
        return total, far, near, outer, inner

    sent = (whole, whole, one_row, one_row)
    copied = SETS * MUS * ENTRIES - (2 * MUS + 2) * ENTRIES // 8 * 8
    start, far, near, outer, inner, coefs = call(
        functools.partial(begin_kernel, rows), "begin", (source_slice, band_width, flow_steps, adjoint, links),
        (whole,) + sent + (coefs,), 5, pltpu.HBM,
        [pltpu.SMEM((1,), jnp.int32)] * 3
        + [
            pltpu.VMEM(adjoint.shape, jnp.float32),
            pltpu.VMEM((rows, copied, flowed.shape[-1]), jnp.float32),
            pltpu.SemaphoreType.DMA((4 + rows,)),
        ],
    )
    third, far, near, outer, inner = call(
        functools.partial(third_kernel, rows), "third",
        (coefs, links) + arrivals(2, start, far, near, outer, inner), (whole,) + sent, 10,
    )
    mixed, far, near, outer, inner, base = call(
        functools.partial(second_kernel, rows), "second",
        (coefs, links) + arrivals(1, third, far, near, outer, inner) + (start, third),
        (whole,) + sent + (whole,), 10,
    )
    return call(
        functools.partial(last_kernel, rows), "last",
        (coefs, links) + arrivals(0, mixed, far, near, outer, inner) + (base,), whole, 5,
    )


def solution(mesh):
    in_specs = (
        P(("cfg", "gz"), None, None, None, None),
        P(("cfg", "gz"), None, None, None, None, None, None),
        P("cfg"),
        P("cfg"),
        P("cfg"),
    )
    out_specs = P(("cfg", "gz"), None, None, None, None)
    return jax.shard_map(body, mesh=mesh, in_specs=in_specs, out_specs=out_specs, check_vma=False)
```

```python
import functools

import jax
import jax.numpy as jnp
from jax import lax
from jax.experimental import pallas as pl
from jax.experimental.pallas import tpu as pltpu
from jax.sharding import PartitionSpec as P

BAND = 32
LX = 8
SETS = 3
MUS = 4
ENTRIES = 18


def load_field(ref, row):
    return [[ref[row, c, a] for a in range(3)] for c in range(2)]


def store_field(ref, row, field):
    for c in range(2):
        for a in range(3):
            ref[row, c, a] = field[c][a]


def combine(function, *fields):
    return [[function(*(f[c][a] for f in fields)) for a in range(3)] for c in range(2)]


def links_at(links_ref, row, link_set, mu):
    return links_ref, ((row * SETS + link_set) * MUS + mu) * ENTRIES


def entry(matrices, a, b, c, shape):
    ref, base = matrices
    return jnp.broadcast_to(ref[pl.ds(base + (a * 3 + b) * 2 + c, 1), :], shape)


def transport(matrices, ahead, here):
    forward = [[None] * 3, [None] * 3]
    backward = [[None] * 3, [None] * 3]
    shape = (ahead if ahead is not None else here)[0][0].shape

    def add(total, c, a, value):
        total[c][a] = value if total[c][a] is None else total[c][a] + value

    for a in range(3):
        for b in range(3):
            real = entry(matrices, a, b, 0, shape)
            imag = entry(matrices, a, b, 1, shape)
            if ahead is not None:
                add(forward, 0, a, real * ahead[0][b] - imag * ahead[1][b])
                add(forward, 1, a, real * ahead[1][b] + imag * ahead[0][b])
            if here is not None:
                add(backward, 0, b, real * here[0][a] + imag * here[1][a])
                add(backward, 1, b, real * here[1][a] - imag * here[0][a])
    return forward, backward


def roll(plane, by):
    return pltpu.roll(plane, by % plane.shape[-1], plane.ndim - 1)


def place(rows):
    first = lax.axis_index("gz") * rows
    plane, first_pos = first // BAND, lax.rem(first, BAND)
    return plane, first_pos, lax.rem(plane, 2) == 1, lax.rem(first_pos // rows, 2) == 1


def taper_kernel(rows, source_ref, width_ref, steps_ref, coefs_ref):
    _, first_pos, _, _ = place(rows)
    ones = jnp.ones((8, 128), jnp.float32)
    per_width = ones * width_ref[0].astype(jnp.float32)
    for i in range(rows + 2):
        distance = ones * (first_pos + i - 1 - source_ref[0]).astype(jnp.float32) / per_width
        coefs_ref[i] = 1.0 / (1.0 + distance * distance)
    coefs_ref[rows + 2] = 0.25 / (ones * steps_ref[0].astype(jnp.float32))


def store_z(rows, matrices, row, field, far_ref, near_ref):
    _, _, odd_plane, _ = place(rows)
    _, up = transport(matrices, None, field)
    store_field(far_ref, row, combine(lambda v, h: jnp.where(odd_plane, h, v), field, up))
    store_field(near_ref, row, combine(lambda v, h: jnp.where(odd_plane, v, h), field, up))


def store_t(rows, matrices, field_ref, outer_ref, inner_ref):
    _, _, _, odd_block = place(rows)
    first = load_field(field_ref, 0)
    _, last = transport(matrices, None, load_field(field_ref, rows - 1))
    store_field(outer_ref, 0, combine(lambda p, q: jnp.where(odd_block, q, p), first, last))
    store_field(inner_ref, 0, combine(lambda p, q: jnp.where(odd_block, p, q), first, last))


def begin_kernel(
    rows, adjoint_hbm, links_hbm, far_ref, near_ref, outer_ref, inner_ref, adjoint_ref, links_ref, sems
):
    row_entries = SETS * MUS * ENTRIES
    z_first = (2 * MUS + 2) * ENTRIES
    aligned = z_first // 8 * 8
    copies = [pltpu.make_async_copy(adjoint_hbm, adjoint_ref, sems.at[rows])]
    for row in range(rows):
        part = links_hbm.at[pl.ds(row * row_entries + aligned, row_entries - aligned), :]
        copies.append(pltpu.make_async_copy(part, links_ref.at[row], sems.at[row]))
    for copy in copies:
        copy.start()
    for copy in copies:
        copy.wait()
    for row in range(rows):
        matrices = links_ref.at[row], z_first - aligned
        store_z(rows, matrices, row, load_field(adjoint_ref, row), far_ref, near_ref)
    store_t(rows, (links_ref.at[rows - 1], z_first + ENTRIES - aligned), adjoint_ref, outer_ref, inner_ref)


def start_kernel(rows, link_set, coefs_ref, adjoint_ref, links_ref, sum_ref, start_ref):
    for row in range(rows):
        inside = coefs_ref[row + 1]
        store_field(start_ref, row, combine(lambda v: inside * v, load_field(adjoint_ref, row)))
    local_kernel(rows, link_set, start_ref, links_ref, sum_ref)


def local_kernel(rows, link_set, field_ref, links_ref, sum_ref):
    shape = field_ref.shape[-2:]
    x_pos = lax.broadcasted_iota(jnp.int32, shape, 1) % LX
    at_last = x_pos == LX - 1
    at_first = x_pos == 0

    def one(row, carry):
        here = load_field(field_ref, row)
        ahead = combine(lambda v: jnp.where(at_last, roll(v, LX - 1), roll(v, -1)), here)
        ahead_x, hop = transport(links_at(links_ref, row, link_set, 0), ahead, here)
        total = combine(
            lambda v, f, h: f + jnp.where(at_first, roll(h, 1 - LX), roll(h, 1)) - 8.0 * v, here, ahead_x, hop
        )
        ahead = combine(lambda v: roll(v, -LX), here)
        ahead_y, hop = transport(links_at(links_ref, row, link_set, 1), ahead, here)
        total = combine(lambda s, f, h: s + f + roll(h, LX), total, ahead_y, hop)
        store_field(sum_ref, row, total)
        return carry

    lax.fori_loop(0, rows, one, 0)

    def between(row, carry):
        ahead_t, hop = transport(
            links_at(links_ref, row, link_set, 3), load_field(field_ref, row + 1), load_field(field_ref, row)
        )
        store_field(sum_ref, row, combine(lambda s, f: s + f, load_field(sum_ref, row), ahead_t))
        store_field(sum_ref, row + 1, combine(lambda s, h: s + h, load_field(sum_ref, row + 1), hop))
        return carry

    lax.fori_loop(0, rows - 1, between, 0)


def arrived_sum(links_ref, link_set, row, rows, arrivals, coefs_ref=None):
    sum_ref, far_ref, near_ref, outer_ref, inner_ref = arrivals
    _, first_pos, odd_plane, odd_block = place(rows)
    far, near = load_field(far_ref, row), load_field(near_ref, row)
    if coefs_ref is not None:
        far, near = (combine(lambda v: coefs_ref[row + 1] * v, f) for f in (far, near))
    above = combine(lambda p, q: jnp.where(odd_plane, p, q), far, near)
    ahead_z, _ = transport(links_at(links_ref, row, link_set, 2), above, None)
    total = combine(
        lambda s, f, p, q: s + f + jnp.where(odd_plane, q, p), load_field(sum_ref, row), ahead_z, far, near
    )
    outer, inner = load_field(outer_ref, 0), load_field(inner_ref, 0)
    if row == 0:
        exists = jnp.where(first_pos != 0, 1.0, 0.0)
        if coefs_ref is not None:
            exists = exists * coefs_ref[0]
        total = combine(lambda s, p, q: s + exists * jnp.where(odd_block, q, p), total, outer, inner)
    if row == rows - 1:
        exists = jnp.where(first_pos != BAND - rows, 1.0, 0.0)
        if coefs_ref is not None:
            exists = exists * coefs_ref[rows + 1]
        later = combine(lambda p, q: exists * jnp.where(odd_block, p, q), outer, inner)
        ahead_t, _ = transport(links_at(links_ref, row, link_set, 3), later, None)
        total = combine(lambda s, f: s + f, total, ahead_t)
    return total


def third_kernel(rows, coefs_ref, links_ref, *refs):
    arrivals, (third_ref, far_ref, near_ref, outer_ref, inner_ref) = refs[:5], refs[5:]
    for row in range(rows):
        inside, eps = coefs_ref[row + 1], coefs_ref[rows + 2]
        total = arrived_sum(links_ref, 2, row, rows, arrivals, coefs_ref)
        third = combine(lambda s: 0.75 * (inside * (eps * s)), total)
        store_field(third_ref, row, third)
        store_z(rows, links_at(links_ref, row, 1, 2), row, third, far_ref, near_ref)
    store_t(rows, links_at(links_ref, rows - 1, 1, 3), third_ref, outer_ref, inner_ref)


def second_kernel(rows, coefs_ref, links_ref, *refs):
    arrivals, (start_ref, third_ref, mixed_ref, far_ref, near_ref, outer_ref, inner_ref, base_ref) = refs[:5], refs[5:]
    for row in range(rows):
        inside, eps = coefs_ref[row + 1], coefs_ref[rows + 2]
        total = arrived_sum(links_ref, 1, row, rows, arrivals)
        third = load_field(third_ref, row)
        second = combine(lambda v, s: v + (8.0 / 9.0) * (inside * (eps * s)), load_field(start_ref, row), total)
        mixed = combine(lambda p, q: 0.25 * p - (2.0 / 9.0) * q, second, third)
        store_field(mixed_ref, row, mixed)
        store_field(base_ref, row, combine(lambda p, q: p + q, second, third))
        store_z(rows, links_at(links_ref, row, 0, 2), row, mixed, far_ref, near_ref)
    store_t(rows, links_at(links_ref, rows - 1, 0, 3), mixed_ref, outer_ref, inner_ref)


def last_kernel(rows, coefs_ref, links_ref, *refs):
    arrivals, (base_ref, out_ref) = refs[:5], refs[5:]
    for row in range(rows):
        inside, eps = coefs_ref[row + 1], coefs_ref[rows + 2]
        total = arrived_sum(links_ref, 0, row, rows, arrivals)
        store_field(out_ref, row, combine(lambda p, s: p + inside * (eps * s), load_field(base_ref, row), total))


def call(kernel, name, operands, out_shapes, matvecs, space=pltpu.VMEM, scratch=()):
    vmem = pl.BlockSpec(memory_space=pltpu.VMEM)
    return pl.pallas_call(
        kernel,
        name=name,
        out_shape=out_shapes,
        in_specs=[pl.BlockSpec(memory_space=space)] * len(operands),
        out_specs=jax.tree.map(lambda _: vmem, out_shapes),
        scratch_shapes=scratch,
        cost_estimate=pl.CostEstimate(flops=matvecs * 72 * 1024, bytes_accessed=4096 * 18 * matvecs, transcendentals=0),
        compiler_params=pltpu.CompilerParams(vmem_limit_bytes=16 * 2**20),
    )(*operands)


def body(adjoint, flowed, source_slice, band_width, flow_steps):
    rows = adjoint.shape[0]
    per_plane = BAND // rows
    count = lax.axis_size("gz")
    links = jnp.transpose(flowed, (0, 1, 2, 4, 5, 3, 6)).reshape(-1, flowed.shape[-1])
    whole = jax.ShapeDtypeStruct(adjoint.shape, jnp.float32)
    one_row = jax.ShapeDtypeStruct((1,) + adjoint.shape[1:], jnp.float32)
    coefs_shape = jax.ShapeDtypeStruct((rows + 3,) + adjoint.shape[3:], jnp.float32)

    def in_plane(i, by):
        return i - i % per_plane + (i + by) % per_plane

    def in_line(i, by):
        return (i + by * per_plane) % count

    far_pairs = [(i, in_line(i, 1 if i // per_plane % 2 else -1)) for i in range(count)]
    near_pairs = [(i, in_line(i, -1 if i // per_plane % 2 else 1)) for i in range(count)]
    outer_pairs = [(i, in_plane(i, 1 if i % 2 else -1)) for i in range(count)]
    inner_pairs = [(i, in_plane(i, -1 if i % 2 else 1)) for i in range(count)]

    def sent_on(far, near, outer, inner):
        return (
            lax.ppermute(far, "gz", far_pairs),
            lax.ppermute(near, "gz", near_pairs),
            lax.ppermute(outer, "gz", outer_pairs),
            lax.ppermute(inner, "gz", inner_pairs),
        )

    def local(link_set, field):
        return call(functools.partial(local_kernel, rows, link_set), f"local_{link_set}", (field, links), whole, 22)

    sent = (whole, whole, one_row, one_row)
    copied = SETS * MUS * ENTRIES - (2 * MUS + 2) * ENTRIES // 8 * 8
    sending = call(
        functools.partial(begin_kernel, rows), "begin",
        tuple(pltpu.with_memory_space_constraint(a, pltpu.HBM) for a in (adjoint, links)), sent, 5, pltpu.HBM,
        [
            pltpu.VMEM(adjoint.shape, jnp.float32),
            pltpu.VMEM((rows, copied, flowed.shape[-1]), jnp.float32),
            pltpu.SemaphoreType.DMA((rows + 1,)),
        ],
    )
    arrived = sent_on(*sending)
    coefs = call(
        functools.partial(taper_kernel, rows), "tapers", (source_slice, band_width, flow_steps), coefs_shape, 1,
        pltpu.SMEM,
    )
    total, start = call(
        functools.partial(start_kernel, rows, 2), "start", (coefs, adjoint, links), (whole, whole), 22
    )
    third, *sending = call(
        functools.partial(third_kernel, rows), "third", (coefs, links, total) + arrived, (whole,) + sent, 10
    )
    arrived = sent_on(*sending)
    mixed, *sending, base = call(
        functools.partial(second_kernel, rows), "second", (coefs, links, local(1, third)) + arrived + (start, third),
        (whole,) + sent + (whole,), 10,
    )
    arrived = sent_on(*sending)
    return call(
        functools.partial(last_kernel, rows), "last", (coefs, links, local(0, mixed)) + arrived + (base,), whole, 5
    )


def solution(mesh):
    in_specs = (
        P(("cfg", "gz"), None, None, None, None),
        P(("cfg", "gz"), None, None, None, None, None, None),
        P("cfg"),
        P("cfg"),
        P("cfg"),
    )
    out_specs = P(("cfg", "gz"), None, None, None, None)
    return jax.shard_map(body, mesh=mesh, in_specs=in_specs, out_specs=out_specs, check_vma=False)
```

```python
import functools

import jax
import jax.numpy as jnp
from jax import lax
from jax.experimental import pallas as pl
from jax.experimental.pallas import tpu as pltpu
from jax.sharding import PartitionSpec as P

BAND = 32
LX = 8
SETS = 3
MUS = 4
ENTRIES = 18


def load_field(ref, row):
    return [[ref[row, c, a] for a in range(3)] for c in range(2)]


def store_field(ref, row, field):
    for c in range(2):
        for a in range(3):
            ref[row, c, a] = field[c][a]


def combine(function, *fields):
    return [[function(*(f[c][a] for f in fields)) for a in range(3)] for c in range(2)]


def links_at(links_ref, row, link_set, mu):
    return links_ref, ((row * SETS + link_set) * MUS + mu) * ENTRIES


def entry(matrices, a, b, c, shape):
    ref, base = matrices
    return jnp.broadcast_to(ref[pl.ds(base + (a * 3 + b) * 2 + c, 1), :], shape)


def transport(matrices, ahead, here):
    forward = [[None] * 3, [None] * 3]
    backward = [[None] * 3, [None] * 3]
    shape = (ahead if ahead is not None else here)[0][0].shape

    def add(total, c, a, value):
        total[c][a] = value if total[c][a] is None else total[c][a] + value

    for a in range(3):
        for b in range(3):
            real = entry(matrices, a, b, 0, shape)
            imag = entry(matrices, a, b, 1, shape)
            if ahead is not None:
                add(forward, 0, a, real * ahead[0][b] - imag * ahead[1][b])
                add(forward, 1, a, real * ahead[1][b] + imag * ahead[0][b])
            if here is not None:
                add(backward, 0, b, real * here[0][a] + imag * here[1][a])
                add(backward, 1, b, real * here[1][a] - imag * here[0][a])
    return forward, backward


def roll(plane, by):
    return pltpu.roll(plane, by % plane.shape[-1], plane.ndim - 1)


def place(rows):
    first = lax.axis_index("gz") * rows
    plane, first_pos = first // BAND, lax.rem(first, BAND)
    return plane, first_pos, lax.rem(plane, 2) == 1, lax.rem(first_pos // rows, 2) == 1


def taper_kernel(rows, source_ref, width_ref, steps_ref, coefs_ref):
    _, first_pos, _, _ = place(rows)
    ones = jnp.ones((8, 128), jnp.float32)
    per_width = ones * width_ref[0].astype(jnp.float32)
    for i in range(rows + 2):
        distance = ones * (first_pos + i - 1 - source_ref[0]).astype(jnp.float32) / per_width
        coefs_ref[i] = 1.0 / (1.0 + distance * distance)
    coefs_ref[rows + 2] = 0.25 / (ones * steps_ref[0].astype(jnp.float32))


def store_z(rows, matrices, row, field, far_ref, near_ref):
    _, _, odd_plane, _ = place(rows)
    _, up = transport(matrices, None, field)
    store_field(far_ref, row, combine(lambda v, h: jnp.where(odd_plane, h, v), field, up))
    store_field(near_ref, row, combine(lambda v, h: jnp.where(odd_plane, v, h), field, up))


def store_t(rows, matrices, field_ref, outer_ref, inner_ref):
    _, _, _, odd_block = place(rows)
    first = load_field(field_ref, 0)
    _, last = transport(matrices, None, load_field(field_ref, rows - 1))
    store_field(outer_ref, 0, combine(lambda p, q: jnp.where(odd_block, q, p), first, last))
    store_field(inner_ref, 0, combine(lambda p, q: jnp.where(odd_block, p, q), first, last))


def begin_kernel(
    rows, adjoint_hbm, links_hbm, far_ref, near_ref, outer_ref, inner_ref, adjoint_ref, links_ref, sems
):
    row_entries = SETS * MUS * ENTRIES
    z_first = (2 * MUS + 2) * ENTRIES
    aligned = z_first // 8 * 8
    copies = [pltpu.make_async_copy(adjoint_hbm, adjoint_ref, sems.at[rows])]
    for row in range(rows):
        part = links_hbm.at[pl.ds(row * row_entries + aligned, row_entries - aligned), :]
        copies.append(pltpu.make_async_copy(part, links_ref.at[row], sems.at[row]))
    for copy in copies:
        copy.start()
    for copy in copies:
        copy.wait()
    for row in range(rows):
        matrices = links_ref.at[row], z_first - aligned
        store_z(rows, matrices, row, load_field(adjoint_ref, row), far_ref, near_ref)
    store_t(rows, (links_ref.at[rows - 1], z_first + ENTRIES - aligned), adjoint_ref, outer_ref, inner_ref)


def start_kernel(rows, link_set, coefs_ref, adjoint_ref, links_ref, sum_ref, start_ref):
    for row in range(rows):
        inside = coefs_ref[row + 1]
        store_field(start_ref, row, combine(lambda v: inside * v, load_field(adjoint_ref, row)))
    local_kernel(rows, link_set, start_ref, links_ref, sum_ref)


def local_kernel(rows, link_set, field_ref, links_ref, sum_ref):
    shape = field_ref.shape[-2:]
    x_pos = lax.broadcasted_iota(jnp.int32, shape, 1) % LX
    at_last = x_pos == LX - 1
    at_first = x_pos == 0

    def one(row, carry):
        here = load_field(field_ref, row)
        ahead = combine(lambda v: jnp.where(at_last, roll(v, LX - 1), roll(v, -1)), here)
        ahead_x, hop = transport(links_at(links_ref, row, link_set, 0), ahead, here)
        total = combine(
            lambda v, f, h: f + jnp.where(at_first, roll(h, 1 - LX), roll(h, 1)) - 8.0 * v, here, ahead_x, hop
        )
        ahead = combine(lambda v: roll(v, -LX), here)
        ahead_y, hop = transport(links_at(links_ref, row, link_set, 1), ahead, here)
        total = combine(lambda s, f, h: s + f + roll(h, LX), total, ahead_y, hop)
        store_field(sum_ref, row, total)
        return carry

    lax.fori_loop(0, rows, one, 0)

    def between(row, carry):
        ahead_t, hop = transport(
            links_at(links_ref, row, link_set, 3), load_field(field_ref, row + 1), load_field(field_ref, row)
        )
        store_field(sum_ref, row, combine(lambda s, f: s + f, load_field(sum_ref, row), ahead_t))
        store_field(sum_ref, row + 1, combine(lambda s, h: s + h, load_field(sum_ref, row + 1), hop))
        return carry

    lax.fori_loop(0, rows - 1, between, 0)


def arrived_sum(links_ref, link_set, row, rows, arrivals, coefs_ref=None):
    sum_ref, far_ref, near_ref, outer_ref, inner_ref = arrivals
    _, first_pos, odd_plane, odd_block = place(rows)
    far, near = load_field(far_ref, row), load_field(near_ref, row)
    if coefs_ref is not None:
        far, near = (combine(lambda v: coefs_ref[row + 1] * v, f) for f in (far, near))
    above = combine(lambda p, q: jnp.where(odd_plane, p, q), far, near)
    ahead_z, _ = transport(links_at(links_ref, row, link_set, 2), above, None)
    total = combine(
        lambda s, f, p, q: s + f + jnp.where(odd_plane, q, p), load_field(sum_ref, row), ahead_z, far, near
    )
    outer, inner = load_field(outer_ref, 0), load_field(inner_ref, 0)
    if row == 0:
        exists = jnp.where(first_pos != 0, 1.0, 0.0)
        if coefs_ref is not None:
            exists = exists * coefs_ref[0]
        total = combine(lambda s, p, q: s + exists * jnp.where(odd_block, q, p), total, outer, inner)
    if row == rows - 1:
        exists = jnp.where(first_pos != BAND - rows, 1.0, 0.0)
        if coefs_ref is not None:
            exists = exists * coefs_ref[rows + 1]
        later = combine(lambda p, q: exists * jnp.where(odd_block, p, q), outer, inner)
        ahead_t, _ = transport(links_at(links_ref, row, link_set, 3), later, None)
        total = combine(lambda s, f: s + f, total, ahead_t)
    return total


def third_kernel(rows, coefs_ref, links_ref, *refs):
    arrivals, (third_ref, far_ref, near_ref, outer_ref, inner_ref) = refs[:5], refs[5:]
    for row in range(rows):
        inside, eps = coefs_ref[row + 1], coefs_ref[rows + 2]
        total = arrived_sum(links_ref, 2, row, rows, arrivals, coefs_ref)
        third = combine(lambda s: 0.75 * (inside * (eps * s)), total)
        store_field(third_ref, row, third)
        store_z(rows, links_at(links_ref, row, 1, 2), row, third, far_ref, near_ref)
    store_t(rows, links_at(links_ref, rows - 1, 1, 3), third_ref, outer_ref, inner_ref)


def second_kernel(rows, coefs_ref, links_ref, *refs):
    arrivals, (start_ref, third_ref, mixed_ref, far_ref, near_ref, outer_ref, inner_ref, base_ref) = refs[:5], refs[5:]
    for row in range(rows):
        inside, eps = coefs_ref[row + 1], coefs_ref[rows + 2]
        total = arrived_sum(links_ref, 1, row, rows, arrivals)
        third = load_field(third_ref, row)
        second = combine(lambda v, s: v + (8.0 / 9.0) * (inside * (eps * s)), load_field(start_ref, row), total)
        mixed = combine(lambda p, q: 0.25 * p - (2.0 / 9.0) * q, second, third)
        store_field(mixed_ref, row, mixed)
        store_field(base_ref, row, combine(lambda p, q: p + q, second, third))
        store_z(rows, links_at(links_ref, row, 0, 2), row, mixed, far_ref, near_ref)
    store_t(rows, links_at(links_ref, rows - 1, 0, 3), mixed_ref, outer_ref, inner_ref)


def last_kernel(rows, coefs_ref, links_ref, *refs):
    arrivals, (base_ref, out_ref) = refs[:5], refs[5:]
    for row in range(rows):
        inside, eps = coefs_ref[row + 1], coefs_ref[rows + 2]
        total = arrived_sum(links_ref, 0, row, rows, arrivals)
        store_field(out_ref, row, combine(lambda p, s: p + inside * (eps * s), load_field(base_ref, row), total))


def call(kernel, name, operands, out_shapes, matvecs, space=pltpu.VMEM, scratch=()):
    vmem = pl.BlockSpec(memory_space=pltpu.VMEM)
    return pl.pallas_call(
        kernel,
        name=name,
        out_shape=out_shapes,
        in_specs=[pl.BlockSpec(memory_space=space)] * len(operands),
        out_specs=jax.tree.map(lambda _: vmem, out_shapes),
        scratch_shapes=scratch,
        cost_estimate=pl.CostEstimate(flops=matvecs * 72 * 1024, bytes_accessed=4096 * 18 * matvecs, transcendentals=0),
        compiler_params=pltpu.CompilerParams(vmem_limit_bytes=16 * 2**20),
    )(*operands)


def body(adjoint, flowed, source_slice, band_width, flow_steps):
    rows = adjoint.shape[0]
    per_plane = BAND // rows
    count = lax.axis_size("gz")
    links = jnp.transpose(flowed, (0, 1, 2, 4, 5, 3, 6)).reshape(-1, flowed.shape[-1])
    whole = jax.ShapeDtypeStruct(adjoint.shape, jnp.float32)
    one_row = jax.ShapeDtypeStruct((1,) + adjoint.shape[1:], jnp.float32)
    coefs_shape = jax.ShapeDtypeStruct((rows + 3,) + adjoint.shape[3:], jnp.float32)

    def in_plane(i, by):
        return i - i % per_plane + (i + by) % per_plane

    def in_line(i, by):
        return (i + by * per_plane) % count

    far_pairs = [(i, in_line(i, 1 if i // per_plane % 2 else -1)) for i in range(count)]
    near_pairs = [(i, in_line(i, -1 if i // per_plane % 2 else 1)) for i in range(count)]
    outer_pairs = [(i, in_plane(i, 1 if i % 2 else -1)) for i in range(count)]
    inner_pairs = [(i, in_plane(i, -1 if i % 2 else 1)) for i in range(count)]

    def sent_on(far, near, outer, inner):
        near = lax.ppermute(near, "gz", near_pairs)
        far = lax.ppermute(far, "gz", far_pairs)
        outer = lax.ppermute(outer, "gz", outer_pairs)
        inner = lax.ppermute(inner, "gz", inner_pairs)
        return far, near, outer, inner

    def local(link_set, field):
        return call(functools.partial(local_kernel, rows, link_set), f"local_{link_set}", (field, links), whole, 22)

    sent = (whole, whole, one_row, one_row)
    copied = SETS * MUS * ENTRIES - (2 * MUS + 2) * ENTRIES // 8 * 8
    sending = call(
        functools.partial(begin_kernel, rows), "begin",
        tuple(pltpu.with_memory_space_constraint(a, pltpu.HBM) for a in (adjoint, links)), sent, 5, pltpu.HBM,
        [
            pltpu.VMEM(adjoint.shape, jnp.float32),
            pltpu.VMEM((rows, copied, flowed.shape[-1]), jnp.float32),
            pltpu.SemaphoreType.DMA((rows + 1,)),
        ],
    )
    arrived = sent_on(*sending)
    coefs = call(
        functools.partial(taper_kernel, rows), "tapers", (source_slice, band_width, flow_steps), coefs_shape, 1,
        pltpu.SMEM,
    )
    total, start = call(
        functools.partial(start_kernel, rows, 2), "start", (coefs, adjoint, links), (whole, whole), 22
    )
    third, *sending = call(
        functools.partial(third_kernel, rows), "third", (coefs, links, total) + arrived, (whole,) + sent, 10
    )
    arrived = sent_on(*sending)
    mixed, *sending, base = call(
        functools.partial(second_kernel, rows), "second", (coefs, links, local(1, third)) + arrived + (start, third),
        (whole,) + sent + (whole,), 10,
    )
    arrived = sent_on(*sending)
    return call(
        functools.partial(last_kernel, rows), "last", (coefs, links, local(0, mixed)) + arrived + (base,), whole, 5
    )


def solution(mesh):
    in_specs = (
        P(("cfg", "gz"), None, None, None, None),
        P(("cfg", "gz"), None, None, None, None, None, None),
        P("cfg"),
        P("cfg"),
        P("cfg"),
    )
    out_specs = P(("cfg", "gz"), None, None, None, None)
    return jax.shard_map(body, mesh=mesh, in_specs=in_specs, out_specs=out_specs, check_vma=False)
```

```python
import functools

import jax
import jax.numpy as jnp
from jax import lax
from jax.experimental import pallas as pl
from jax.experimental.pallas import tpu as pltpu
from jax.sharding import PartitionSpec as P

BAND = 32
LX = 8
SETS = 3
MUS = 4
ENTRIES = 18


def load_field(ref, row):
    return [[ref[row, c, a] for a in range(3)] for c in range(2)]


def store_field(ref, row, field):
    for c in range(2):
        for a in range(3):
            ref[row, c, a] = field[c][a]


def combine(function, *fields):
    return [[function(*(f[c][a] for f in fields)) for a in range(3)] for c in range(2)]


def links_at(links_ref, row, link_set, mu):
    return links_ref, ((row * SETS + link_set) * MUS + mu) * ENTRIES


def entry(matrices, a, b, c, shape):
    ref, base = matrices
    return jnp.broadcast_to(ref[pl.ds(base + (a * 3 + b) * 2 + c, 1), :], shape)


def transport(matrices, ahead, here):
    forward = [[None] * 3, [None] * 3]
    backward = [[None] * 3, [None] * 3]
    shape = (ahead if ahead is not None else here)[0][0].shape

    def add(total, c, a, value):
        total[c][a] = value if total[c][a] is None else total[c][a] + value

    for a in range(3):
        for b in range(3):
            real = entry(matrices, a, b, 0, shape)
            imag = entry(matrices, a, b, 1, shape)
            if ahead is not None:
                add(forward, 0, a, real * ahead[0][b] - imag * ahead[1][b])
                add(forward, 1, a, real * ahead[1][b] + imag * ahead[0][b])
            if here is not None:
                add(backward, 0, b, real * here[0][a] + imag * here[1][a])
                add(backward, 1, b, real * here[1][a] - imag * here[0][a])
    return forward, backward


def roll(plane, by):
    return pltpu.roll(plane, by % plane.shape[-1], plane.ndim - 1)


def place(rows):
    first = lax.axis_index("gz") * rows
    plane, first_pos = first // BAND, lax.rem(first, BAND)
    return plane, first_pos, lax.rem(plane, 2) == 1, lax.rem(first_pos // rows, 2) == 1


def taper_kernel(rows, source_ref, width_ref, steps_ref, coefs_ref):
    _, first_pos, _, _ = place(rows)
    ones = jnp.ones((8, 128), jnp.float32)
    per_width = ones * width_ref[0].astype(jnp.float32)
    for i in range(rows + 2):
        distance = ones * (first_pos + i - 1 - source_ref[0]).astype(jnp.float32) / per_width
        coefs_ref[i] = 1.0 / (1.0 + distance * distance)
    coefs_ref[rows + 2] = 0.25 / (ones * steps_ref[0].astype(jnp.float32))


def store_z(rows, matrices, row, field, far_ref, near_ref):
    _, _, odd_plane, _ = place(rows)
    _, up = transport(matrices, None, field)
    store_field(far_ref, row, combine(lambda v, h: jnp.where(odd_plane, h, v), field, up))
    store_field(near_ref, row, combine(lambda v, h: jnp.where(odd_plane, v, h), field, up))


def store_t(rows, matrices, field_ref, outer_ref, inner_ref):
    _, _, _, odd_block = place(rows)
    first = load_field(field_ref, 0)
    _, last = transport(matrices, None, load_field(field_ref, rows - 1))
    store_field(outer_ref, 0, combine(lambda p, q: jnp.where(odd_block, q, p), first, last))
    store_field(inner_ref, 0, combine(lambda p, q: jnp.where(odd_block, p, q), first, last))


def begin_kernel(
    rows, adjoint_hbm, links_hbm, far_ref, near_ref, outer_ref, inner_ref, adjoint_ref, links_ref, sems
):
    row_entries = SETS * MUS * ENTRIES
    z_first = (2 * MUS + 2) * ENTRIES
    aligned = z_first // 8 * 8
    copies = [pltpu.make_async_copy(adjoint_hbm, adjoint_ref, sems.at[rows])]
    for row in range(rows):
        part = links_hbm.at[pl.ds(row * row_entries + aligned, row_entries - aligned), :]
        copies.append(pltpu.make_async_copy(part, links_ref.at[row], sems.at[row]))
    for copy in copies:
        copy.start()
    for copy in copies:
        copy.wait()
    for row in range(rows):
        matrices = links_ref.at[row], z_first - aligned
        store_z(rows, matrices, row, load_field(adjoint_ref, row), far_ref, near_ref)
    store_t(rows, (links_ref.at[rows - 1], z_first + ENTRIES - aligned), adjoint_ref, outer_ref, inner_ref)


def start_kernel(rows, link_set, coefs_ref, adjoint_ref, links_ref, sum_ref, start_ref):
    for row in range(rows):
        inside = coefs_ref[row + 1]
        store_field(start_ref, row, combine(lambda v: inside * v, load_field(adjoint_ref, row)))
    local_kernel(rows, link_set, start_ref, links_ref, sum_ref)


def local_kernel(rows, link_set, field_ref, links_ref, sum_ref):
    shape = field_ref.shape[-2:]
    x_pos = lax.broadcasted_iota(jnp.int32, shape, 1) % LX
    at_last = x_pos == LX - 1
    at_first = x_pos == 0

    def one(row, carry):
        here = load_field(field_ref, row)
        ahead = combine(lambda v: jnp.where(at_last, roll(v, LX - 1), roll(v, -1)), here)
        ahead_x, hop = transport(links_at(links_ref, row, link_set, 0), ahead, here)
        total = combine(
            lambda v, f, h: f + jnp.where(at_first, roll(h, 1 - LX), roll(h, 1)) - 8.0 * v, here, ahead_x, hop
        )
        ahead = combine(lambda v: roll(v, -LX), here)
        ahead_y, hop = transport(links_at(links_ref, row, link_set, 1), ahead, here)
        total = combine(lambda s, f, h: s + f + roll(h, LX), total, ahead_y, hop)
        store_field(sum_ref, row, total)
        return carry

    lax.fori_loop(0, rows, one, 0)

    def between(row, carry):
        ahead_t, hop = transport(
            links_at(links_ref, row, link_set, 3), load_field(field_ref, row + 1), load_field(field_ref, row)
        )
        store_field(sum_ref, row, combine(lambda s, f: s + f, load_field(sum_ref, row), ahead_t))
        store_field(sum_ref, row + 1, combine(lambda s, h: s + h, load_field(sum_ref, row + 1), hop))
        return carry

    lax.fori_loop(0, rows - 1, between, 0)


def arrived_sum(links_ref, link_set, row, rows, arrivals, coefs_ref=None):
    sum_ref, near_ref, far_ref, outer_ref, inner_ref = arrivals
    _, first_pos, odd_plane, odd_block = place(rows)
    far, near = load_field(far_ref, row), load_field(near_ref, row)
    if coefs_ref is not None:
        far, near = (combine(lambda v: coefs_ref[row + 1] * v, f) for f in (far, near))
    above = combine(lambda p, q: jnp.where(odd_plane, p, q), far, near)
    ahead_z, _ = transport(links_at(links_ref, row, link_set, 2), above, None)
    total = combine(
        lambda s, f, p, q: s + f + jnp.where(odd_plane, q, p), load_field(sum_ref, row), ahead_z, far, near
    )
    outer, inner = load_field(outer_ref, 0), load_field(inner_ref, 0)
    if row == 0:
        exists = jnp.where(first_pos != 0, 1.0, 0.0)
        if coefs_ref is not None:
            exists = exists * coefs_ref[0]
        total = combine(lambda s, p, q: s + exists * jnp.where(odd_block, q, p), total, outer, inner)
    if row == rows - 1:
        exists = jnp.where(first_pos != BAND - rows, 1.0, 0.0)
        if coefs_ref is not None:
            exists = exists * coefs_ref[rows + 1]
        later = combine(lambda p, q: exists * jnp.where(odd_block, p, q), outer, inner)
        ahead_t, _ = transport(links_at(links_ref, row, link_set, 3), later, None)
        total = combine(lambda s, f: s + f, total, ahead_t)
    return total


def third_kernel(rows, coefs_ref, links_ref, *refs):
    arrivals, (third_ref, far_ref, near_ref, outer_ref, inner_ref) = refs[:5], refs[5:]
    for row in range(rows):
        inside, eps = coefs_ref[row + 1], coefs_ref[rows + 2]
        total = arrived_sum(links_ref, 2, row, rows, arrivals, coefs_ref)
        third = combine(lambda s: 0.75 * (inside * (eps * s)), total)
        store_field(third_ref, row, third)
        store_z(rows, links_at(links_ref, row, 1, 2), row, third, far_ref, near_ref)
    store_t(rows, links_at(links_ref, rows - 1, 1, 3), third_ref, outer_ref, inner_ref)


def second_kernel(rows, coefs_ref, links_ref, *refs):
    arrivals, (start_ref, third_ref, mixed_ref, far_ref, near_ref, outer_ref, inner_ref, base_ref) = refs[:5], refs[5:]
    for row in range(rows):
        inside, eps = coefs_ref[row + 1], coefs_ref[rows + 2]
        total = arrived_sum(links_ref, 1, row, rows, arrivals)
        third = load_field(third_ref, row)
        second = combine(lambda v, s: v + (8.0 / 9.0) * (inside * (eps * s)), load_field(start_ref, row), total)
        mixed = combine(lambda p, q: 0.25 * p - (2.0 / 9.0) * q, second, third)
        store_field(mixed_ref, row, mixed)
        store_field(base_ref, row, combine(lambda p, q: p + q, second, third))
        store_z(rows, links_at(links_ref, row, 0, 2), row, mixed, far_ref, near_ref)
    store_t(rows, links_at(links_ref, rows - 1, 0, 3), mixed_ref, outer_ref, inner_ref)


def last_kernel(rows, coefs_ref, links_ref, *refs):
    arrivals, (base_ref, out_ref) = refs[:5], refs[5:]
    for row in range(rows):
        inside, eps = coefs_ref[row + 1], coefs_ref[rows + 2]
        total = arrived_sum(links_ref, 0, row, rows, arrivals)
        store_field(out_ref, row, combine(lambda p, s: p + inside * (eps * s), load_field(base_ref, row), total))


def call(kernel, name, operands, out_shapes, matvecs, space=pltpu.VMEM, scratch=()):
    vmem = pl.BlockSpec(memory_space=pltpu.VMEM)
    return pl.pallas_call(
        kernel,
        name=name,
        out_shape=out_shapes,
        in_specs=[pl.BlockSpec(memory_space=space)] * len(operands),
        out_specs=jax.tree.map(lambda _: vmem, out_shapes),
        scratch_shapes=scratch,
        cost_estimate=pl.CostEstimate(flops=matvecs * 72 * 1024, bytes_accessed=4096 * 18 * matvecs, transcendentals=0),
        compiler_params=pltpu.CompilerParams(vmem_limit_bytes=16 * 2**20),
    )(*operands)


def body(adjoint, flowed, source_slice, band_width, flow_steps):
    rows = adjoint.shape[0]
    per_plane = BAND // rows
    count = lax.axis_size("gz")
    links = jnp.transpose(flowed, (0, 1, 2, 4, 5, 3, 6)).reshape(-1, flowed.shape[-1])
    whole = jax.ShapeDtypeStruct(adjoint.shape, jnp.float32)
    one_row = jax.ShapeDtypeStruct((1,) + adjoint.shape[1:], jnp.float32)
    coefs_shape = jax.ShapeDtypeStruct((rows + 3,) + adjoint.shape[3:], jnp.float32)

    def in_plane(i, by):
        return i - i % per_plane + (i + by) % per_plane

    def in_line(i, by):
        return (i + by * per_plane) % count

    far_pairs = [(i, in_line(i, 1 if i // per_plane % 2 else -1)) for i in range(count)]
    near_pairs = [(i, in_line(i, -1 if i // per_plane % 2 else 1)) for i in range(count)]
    outer_pairs = [(i, in_plane(i, 1 if i % 2 else -1)) for i in range(count)]
    inner_pairs = [(i, in_plane(i, -1 if i % 2 else 1)) for i in range(count)]

    def sent_on(far, near, outer, inner):
        near = lax.ppermute(near, "gz", near_pairs)
        far = lax.ppermute(far, "gz", far_pairs)
        outer = lax.ppermute(outer, "gz", outer_pairs)
        inner = lax.ppermute(inner, "gz", inner_pairs)
        return near, far, outer, inner

    def local(link_set, field):
        return call(functools.partial(local_kernel, rows, link_set), f"local_{link_set}", (field, links), whole, 22)

    sent = (whole, whole, one_row, one_row)
    copied = SETS * MUS * ENTRIES - (2 * MUS + 2) * ENTRIES // 8 * 8
    sending = call(
        functools.partial(begin_kernel, rows), "begin",
        tuple(pltpu.with_memory_space_constraint(a, pltpu.HBM) for a in (adjoint, links)), sent, 5, pltpu.HBM,
        [
            pltpu.VMEM(adjoint.shape, jnp.float32),
            pltpu.VMEM((rows, copied, flowed.shape[-1]), jnp.float32),
            pltpu.SemaphoreType.DMA((rows + 1,)),
        ],
    )
    arrived = sent_on(*sending)
    coefs = call(
        functools.partial(taper_kernel, rows), "tapers", (source_slice, band_width, flow_steps), coefs_shape, 1,
        pltpu.SMEM,
    )
    total, start = call(
        functools.partial(start_kernel, rows, 2), "start", (coefs, adjoint, links), (whole, whole), 22
    )
    third, *sending = call(
        functools.partial(third_kernel, rows), "third", (coefs, links, total) + arrived, (whole,) + sent, 10
    )
    arrived = sent_on(*sending)
    mixed, *sending, base = call(
        functools.partial(second_kernel, rows), "second", (coefs, links, local(1, third)) + arrived + (start, third),
        (whole,) + sent + (whole,), 10,
    )
    arrived = sent_on(*sending)
    return call(
        functools.partial(last_kernel, rows), "last", (coefs, links, local(0, mixed)) + arrived + (base,), whole, 5
    )


def solution(mesh):
    in_specs = (
        P(("cfg", "gz"), None, None, None, None),
        P(("cfg", "gz"), None, None, None, None, None, None),
        P("cfg"),
        P("cfg"),
        P("cfg"),
    )
    out_specs = P(("cfg", "gz"), None, None, None, None)
    return jax.shard_map(body, mesh=mesh, in_specs=in_specs, out_specs=out_specs, check_vma=False)
```

```python
import functools

import jax
import jax.numpy as jnp
from jax import lax
from jax.experimental import pallas as pl
from jax.experimental.pallas import tpu as pltpu
from jax.sharding import PartitionSpec as P

BAND = 32
LX = 8
SETS = 3
MUS = 4
ENTRIES = 18


def load_field(ref, row):
    return [[ref[row, c, a] for a in range(3)] for c in range(2)]


def store_field(ref, row, field):
    for c in range(2):
        for a in range(3):
            ref[row, c, a] = field[c][a]


def combine(function, *fields):
    return [[function(*(f[c][a] for f in fields)) for a in range(3)] for c in range(2)]


def links_at(links_ref, row, link_set, mu):
    return links_ref, ((row * SETS + link_set) * MUS + mu) * ENTRIES


def entry(matrices, a, b, c, shape):
    ref, base = matrices
    return jnp.broadcast_to(ref[pl.ds(base + (a * 3 + b) * 2 + c, 1), :], shape)


def transport(matrices, ahead, here):
    forward = [[None] * 3, [None] * 3]
    backward = [[None] * 3, [None] * 3]
    shape = (ahead if ahead is not None else here)[0][0].shape

    def add(total, c, a, value):
        total[c][a] = value if total[c][a] is None else total[c][a] + value

    for a in range(3):
        for b in range(3):
            real = entry(matrices, a, b, 0, shape)
            imag = entry(matrices, a, b, 1, shape)
            if ahead is not None:
                add(forward, 0, a, real * ahead[0][b] - imag * ahead[1][b])
                add(forward, 1, a, real * ahead[1][b] + imag * ahead[0][b])
            if here is not None:
                add(backward, 0, b, real * here[0][a] + imag * here[1][a])
                add(backward, 1, b, real * here[1][a] - imag * here[0][a])
    return forward, backward


def roll(plane, by):
    return pltpu.roll(plane, by % plane.shape[-1], plane.ndim - 1)


def place(rows):
    first = lax.axis_index("gz") * rows
    plane, first_pos = first // BAND, lax.rem(first, BAND)
    block = first_pos // rows
    return first_pos, lax.rem(plane + block, 2) == 1, lax.rem(block, 2) == 1


def taper_kernel(rows, source_ref, width_ref, steps_ref, coefs_ref):
    first_pos, _, _ = place(rows)
    ones = jnp.ones((8, 128), jnp.float32)
    per_width = ones * width_ref[0].astype(jnp.float32)
    for i in range(rows + 2):
        distance = ones * (first_pos + i - 1 - source_ref[0]).astype(jnp.float32) / per_width
        coefs_ref[i] = 1.0 / (1.0 + distance * distance)
    coefs_ref[rows + 2] = 0.25 / (ones * steps_ref[0].astype(jnp.float32))


def store_z(rows, matrices, row, field, one_ref, two_ref):
    _, above_first, _ = place(rows)
    _, up = transport(matrices, None, field)
    store_field(one_ref, row, combine(lambda v, h: jnp.where(above_first, h, v), field, up))
    store_field(two_ref, row, combine(lambda v, h: jnp.where(above_first, v, h), field, up))


def store_t(rows, matrices, field_ref, outer_ref, inner_ref):
    _, _, odd_block = place(rows)
    first = load_field(field_ref, 0)
    _, last = transport(matrices, None, load_field(field_ref, rows - 1))
    store_field(outer_ref, 0, combine(lambda p, q: jnp.where(odd_block, q, p), first, last))
    store_field(inner_ref, 0, combine(lambda p, q: jnp.where(odd_block, p, q), first, last))


def begin_kernel(
    rows, adjoint_hbm, links_hbm, one_ref, two_ref, outer_ref, inner_ref, adjoint_ref, links_ref, sems
):
    row_entries = SETS * MUS * ENTRIES
    z_first = (2 * MUS + 2) * ENTRIES
    aligned = z_first // 8 * 8
    copies = [pltpu.make_async_copy(adjoint_hbm, adjoint_ref, sems.at[rows])]
    for row in range(rows):
        part = links_hbm.at[pl.ds(row * row_entries + aligned, row_entries - aligned), :]
        copies.append(pltpu.make_async_copy(part, links_ref.at[row], sems.at[row]))
    for copy in copies:
        copy.start()
    for copy in copies:
        copy.wait()
    for row in range(rows):
        matrices = links_ref.at[row], z_first - aligned
        store_z(rows, matrices, row, load_field(adjoint_ref, row), one_ref, two_ref)
    store_t(rows, (links_ref.at[rows - 1], z_first + ENTRIES - aligned), adjoint_ref, outer_ref, inner_ref)


def start_kernel(rows, link_set, coefs_ref, adjoint_ref, links_ref, sum_ref, start_ref):
    for row in range(rows):
        inside = coefs_ref[row + 1]
        store_field(start_ref, row, combine(lambda v: inside * v, load_field(adjoint_ref, row)))
    local_kernel(rows, link_set, start_ref, links_ref, sum_ref)


def local_kernel(rows, link_set, field_ref, links_ref, sum_ref):
    shape = field_ref.shape[-2:]
    x_pos = lax.broadcasted_iota(jnp.int32, shape, 1) % LX
    at_last = x_pos == LX - 1
    at_first = x_pos == 0

    def one(row, carry):
        here = load_field(field_ref, row)
        ahead = combine(lambda v: jnp.where(at_last, roll(v, LX - 1), roll(v, -1)), here)
        ahead_x, hop = transport(links_at(links_ref, row, link_set, 0), ahead, here)
        total = combine(
            lambda v, f, h: f + jnp.where(at_first, roll(h, 1 - LX), roll(h, 1)) - 8.0 * v, here, ahead_x, hop
        )
        ahead = combine(lambda v: roll(v, -LX), here)
        ahead_y, hop = transport(links_at(links_ref, row, link_set, 1), ahead, here)
        total = combine(lambda s, f, h: s + f + roll(h, LX), total, ahead_y, hop)
        store_field(sum_ref, row, total)
        return carry

    lax.fori_loop(0, rows, one, 0)

    def between(row, carry):
        ahead_t, hop = transport(
            links_at(links_ref, row, link_set, 3), load_field(field_ref, row + 1), load_field(field_ref, row)
        )
        store_field(sum_ref, row, combine(lambda s, f: s + f, load_field(sum_ref, row), ahead_t))
        store_field(sum_ref, row + 1, combine(lambda s, h: s + h, load_field(sum_ref, row + 1), hop))
        return carry

    lax.fori_loop(0, rows - 1, between, 0)


def arrived_sum(links_ref, link_set, row, rows, arrivals, coefs_ref=None):
    sum_ref, one_ref, two_ref, outer_ref, inner_ref = arrivals
    first_pos, above_first, odd_block = place(rows)
    one, two = load_field(one_ref, row), load_field(two_ref, row)
    if coefs_ref is not None:
        one, two = (combine(lambda v: coefs_ref[row + 1] * v, f) for f in (one, two))
    above = combine(lambda p, q: jnp.where(above_first, p, q), one, two)
    ahead_z, _ = transport(links_at(links_ref, row, link_set, 2), above, None)
    total = combine(
        lambda s, f, p, q: s + f + jnp.where(above_first, q, p), load_field(sum_ref, row), ahead_z, one, two
    )
    outer, inner = load_field(outer_ref, 0), load_field(inner_ref, 0)
    if row == 0:
        exists = jnp.where(first_pos != 0, 1.0, 0.0)
        if coefs_ref is not None:
            exists = exists * coefs_ref[0]
        total = combine(lambda s, p, q: s + exists * jnp.where(odd_block, q, p), total, outer, inner)
    if row == rows - 1:
        exists = jnp.where(first_pos != BAND - rows, 1.0, 0.0)
        if coefs_ref is not None:
            exists = exists * coefs_ref[rows + 1]
        later = combine(lambda p, q: exists * jnp.where(odd_block, p, q), outer, inner)
        ahead_t, _ = transport(links_at(links_ref, row, link_set, 3), later, None)
        total = combine(lambda s, f: s + f, total, ahead_t)
    return total


def third_kernel(rows, coefs_ref, links_ref, *refs):
    arrivals, (third_ref, one_ref, two_ref, outer_ref, inner_ref) = refs[:5], refs[5:]
    for row in range(rows):
        inside, eps = coefs_ref[row + 1], coefs_ref[rows + 2]
        total = arrived_sum(links_ref, 2, row, rows, arrivals, coefs_ref)
        third = combine(lambda s: 0.75 * (inside * (eps * s)), total)
        store_field(third_ref, row, third)
        store_z(rows, links_at(links_ref, row, 1, 2), row, third, one_ref, two_ref)
    store_t(rows, links_at(links_ref, rows - 1, 1, 3), third_ref, outer_ref, inner_ref)


def second_kernel(rows, coefs_ref, links_ref, *refs):
    arrivals, (start_ref, third_ref, mixed_ref, one_ref, two_ref, outer_ref, inner_ref, base_ref) = refs[:5], refs[5:]
    for row in range(rows):
        inside, eps = coefs_ref[row + 1], coefs_ref[rows + 2]
        total = arrived_sum(links_ref, 1, row, rows, arrivals)
        third = load_field(third_ref, row)
        second = combine(lambda v, s: v + (8.0 / 9.0) * (inside * (eps * s)), load_field(start_ref, row), total)
        mixed = combine(lambda p, q: 0.25 * p - (2.0 / 9.0) * q, second, third)
        store_field(mixed_ref, row, mixed)
        store_field(base_ref, row, combine(lambda p, q: p + q, second, third))
        store_z(rows, links_at(links_ref, row, 0, 2), row, mixed, one_ref, two_ref)
    store_t(rows, links_at(links_ref, rows - 1, 0, 3), mixed_ref, outer_ref, inner_ref)


def last_kernel(rows, coefs_ref, links_ref, *refs):
    arrivals, (base_ref, out_ref) = refs[:5], refs[5:]
    for row in range(rows):
        inside, eps = coefs_ref[row + 1], coefs_ref[rows + 2]
        total = arrived_sum(links_ref, 0, row, rows, arrivals)
        store_field(out_ref, row, combine(lambda p, s: p + inside * (eps * s), load_field(base_ref, row), total))


def call(kernel, name, operands, out_shapes, matvecs, space=pltpu.VMEM, scratch=()):
    vmem = pl.BlockSpec(memory_space=pltpu.VMEM)
    return pl.pallas_call(
        kernel,
        name=name,
        out_shape=out_shapes,
        in_specs=[pl.BlockSpec(memory_space=space)] * len(operands),
        out_specs=jax.tree.map(lambda _: vmem, out_shapes),
        scratch_shapes=scratch,
        cost_estimate=pl.CostEstimate(flops=matvecs * 72 * 1024, bytes_accessed=4096 * 18 * matvecs, transcendentals=0),
        compiler_params=pltpu.CompilerParams(vmem_limit_bytes=16 * 2**20),
    )(*operands)


def body(adjoint, flowed, source_slice, band_width, flow_steps):
    rows = adjoint.shape[0]
    per_plane = BAND // rows
    count = lax.axis_size("gz")
    links = jnp.transpose(flowed, (0, 1, 2, 4, 5, 3, 6)).reshape(-1, flowed.shape[-1])
    whole = jax.ShapeDtypeStruct(adjoint.shape, jnp.float32)
    one_row = jax.ShapeDtypeStruct((1,) + adjoint.shape[1:], jnp.float32)
    coefs_shape = jax.ShapeDtypeStruct((rows + 3,) + adjoint.shape[3:], jnp.float32)

    def in_plane(i, by):
        return i - i % per_plane + (i + by) % per_plane

    def in_line(i, by):
        return (i + by * per_plane) % count

    one_pairs = [(i, in_line(i, 1 if (i // per_plane + i) % 2 else -1)) for i in range(count)]
    two_pairs = [(i, in_line(i, -1 if (i // per_plane + i) % 2 else 1)) for i in range(count)]
    outer_pairs = [(i, in_plane(i, 1 if i % 2 else -1)) for i in range(count)]
    inner_pairs = [(i, in_plane(i, -1 if i % 2 else 1)) for i in range(count)]

    def sent_on(one, two, outer, inner):
        one = lax.ppermute(one, "gz", one_pairs)
        two = lax.ppermute(two, "gz", two_pairs)
        outer = lax.ppermute(outer, "gz", outer_pairs)
        inner = lax.ppermute(inner, "gz", inner_pairs)
        return one, two, outer, inner

    def local(link_set, field):
        return call(functools.partial(local_kernel, rows, link_set), f"local_{link_set}", (field, links), whole, 22)

    sent = (whole, whole, one_row, one_row)
    copied = SETS * MUS * ENTRIES - (2 * MUS + 2) * ENTRIES // 8 * 8
    sending = call(
        functools.partial(begin_kernel, rows), "begin",
        tuple(pltpu.with_memory_space_constraint(a, pltpu.HBM) for a in (adjoint, links)), sent, 5, pltpu.HBM,
        [
            pltpu.VMEM(adjoint.shape, jnp.float32),
            pltpu.VMEM((rows, copied, flowed.shape[-1]), jnp.float32),
            pltpu.SemaphoreType.DMA((rows + 1,)),
        ],
    )
    arrived = sent_on(*sending)
    coefs = call(
        functools.partial(taper_kernel, rows), "tapers", (source_slice, band_width, flow_steps), coefs_shape, 1,
        pltpu.SMEM,
    )
    total, start = call(
        functools.partial(start_kernel, rows, 2), "start", (coefs, adjoint, links), (whole, whole), 22
    )
    third, *sending = call(
        functools.partial(third_kernel, rows), "third", (coefs, links, total) + arrived, (whole,) + sent, 10
    )
    arrived = sent_on(*sending)
    mixed, *sending, base = call(
        functools.partial(second_kernel, rows), "second", (coefs, links, local(1, third)) + arrived + (start, third),
        (whole,) + sent + (whole,), 10,
    )
    arrived = sent_on(*sending)
    return call(
        functools.partial(last_kernel, rows), "last", (coefs, links, local(0, mixed)) + arrived + (base,), whole, 5
    )


def solution(mesh):
    in_specs = (
        P(("cfg", "gz"), None, None, None, None),
        P(("cfg", "gz"), None, None, None, None, None, None),
        P("cfg"),
        P("cfg"),
        P("cfg"),
    )
    out_specs = P(("cfg", "gz"), None, None, None, None)
    return jax.shard_map(body, mesh=mesh, in_specs=in_specs, out_specs=out_specs, check_vma=False)
```

```python
import functools

import jax
import jax.numpy as jnp
from jax import lax
from jax.experimental import pallas as pl
from jax.experimental.pallas import tpu as pltpu
from jax.sharding import PartitionSpec as P

BAND = 32
LX = 8
SETS = 3
MUS = 4
ENTRIES = 18


def load_field(ref, row):
    return [[ref[row, c, a] for a in range(3)] for c in range(2)]


def store_field(ref, row, field):
    for c in range(2):
        for a in range(3):
            ref[row, c, a] = field[c][a]


def combine(function, *fields):
    return [[function(*(f[c][a] for f in fields)) for a in range(3)] for c in range(2)]


def links_at(links_ref, row, link_set, mu):
    return links_ref, ((row * SETS + link_set) * MUS + mu) * ENTRIES


def entry(matrices, a, b, c, shape):
    ref, base = matrices
    return jnp.broadcast_to(ref[pl.ds(base + (a * 3 + b) * 2 + c, 1), :], shape)


def transport(matrices, ahead, here):
    forward = [[None] * 3, [None] * 3]
    backward = [[None] * 3, [None] * 3]
    shape = (ahead if ahead is not None else here)[0][0].shape

    def add(total, c, a, value):
        total[c][a] = value if total[c][a] is None else total[c][a] + value

    for a in range(3):
        for b in range(3):
            real = entry(matrices, a, b, 0, shape)
            imag = entry(matrices, a, b, 1, shape)
            if ahead is not None:
                add(forward, 0, a, real * ahead[0][b] - imag * ahead[1][b])
                add(forward, 1, a, real * ahead[1][b] + imag * ahead[0][b])
            if here is not None:
                add(backward, 0, b, real * here[0][a] + imag * here[1][a])
                add(backward, 1, b, real * here[1][a] - imag * here[0][a])
    return forward, backward


def roll(plane, by):
    return pltpu.roll(plane, by % plane.shape[-1], plane.ndim - 1)


def place(rows):
    first = lax.axis_index("gz") * rows
    plane, first_pos = first // BAND, lax.rem(first, BAND)
    block = first_pos // rows
    return first_pos, lax.rem(plane + block, 2) == 0, lax.rem(block, 2) == 1


def taper_kernel(rows, source_ref, width_ref, steps_ref, coefs_ref):
    first_pos, _, _ = place(rows)
    ones = jnp.ones((8, 128), jnp.float32)
    per_width = ones * width_ref[0].astype(jnp.float32)
    for i in range(rows + 2):
        distance = ones * (first_pos + i - 1 - source_ref[0]).astype(jnp.float32) / per_width
        coefs_ref[i] = 1.0 / (1.0 + distance * distance)
    coefs_ref[rows + 2] = 0.25 / (ones * steps_ref[0].astype(jnp.float32))


def store_z(rows, matrices, row, field, one_ref, two_ref):
    _, above_first, _ = place(rows)
    _, up = transport(matrices, None, field)
    store_field(one_ref, row, combine(lambda v, h: jnp.where(above_first, h, v), field, up))
    store_field(two_ref, row, combine(lambda v, h: jnp.where(above_first, v, h), field, up))


def store_t(rows, matrices, field_ref, outer_ref, inner_ref):
    _, _, odd_block = place(rows)
    first = load_field(field_ref, 0)
    _, last = transport(matrices, None, load_field(field_ref, rows - 1))
    store_field(outer_ref, 0, combine(lambda p, q: jnp.where(odd_block, q, p), first, last))
    store_field(inner_ref, 0, combine(lambda p, q: jnp.where(odd_block, p, q), first, last))


def begin_kernel(
    rows, adjoint_hbm, links_hbm, one_ref, two_ref, outer_ref, inner_ref, adjoint_ref, links_ref, sems
):
    row_entries = SETS * MUS * ENTRIES
    z_first = (2 * MUS + 2) * ENTRIES
    aligned = z_first // 8 * 8
    copies = [pltpu.make_async_copy(adjoint_hbm, adjoint_ref, sems.at[rows])]
    for row in range(rows):
        part = links_hbm.at[pl.ds(row * row_entries + aligned, row_entries - aligned), :]
        copies.append(pltpu.make_async_copy(part, links_ref.at[row], sems.at[row]))
    for copy in copies:
        copy.start()
    for copy in copies:
        copy.wait()
    for row in range(rows):
        matrices = links_ref.at[row], z_first - aligned
        store_z(rows, matrices, row, load_field(adjoint_ref, row), one_ref, two_ref)
    store_t(rows, (links_ref.at[rows - 1], z_first + ENTRIES - aligned), adjoint_ref, outer_ref, inner_ref)


def start_kernel(rows, link_set, coefs_ref, adjoint_ref, links_ref, sum_ref, start_ref):
    for row in range(rows):
        inside = coefs_ref[row + 1]
        store_field(start_ref, row, combine(lambda v: inside * v, load_field(adjoint_ref, row)))
    local_kernel(rows, link_set, start_ref, links_ref, sum_ref)


def local_kernel(rows, link_set, field_ref, links_ref, sum_ref):
    shape = field_ref.shape[-2:]
    x_pos = lax.broadcasted_iota(jnp.int32, shape, 1) % LX
    at_last = x_pos == LX - 1
    at_first = x_pos == 0

    def one(row, carry):
        here = load_field(field_ref, row)
        ahead = combine(lambda v: jnp.where(at_last, roll(v, LX - 1), roll(v, -1)), here)
        ahead_x, hop = transport(links_at(links_ref, row, link_set, 0), ahead, here)
        total = combine(
            lambda v, f, h: f + jnp.where(at_first, roll(h, 1 - LX), roll(h, 1)) - 8.0 * v, here, ahead_x, hop
        )
        ahead = combine(lambda v: roll(v, -LX), here)
        ahead_y, hop = transport(links_at(links_ref, row, link_set, 1), ahead, here)
        total = combine(lambda s, f, h: s + f + roll(h, LX), total, ahead_y, hop)
        store_field(sum_ref, row, total)
        return carry

    lax.fori_loop(0, rows, one, 0)

    def between(row, carry):
        ahead_t, hop = transport(
            links_at(links_ref, row, link_set, 3), load_field(field_ref, row + 1), load_field(field_ref, row)
        )
        store_field(sum_ref, row, combine(lambda s, f: s + f, load_field(sum_ref, row), ahead_t))
        store_field(sum_ref, row + 1, combine(lambda s, h: s + h, load_field(sum_ref, row + 1), hop))
        return carry

    lax.fori_loop(0, rows - 1, between, 0)


def arrived_sum(links_ref, link_set, row, rows, arrivals, coefs_ref=None):
    sum_ref, one_ref, two_ref, outer_ref, inner_ref = arrivals
    first_pos, above_first, odd_block = place(rows)
    one, two = load_field(one_ref, row), load_field(two_ref, row)
    if coefs_ref is not None:
        one, two = (combine(lambda v: coefs_ref[row + 1] * v, f) for f in (one, two))
    above = combine(lambda p, q: jnp.where(above_first, p, q), one, two)
    ahead_z, _ = transport(links_at(links_ref, row, link_set, 2), above, None)
    total = combine(
        lambda s, f, p, q: s + f + jnp.where(above_first, q, p), load_field(sum_ref, row), ahead_z, one, two
    )
    outer, inner = load_field(outer_ref, 0), load_field(inner_ref, 0)
    if row == 0:
        exists = jnp.where(first_pos != 0, 1.0, 0.0)
        if coefs_ref is not None:
            exists = exists * coefs_ref[0]
        total = combine(lambda s, p, q: s + exists * jnp.where(odd_block, q, p), total, outer, inner)
    if row == rows - 1:
        exists = jnp.where(first_pos != BAND - rows, 1.0, 0.0)
        if coefs_ref is not None:
            exists = exists * coefs_ref[rows + 1]
        later = combine(lambda p, q: exists * jnp.where(odd_block, p, q), outer, inner)
        ahead_t, _ = transport(links_at(links_ref, row, link_set, 3), later, None)
        total = combine(lambda s, f: s + f, total, ahead_t)
    return total


def third_kernel(rows, coefs_ref, links_ref, *refs):
    arrivals, (third_ref, one_ref, two_ref, outer_ref, inner_ref) = refs[:5], refs[5:]
    for row in range(rows):
        inside, eps = coefs_ref[row + 1], coefs_ref[rows + 2]
        total = arrived_sum(links_ref, 2, row, rows, arrivals, coefs_ref)
        third = combine(lambda s: 0.75 * (inside * (eps * s)), total)
        store_field(third_ref, row, third)
        store_z(rows, links_at(links_ref, row, 1, 2), row, third, one_ref, two_ref)
    store_t(rows, links_at(links_ref, rows - 1, 1, 3), third_ref, outer_ref, inner_ref)


def second_kernel(rows, coefs_ref, links_ref, *refs):
    arrivals, (start_ref, third_ref, mixed_ref, one_ref, two_ref, outer_ref, inner_ref, base_ref) = refs[:5], refs[5:]
    for row in range(rows):
        inside, eps = coefs_ref[row + 1], coefs_ref[rows + 2]
        total = arrived_sum(links_ref, 1, row, rows, arrivals)
        third = load_field(third_ref, row)
        second = combine(lambda v, s: v + (8.0 / 9.0) * (inside * (eps * s)), load_field(start_ref, row), total)
        mixed = combine(lambda p, q: 0.25 * p - (2.0 / 9.0) * q, second, third)
        store_field(mixed_ref, row, mixed)
        store_field(base_ref, row, combine(lambda p, q: p + q, second, third))
        store_z(rows, links_at(links_ref, row, 0, 2), row, mixed, one_ref, two_ref)
    store_t(rows, links_at(links_ref, rows - 1, 0, 3), mixed_ref, outer_ref, inner_ref)


def last_kernel(rows, coefs_ref, links_ref, *refs):
    arrivals, (base_ref, out_ref) = refs[:5], refs[5:]
    for row in range(rows):
        inside, eps = coefs_ref[row + 1], coefs_ref[rows + 2]
        total = arrived_sum(links_ref, 0, row, rows, arrivals)
        store_field(out_ref, row, combine(lambda p, s: p + inside * (eps * s), load_field(base_ref, row), total))


def call(kernel, name, operands, out_shapes, matvecs, space=pltpu.VMEM, scratch=()):
    vmem = pl.BlockSpec(memory_space=pltpu.VMEM)
    return pl.pallas_call(
        kernel,
        name=name,
        out_shape=out_shapes,
        in_specs=[pl.BlockSpec(memory_space=space)] * len(operands),
        out_specs=jax.tree.map(lambda _: vmem, out_shapes),
        scratch_shapes=scratch,
        cost_estimate=pl.CostEstimate(flops=matvecs * 72 * 1024, bytes_accessed=4096 * 18 * matvecs, transcendentals=0),
        compiler_params=pltpu.CompilerParams(vmem_limit_bytes=16 * 2**20),
    )(*operands)


def body(adjoint, flowed, source_slice, band_width, flow_steps):
    rows = adjoint.shape[0]
    per_plane = BAND // rows
    count = lax.axis_size("gz")
    links = jnp.transpose(flowed, (0, 1, 2, 4, 5, 3, 6)).reshape(-1, flowed.shape[-1])
    whole = jax.ShapeDtypeStruct(adjoint.shape, jnp.float32)
    one_row = jax.ShapeDtypeStruct((1,) + adjoint.shape[1:], jnp.float32)
    coefs_shape = jax.ShapeDtypeStruct((rows + 3,) + adjoint.shape[3:], jnp.float32)

    def in_plane(i, by):
        return i - i % per_plane + (i + by) % per_plane

    def in_line(i, by):
        return (i + by * per_plane) % count

    one_pairs = [(i, in_line(i, -1 if (i // per_plane + i) % 2 else 1)) for i in range(count)]
    two_pairs = [(i, in_line(i, 1 if (i // per_plane + i) % 2 else -1)) for i in range(count)]
    outer_pairs = [(i, in_plane(i, 1 if i % 2 else -1)) for i in range(count)]
    inner_pairs = [(i, in_plane(i, -1 if i % 2 else 1)) for i in range(count)]

    def sent_on(one, two, outer, inner):
        one = lax.ppermute(one, "gz", one_pairs)
        two = lax.ppermute(two, "gz", two_pairs)
        outer = lax.ppermute(outer, "gz", outer_pairs)
        inner = lax.ppermute(inner, "gz", inner_pairs)
        return one, two, outer, inner

    def local(link_set, field):
        return call(functools.partial(local_kernel, rows, link_set), f"local_{link_set}", (field, links), whole, 22)

    sent = (whole, whole, one_row, one_row)
    copied = SETS * MUS * ENTRIES - (2 * MUS + 2) * ENTRIES // 8 * 8
    sending = call(
        functools.partial(begin_kernel, rows), "begin",
        tuple(pltpu.with_memory_space_constraint(a, pltpu.HBM) for a in (adjoint, links)), sent, 5, pltpu.HBM,
        [
            pltpu.VMEM(adjoint.shape, jnp.float32),
            pltpu.VMEM((rows, copied, flowed.shape[-1]), jnp.float32),
            pltpu.SemaphoreType.DMA((rows + 1,)),
        ],
    )
    arrived = sent_on(*sending)
    coefs = call(
        functools.partial(taper_kernel, rows), "tapers", (source_slice, band_width, flow_steps), coefs_shape, 1,
        pltpu.SMEM,
    )
    total, start = call(
        functools.partial(start_kernel, rows, 2), "start", (coefs, adjoint, links), (whole, whole), 22
    )
    third, *sending = call(
        functools.partial(third_kernel, rows), "third", (coefs, links, total) + arrived, (whole,) + sent, 10
    )
    arrived = sent_on(*sending)
    mixed, *sending, base = call(
        functools.partial(second_kernel, rows), "second", (coefs, links, local(1, third)) + arrived + (start, third),
        (whole,) + sent + (whole,), 10,
    )
    arrived = sent_on(*sending)
    return call(
        functools.partial(last_kernel, rows), "last", (coefs, links, local(0, mixed)) + arrived + (base,), whole, 5
    )


def solution(mesh):
    in_specs = (
        P(("cfg", "gz"), None, None, None, None),
        P(("cfg", "gz"), None, None, None, None, None, None),
        P("cfg"),
        P("cfg"),
        P("cfg"),
    )
    out_specs = P(("cfg", "gz"), None, None, None, None)
    return jax.shard_map(body, mesh=mesh, in_specs=in_specs, out_specs=out_specs, check_vma=False)
```

```python
import functools

import jax
import jax.numpy as jnp
from jax import lax
from jax.experimental import pallas as pl
from jax.experimental.pallas import tpu as pltpu
from jax.sharding import PartitionSpec as P

BAND = 32
LX = 8
SETS = 3
MUS = 4
ENTRIES = 18


def load_field(ref, row):
    return [[ref[row, c, a] for a in range(3)] for c in range(2)]


def store_field(ref, row, field):
    for c in range(2):
        for a in range(3):
            ref[row, c, a] = field[c][a]


def combine(function, *fields):
    return [[function(*(f[c][a] for f in fields)) for a in range(3)] for c in range(2)]


def links_at(links_ref, row, link_set, mu):
    return links_ref, ((row * SETS + link_set) * MUS + mu) * ENTRIES


def entry(matrices, a, b, c, shape):
    ref, base = matrices
    return jnp.broadcast_to(ref[pl.ds(base + (a * 3 + b) * 2 + c, 1), :], shape)


def transport(matrices, ahead, here):
    forward = [[None] * 3, [None] * 3]
    backward = [[None] * 3, [None] * 3]
    shape = (ahead if ahead is not None else here)[0][0].shape

    def add(total, c, a, value):
        total[c][a] = value if total[c][a] is None else total[c][a] + value

    for a in range(3):
        for b in range(3):
            real = entry(matrices, a, b, 0, shape)
            imag = entry(matrices, a, b, 1, shape)
            if ahead is not None:
                add(forward, 0, a, real * ahead[0][b] - imag * ahead[1][b])
                add(forward, 1, a, real * ahead[1][b] + imag * ahead[0][b])
            if here is not None:
                add(backward, 0, b, real * here[0][a] + imag * here[1][a])
                add(backward, 1, b, real * here[1][a] - imag * here[0][a])
    return forward, backward


def roll(plane, by):
    return pltpu.roll(plane, by % plane.shape[-1], plane.ndim - 1)


def place(rows):
    first = lax.axis_index("gz") * rows
    plane, first_pos = first // BAND, lax.rem(first, BAND)
    return plane, first_pos, lax.rem(plane, 2) == 1, lax.rem(first_pos // rows, 2) == 1


def taper_kernel(rows, source_ref, width_ref, steps_ref, coefs_ref):
    _, first_pos, _, _ = place(rows)
    ones = jnp.ones((8, 128), jnp.float32)
    per_width = ones * width_ref[0].astype(jnp.float32)
    for i in range(rows + 2):
        distance = ones * (first_pos + i - 1 - source_ref[0]).astype(jnp.float32) / per_width
        coefs_ref[i] = 1.0 / (1.0 + distance * distance)
    coefs_ref[rows + 2] = 0.25 / (ones * steps_ref[0].astype(jnp.float32))


def store_z(rows, matrices, row, field, middle_ref, near_ref, wrap_ref):
    _, _, odd_plane, _ = place(rows)
    _, up = transport(matrices, None, field)
    far = combine(lambda v, h: jnp.where(odd_plane, h, v), field, up)
    store_field(middle_ref, row, far)
    store_field(wrap_ref, row, far)
    store_field(near_ref, row, combine(lambda v, h: jnp.where(odd_plane, v, h), field, up))


def store_t(rows, matrices, field_ref, outer_ref, inner_ref):
    _, _, _, odd_block = place(rows)
    first = load_field(field_ref, 0)
    _, last = transport(matrices, None, load_field(field_ref, rows - 1))
    store_field(outer_ref, 0, combine(lambda p, q: jnp.where(odd_block, q, p), first, last))
    store_field(inner_ref, 0, combine(lambda p, q: jnp.where(odd_block, p, q), first, last))


def begin_kernel(
    rows, adjoint_hbm, links_hbm, middle_ref, near_ref, wrap_ref, outer_ref, inner_ref, adjoint_ref, links_ref, sems
):
    row_entries = SETS * MUS * ENTRIES
    z_first = (2 * MUS + 2) * ENTRIES
    aligned = z_first // 8 * 8
    copies = [pltpu.make_async_copy(adjoint_hbm, adjoint_ref, sems.at[rows])]
    for row in range(rows):
        part = links_hbm.at[pl.ds(row * row_entries + aligned, row_entries - aligned), :]
        copies.append(pltpu.make_async_copy(part, links_ref.at[row], sems.at[row]))
    for copy in copies:
        copy.start()
    for copy in copies:
        copy.wait()
    for row in range(rows):
        matrices = links_ref.at[row], z_first - aligned
        store_z(rows, matrices, row, load_field(adjoint_ref, row), middle_ref, near_ref, wrap_ref)
    store_t(rows, (links_ref.at[rows - 1], z_first + ENTRIES - aligned), adjoint_ref, outer_ref, inner_ref)


def start_kernel(rows, link_set, coefs_ref, adjoint_ref, links_ref, sum_ref, start_ref):
    for row in range(rows):
        inside = coefs_ref[row + 1]
        store_field(start_ref, row, combine(lambda v: inside * v, load_field(adjoint_ref, row)))
    local_kernel(rows, link_set, start_ref, links_ref, sum_ref)


def local_kernel(rows, link_set, field_ref, links_ref, sum_ref):
    shape = field_ref.shape[-2:]
    x_pos = lax.broadcasted_iota(jnp.int32, shape, 1) % LX
    at_last = x_pos == LX - 1
    at_first = x_pos == 0

    def one(row, carry):
        here = load_field(field_ref, row)
        ahead = combine(lambda v: jnp.where(at_last, roll(v, LX - 1), roll(v, -1)), here)
        ahead_x, hop = transport(links_at(links_ref, row, link_set, 0), ahead, here)
        total = combine(
            lambda v, f, h: f + jnp.where(at_first, roll(h, 1 - LX), roll(h, 1)) - 8.0 * v, here, ahead_x, hop
        )
        ahead = combine(lambda v: roll(v, -LX), here)
        ahead_y, hop = transport(links_at(links_ref, row, link_set, 1), ahead, here)
        total = combine(lambda s, f, h: s + f + roll(h, LX), total, ahead_y, hop)
        store_field(sum_ref, row, total)
        return carry

    lax.fori_loop(0, rows, one, 0)

    def between(row, carry):
        ahead_t, hop = transport(
            links_at(links_ref, row, link_set, 3), load_field(field_ref, row + 1), load_field(field_ref, row)
        )
        store_field(sum_ref, row, combine(lambda s, f: s + f, load_field(sum_ref, row), ahead_t))
        store_field(sum_ref, row + 1, combine(lambda s, h: s + h, load_field(sum_ref, row + 1), hop))
        return carry

    lax.fori_loop(0, rows - 1, between, 0)


def arrived_sum(links_ref, link_set, row, rows, arrivals, coefs_ref=None):
    sum_ref, middle_ref, near_ref, wrap_ref, outer_ref, inner_ref = arrivals
    plane, first_pos, odd_plane, odd_block = place(rows)
    at_wrap = (plane == 0) | (plane == lax.axis_size("gz") * rows // BAND - 1)
    near = load_field(near_ref, row)
    far = combine(lambda p, q: jnp.where(at_wrap, q, p), load_field(middle_ref, row), load_field(wrap_ref, row))
    if coefs_ref is not None:
        far, near = (combine(lambda v: coefs_ref[row + 1] * v, f) for f in (far, near))
    above = combine(lambda p, q: jnp.where(odd_plane, p, q), far, near)
    ahead_z, _ = transport(links_at(links_ref, row, link_set, 2), above, None)
    total = combine(
        lambda s, f, p, q: s + f + jnp.where(odd_plane, q, p), load_field(sum_ref, row), ahead_z, far, near
    )
    outer, inner = load_field(outer_ref, 0), load_field(inner_ref, 0)
    if row == 0:
        exists = jnp.where(first_pos != 0, 1.0, 0.0)
        if coefs_ref is not None:
            exists = exists * coefs_ref[0]
        total = combine(lambda s, p, q: s + exists * jnp.where(odd_block, q, p), total, outer, inner)
    if row == rows - 1:
        exists = jnp.where(first_pos != BAND - rows, 1.0, 0.0)
        if coefs_ref is not None:
            exists = exists * coefs_ref[rows + 1]
        later = combine(lambda p, q: exists * jnp.where(odd_block, p, q), outer, inner)
        ahead_t, _ = transport(links_at(links_ref, row, link_set, 3), later, None)
        total = combine(lambda s, f: s + f, total, ahead_t)
    return total


def third_kernel(rows, coefs_ref, links_ref, *refs):
    arrivals, (third_ref, middle_ref, near_ref, wrap_ref, outer_ref, inner_ref) = refs[:6], refs[6:]
    for row in range(rows):
        inside, eps = coefs_ref[row + 1], coefs_ref[rows + 2]
        total = arrived_sum(links_ref, 2, row, rows, arrivals, coefs_ref)
        third = combine(lambda s: 0.75 * (inside * (eps * s)), total)
        store_field(third_ref, row, third)
        store_z(rows, links_at(links_ref, row, 1, 2), row, third, middle_ref, near_ref, wrap_ref)
    store_t(rows, links_at(links_ref, rows - 1, 1, 3), third_ref, outer_ref, inner_ref)


def second_kernel(rows, coefs_ref, links_ref, *refs):
    arrivals, (start_ref, third_ref, mixed_ref, *sent, base_ref) = refs[:6], refs[6:]
    middle_ref, near_ref, wrap_ref, outer_ref, inner_ref = sent
    for row in range(rows):
        inside, eps = coefs_ref[row + 1], coefs_ref[rows + 2]
        total = arrived_sum(links_ref, 1, row, rows, arrivals)
        third = load_field(third_ref, row)
        second = combine(lambda v, s: v + (8.0 / 9.0) * (inside * (eps * s)), load_field(start_ref, row), total)
        mixed = combine(lambda p, q: 0.25 * p - (2.0 / 9.0) * q, second, third)
        store_field(mixed_ref, row, mixed)
        store_field(base_ref, row, combine(lambda p, q: p + q, second, third))
        store_z(rows, links_at(links_ref, row, 0, 2), row, mixed, middle_ref, near_ref, wrap_ref)
    store_t(rows, links_at(links_ref, rows - 1, 0, 3), mixed_ref, outer_ref, inner_ref)


def last_kernel(rows, coefs_ref, links_ref, *refs):
    arrivals, (base_ref, out_ref) = refs[:6], refs[6:]
    for row in range(rows):
        inside, eps = coefs_ref[row + 1], coefs_ref[rows + 2]
        total = arrived_sum(links_ref, 0, row, rows, arrivals)
        store_field(out_ref, row, combine(lambda p, s: p + inside * (eps * s), load_field(base_ref, row), total))


def call(kernel, name, operands, out_shapes, matvecs, space=pltpu.VMEM, scratch=()):
    vmem = pl.BlockSpec(memory_space=pltpu.VMEM)
    return pl.pallas_call(
        kernel,
        name=name,
        out_shape=out_shapes,
        in_specs=[pl.BlockSpec(memory_space=space)] * len(operands),
        out_specs=jax.tree.map(lambda _: vmem, out_shapes),
        scratch_shapes=scratch,
        cost_estimate=pl.CostEstimate(flops=matvecs * 72 * 1024, bytes_accessed=4096 * 18 * matvecs, transcendentals=0),
        compiler_params=pltpu.CompilerParams(vmem_limit_bytes=16 * 2**20),
    )(*operands)


def body(adjoint, flowed, source_slice, band_width, flow_steps):
    rows = adjoint.shape[0]
    per_plane = BAND // rows
    count = lax.axis_size("gz")
    links = jnp.transpose(flowed, (0, 1, 2, 4, 5, 3, 6)).reshape(-1, flowed.shape[-1])
    whole = jax.ShapeDtypeStruct(adjoint.shape, jnp.float32)
    one_row = jax.ShapeDtypeStruct((1,) + adjoint.shape[1:], jnp.float32)
    coefs_shape = jax.ShapeDtypeStruct((rows + 3,) + adjoint.shape[3:], jnp.float32)

    def in_plane(i, by):
        return i - i % per_plane + (i + by) % per_plane

    def in_line(i, by):
        return (i + by * per_plane) % count

    planes = count // per_plane

    def far_partner(i, over_wrap):
        plane = i // per_plane
        if (plane in (0, planes - 1)) != over_wrap:
            return i
        return in_line(i, 1 if plane % 2 else -1)

    middle_pairs = [(i, far_partner(i, False)) for i in range(count)]
    wrap_pairs = [(i, far_partner(i, True)) for i in range(count)]
    near_pairs = [(i, in_line(i, -1 if i // per_plane % 2 else 1)) for i in range(count)]
    outer_pairs = [(i, in_plane(i, 1 if i % 2 else -1)) for i in range(count)]
    inner_pairs = [(i, in_plane(i, -1 if i % 2 else 1)) for i in range(count)]

    def sent_on(middle, near, wrap, outer, inner):
        middle = lax.ppermute(middle, "gz", middle_pairs)
        near = lax.ppermute(near, "gz", near_pairs)
        wrap = lax.ppermute(wrap, "gz", wrap_pairs)
        outer = lax.ppermute(outer, "gz", outer_pairs)
        inner = lax.ppermute(inner, "gz", inner_pairs)
        return middle, near, wrap, outer, inner

    def local(link_set, field):
        return call(functools.partial(local_kernel, rows, link_set), f"local_{link_set}", (field, links), whole, 22)

    sent = (whole, whole, whole, one_row, one_row)
    copied = SETS * MUS * ENTRIES - (2 * MUS + 2) * ENTRIES // 8 * 8
    sending = call(
        functools.partial(begin_kernel, rows), "begin",
        tuple(pltpu.with_memory_space_constraint(a, pltpu.HBM) for a in (adjoint, links)), sent, 5, pltpu.HBM,
        [
            pltpu.VMEM(adjoint.shape, jnp.float32),
            pltpu.VMEM((rows, copied, flowed.shape[-1]), jnp.float32),
            pltpu.SemaphoreType.DMA((rows + 1,)),
        ],
    )
    arrived = sent_on(*sending)
    coefs = call(
        functools.partial(taper_kernel, rows), "tapers", (source_slice, band_width, flow_steps), coefs_shape, 1,
        pltpu.SMEM,
    )
    total, start = call(
        functools.partial(start_kernel, rows, 2), "start", (coefs, adjoint, links), (whole, whole), 22
    )
    third, *sending = call(
        functools.partial(third_kernel, rows), "third", (coefs, links, total) + arrived, (whole,) + sent, 10
    )
    arrived = sent_on(*sending)
    mixed, *sending, base = call(
        functools.partial(second_kernel, rows), "second", (coefs, links, local(1, third)) + arrived + (start, third),
        (whole,) + sent + (whole,), 10,
    )
    arrived = sent_on(*sending)
    return call(
        functools.partial(last_kernel, rows), "last", (coefs, links, local(0, mixed)) + arrived + (base,), whole, 5
    )


def solution(mesh):
    in_specs = (
        P(("cfg", "gz"), None, None, None, None),
        P(("cfg", "gz"), None, None, None, None, None, None),
        P("cfg"),
        P("cfg"),
        P("cfg"),
    )
    out_specs = P(("cfg", "gz"), None, None, None, None)
    return jax.shard_map(body, mesh=mesh, in_specs=in_specs, out_specs=out_specs, check_vma=False)
```

```python
import functools

import jax
import jax.numpy as jnp
from jax import lax
from jax.experimental import pallas as pl
from jax.experimental.pallas import tpu as pltpu
from jax.sharding import PartitionSpec as P

BAND = 32
LX = 8
SETS = 3
MUS = 4
ENTRIES = 18


def load_field(ref, row):
    return [[ref[row, c, a] for a in range(3)] for c in range(2)]


def store_field(ref, row, field):
    for c in range(2):
        for a in range(3):
            ref[row, c, a] = field[c][a]


def combine(function, *fields):
    return [[function(*(f[c][a] for f in fields)) for a in range(3)] for c in range(2)]


def links_at(links_ref, row, link_set, mu):
    return links_ref, ((row * SETS + link_set) * MUS + mu) * ENTRIES


def entry(matrices, a, b, c, shape):
    ref, base = matrices
    return jnp.broadcast_to(ref[pl.ds(base + (a * 3 + b) * 2 + c, 1), :], shape)


def transport(matrices, ahead, here):
    forward = [[None] * 3, [None] * 3]
    backward = [[None] * 3, [None] * 3]
    shape = (ahead if ahead is not None else here)[0][0].shape

    def add(total, c, a, value):
        total[c][a] = value if total[c][a] is None else total[c][a] + value

    for a in range(3):
        for b in range(3):
            real = entry(matrices, a, b, 0, shape)
            imag = entry(matrices, a, b, 1, shape)
            if ahead is not None:
                add(forward, 0, a, real * ahead[0][b] - imag * ahead[1][b])
                add(forward, 1, a, real * ahead[1][b] + imag * ahead[0][b])
            if here is not None:
                add(backward, 0, b, real * here[0][a] + imag * here[1][a])
                add(backward, 1, b, real * here[1][a] - imag * here[0][a])
    return forward, backward


def roll(plane, by):
    return pltpu.roll(plane, by % plane.shape[-1], plane.ndim - 1)


def place(rows):
    first = lax.axis_index("gz") * rows
    plane, first_pos = first // BAND, lax.rem(first, BAND)
    return plane, first_pos, lax.rem(plane, 2) == 1, lax.rem(first_pos // rows, 2) == 1


def is_at_wrap(plane, rows):
    return (plane == 0) | (plane == lax.axis_size("gz") * rows // BAND - 1)


def taper_kernel(rows, source_ref, width_ref, steps_ref, coefs_ref):
    _, first_pos, _, _ = place(rows)
    ones = jnp.ones((8, 128), jnp.float32)
    per_width = ones * width_ref[0].astype(jnp.float32)
    for i in range(rows + 2):
        distance = ones * (first_pos + i - 1 - source_ref[0]).astype(jnp.float32) / per_width
        coefs_ref[i] = 1.0 / (1.0 + distance * distance)
    coefs_ref[rows + 2] = 0.25 / (ones * steps_ref[0].astype(jnp.float32))


def store_z(rows, matrices, row, field, middle_ref, near_ref, wrap_ref):
    _, _, odd_plane, _ = place(rows)
    _, up = transport(matrices, None, field)
    far = combine(lambda v, h: jnp.where(odd_plane, h, v), field, up)
    store_field(middle_ref, row, far)
    store_field(wrap_ref, row, far)
    store_field(near_ref, row, combine(lambda v, h: jnp.where(odd_plane, v, h), field, up))


def store_t(rows, matrices, field_ref, outer_ref, middle_ref, wrap_ref):
    plane, _, _, odd_block = place(rows)
    first = load_field(field_ref, 0)
    _, last = transport(matrices, None, load_field(field_ref, rows - 1))
    store_field(outer_ref, 0, combine(lambda p, q: jnp.where(odd_block, q, p), first, last))
    inner = combine(lambda p, q: jnp.where(odd_block, p, q), first, last)
    at_wrap = is_at_wrap(plane, rows)
    middle, wrap = load_field(middle_ref, 0), load_field(wrap_ref, 0)
    store_field(middle_ref, 0, combine(lambda p, q: jnp.where(at_wrap, q, p), middle, inner))
    store_field(wrap_ref, 0, combine(lambda p, q: jnp.where(at_wrap, p, q), wrap, inner))


def begin_kernel(
    rows, adjoint_hbm, links_hbm, middle_ref, near_ref, wrap_ref, outer_ref, adjoint_ref, links_ref, sems
):
    row_entries = SETS * MUS * ENTRIES
    z_first = (2 * MUS + 2) * ENTRIES
    aligned = z_first // 8 * 8
    copies = [pltpu.make_async_copy(adjoint_hbm, adjoint_ref, sems.at[rows])]
    for row in range(rows):
        part = links_hbm.at[pl.ds(row * row_entries + aligned, row_entries - aligned), :]
        copies.append(pltpu.make_async_copy(part, links_ref.at[row], sems.at[row]))
    for copy in copies:
        copy.start()
    for copy in copies:
        copy.wait()
    for row in range(rows):
        matrices = links_ref.at[row], z_first - aligned
        store_z(rows, matrices, row, load_field(adjoint_ref, row), middle_ref, near_ref, wrap_ref)
    store_t(rows, (links_ref.at[rows - 1], z_first + ENTRIES - aligned), adjoint_ref, outer_ref, middle_ref, wrap_ref)


def start_kernel(rows, link_set, coefs_ref, adjoint_ref, links_ref, sum_ref, start_ref):
    for row in range(rows):
        inside = coefs_ref[row + 1]
        store_field(start_ref, row, combine(lambda v: inside * v, load_field(adjoint_ref, row)))
    local_kernel(rows, link_set, start_ref, links_ref, sum_ref)


def local_kernel(rows, link_set, field_ref, links_ref, sum_ref):
    shape = field_ref.shape[-2:]
    x_pos = lax.broadcasted_iota(jnp.int32, shape, 1) % LX
    at_last = x_pos == LX - 1
    at_first = x_pos == 0

    def one(row, carry):
        here = load_field(field_ref, row)
        ahead = combine(lambda v: jnp.where(at_last, roll(v, LX - 1), roll(v, -1)), here)
        ahead_x, hop = transport(links_at(links_ref, row, link_set, 0), ahead, here)
        total = combine(
            lambda v, f, h: f + jnp.where(at_first, roll(h, 1 - LX), roll(h, 1)) - 8.0 * v, here, ahead_x, hop
        )
        ahead = combine(lambda v: roll(v, -LX), here)
        ahead_y, hop = transport(links_at(links_ref, row, link_set, 1), ahead, here)
        total = combine(lambda s, f, h: s + f + roll(h, LX), total, ahead_y, hop)
        store_field(sum_ref, row, total)
        return carry

    lax.fori_loop(0, rows, one, 0)

    def between(row, carry):
        ahead_t, hop = transport(
            links_at(links_ref, row, link_set, 3), load_field(field_ref, row + 1), load_field(field_ref, row)
        )
        store_field(sum_ref, row, combine(lambda s, f: s + f, load_field(sum_ref, row), ahead_t))
        store_field(sum_ref, row + 1, combine(lambda s, h: s + h, load_field(sum_ref, row + 1), hop))
        return carry

    lax.fori_loop(0, rows - 1, between, 0)


def arrived_sum(links_ref, link_set, row, rows, arrivals, coefs_ref=None):
    sum_ref, middle_ref, near_ref, wrap_ref, outer_ref = arrivals
    plane, first_pos, odd_plane, odd_block = place(rows)
    at_wrap = is_at_wrap(plane, rows)
    near = load_field(near_ref, row)
    far = combine(lambda p, q: jnp.where(at_wrap, q, p), load_field(middle_ref, row), load_field(wrap_ref, row))
    if coefs_ref is not None:
        far, near = (combine(lambda v: coefs_ref[row + 1] * v, f) for f in (far, near))
    above = combine(lambda p, q: jnp.where(odd_plane, p, q), far, near)
    ahead_z, _ = transport(links_at(links_ref, row, link_set, 2), above, None)
    total = combine(
        lambda s, f, p, q: s + f + jnp.where(odd_plane, q, p), load_field(sum_ref, row), ahead_z, far, near
    )
    outer = load_field(outer_ref, 0)
    inner = combine(lambda p, q: jnp.where(at_wrap, p, q), load_field(middle_ref, 0), load_field(wrap_ref, 0))
    if row == 0:
        exists = jnp.where(first_pos != 0, 1.0, 0.0)
        if coefs_ref is not None:
            exists = exists * coefs_ref[0]
        total = combine(lambda s, p, q: s + exists * jnp.where(odd_block, q, p), total, outer, inner)
    if row == rows - 1:
        exists = jnp.where(first_pos != BAND - rows, 1.0, 0.0)
        if coefs_ref is not None:
            exists = exists * coefs_ref[rows + 1]
        later = combine(lambda p, q: exists * jnp.where(odd_block, p, q), outer, inner)
        ahead_t, _ = transport(links_at(links_ref, row, link_set, 3), later, None)
        total = combine(lambda s, f: s + f, total, ahead_t)
    return total


def third_kernel(rows, coefs_ref, links_ref, *refs):
    arrivals, (third_ref, middle_ref, near_ref, wrap_ref, outer_ref) = refs[:5], refs[5:]
    for row in range(rows):
        inside, eps = coefs_ref[row + 1], coefs_ref[rows + 2]
        total = arrived_sum(links_ref, 2, row, rows, arrivals, coefs_ref)
        third = combine(lambda s: 0.75 * (inside * (eps * s)), total)
        store_field(third_ref, row, third)
        store_z(rows, links_at(links_ref, row, 1, 2), row, third, middle_ref, near_ref, wrap_ref)
    store_t(rows, links_at(links_ref, rows - 1, 1, 3), third_ref, outer_ref, middle_ref, wrap_ref)


def second_kernel(rows, coefs_ref, links_ref, *refs):
    arrivals, (start_ref, third_ref, mixed_ref, *sent, base_ref) = refs[:5], refs[5:]
    middle_ref, near_ref, wrap_ref, outer_ref = sent
    for row in range(rows):
        inside, eps = coefs_ref[row + 1], coefs_ref[rows + 2]
        total = arrived_sum(links_ref, 1, row, rows, arrivals)
        third = load_field(third_ref, row)
        second = combine(lambda v, s: v + (8.0 / 9.0) * (inside * (eps * s)), load_field(start_ref, row), total)
        mixed = combine(lambda p, q: 0.25 * p - (2.0 / 9.0) * q, second, third)
        store_field(mixed_ref, row, mixed)
        store_field(base_ref, row, combine(lambda p, q: p + q, second, third))
        store_z(rows, links_at(links_ref, row, 0, 2), row, mixed, middle_ref, near_ref, wrap_ref)
    store_t(rows, links_at(links_ref, rows - 1, 0, 3), mixed_ref, outer_ref, middle_ref, wrap_ref)


def last_kernel(rows, coefs_ref, links_ref, *refs):
    arrivals, (base_ref, out_ref) = refs[:5], refs[5:]
    for row in range(rows):
        inside, eps = coefs_ref[row + 1], coefs_ref[rows + 2]
        total = arrived_sum(links_ref, 0, row, rows, arrivals)
        store_field(out_ref, row, combine(lambda p, s: p + inside * (eps * s), load_field(base_ref, row), total))


def call(kernel, name, operands, out_shapes, matvecs, space=pltpu.VMEM, scratch=()):
    vmem = pl.BlockSpec(memory_space=pltpu.VMEM)
    return pl.pallas_call(
        kernel,
        name=name,
        out_shape=out_shapes,
        in_specs=[pl.BlockSpec(memory_space=space)] * len(operands),
        out_specs=jax.tree.map(lambda _: vmem, out_shapes),
        scratch_shapes=scratch,
        cost_estimate=pl.CostEstimate(flops=matvecs * 72 * 1024, bytes_accessed=4096 * 18 * matvecs, transcendentals=0),
        compiler_params=pltpu.CompilerParams(vmem_limit_bytes=16 * 2**20),
    )(*operands)


def body(adjoint, flowed, source_slice, band_width, flow_steps):
    rows = adjoint.shape[0]
    per_plane = BAND // rows
    count = lax.axis_size("gz")
    links = jnp.transpose(flowed, (0, 1, 2, 4, 5, 3, 6)).reshape(-1, flowed.shape[-1])
    whole = jax.ShapeDtypeStruct(adjoint.shape, jnp.float32)
    one_row = jax.ShapeDtypeStruct((1,) + adjoint.shape[1:], jnp.float32)
    coefs_shape = jax.ShapeDtypeStruct((rows + 3,) + adjoint.shape[3:], jnp.float32)

    def in_plane(i, by):
        return i - i % per_plane + (i + by) % per_plane

    def in_line(i, by):
        return (i + by * per_plane) % count

    planes = count // per_plane

    def far_or_inner(i, over_wrap):
        plane = i // per_plane
        if (plane in (0, planes - 1)) != over_wrap:
            return in_plane(i, -1 if i % 2 else 1)
        return in_line(i, 1 if plane % 2 else -1)

    middle_pairs = [(i, far_or_inner(i, False)) for i in range(count)]
    wrap_pairs = [(i, far_or_inner(i, True)) for i in range(count)]
    near_pairs = [(i, in_line(i, -1 if i // per_plane % 2 else 1)) for i in range(count)]
    outer_pairs = [(i, in_plane(i, 1 if i % 2 else -1)) for i in range(count)]

    def sent_on(middle, near, wrap, outer):
        middle = lax.ppermute(middle, "gz", middle_pairs)
        near = lax.ppermute(near, "gz", near_pairs)
        wrap = lax.ppermute(wrap, "gz", wrap_pairs)
        outer = lax.ppermute(outer, "gz", outer_pairs)
        return middle, near, wrap, outer

    def local(link_set, field):
        return call(functools.partial(local_kernel, rows, link_set), f"local_{link_set}", (field, links), whole, 22)

    sent = (whole, whole, whole, one_row)
    copied = SETS * MUS * ENTRIES - (2 * MUS + 2) * ENTRIES // 8 * 8
    sending = call(
        functools.partial(begin_kernel, rows), "begin",
        tuple(pltpu.with_memory_space_constraint(a, pltpu.HBM) for a in (adjoint, links)), sent, 5, pltpu.HBM,
        [
            pltpu.VMEM(adjoint.shape, jnp.float32),
            pltpu.VMEM((rows, copied, flowed.shape[-1]), jnp.float32),
            pltpu.SemaphoreType.DMA((rows + 1,)),
        ],
    )
    arrived = sent_on(*sending)
    coefs = call(
        functools.partial(taper_kernel, rows), "tapers", (source_slice, band_width, flow_steps), coefs_shape, 1,
        pltpu.SMEM,
    )
    total, start = call(
        functools.partial(start_kernel, rows, 2), "start", (coefs, adjoint, links), (whole, whole), 22
    )
    third, *sending = call(
        functools.partial(third_kernel, rows), "third", (coefs, links, total) + arrived, (whole,) + sent, 10
    )
    arrived = sent_on(*sending)
    mixed, *sending, base = call(
        functools.partial(second_kernel, rows), "second", (coefs, links, local(1, third)) + arrived + (start, third),
        (whole,) + sent + (whole,), 10,
    )
    arrived = sent_on(*sending)
    return call(
        functools.partial(last_kernel, rows), "last", (coefs, links, local(0, mixed)) + arrived + (base,), whole, 5
    )


def solution(mesh):
    in_specs = (
        P(("cfg", "gz"), None, None, None, None),
        P(("cfg", "gz"), None, None, None, None, None, None),
        P("cfg"),
        P("cfg"),
        P("cfg"),
    )
    out_specs = P(("cfg", "gz"), None, None, None, None)
    return jax.shard_map(body, mesh=mesh, in_specs=in_specs, out_specs=out_specs, check_vma=False)
```

```python
import functools

import jax
import jax.numpy as jnp
from jax import lax
from jax.experimental import pallas as pl
from jax.experimental.pallas import tpu as pltpu
from jax.sharding import PartitionSpec as P

BAND = 32
LX = 8
SETS = 3
MUS = 4
ENTRIES = 18


def load_field(ref, row):
    return [[ref[row, c, a] for a in range(3)] for c in range(2)]


def store_field(ref, row, field):
    for c in range(2):
        for a in range(3):
            ref[row, c, a] = field[c][a]


def combine(function, *fields):
    return [[function(*(f[c][a] for f in fields)) for a in range(3)] for c in range(2)]


def links_at(links_ref, row, link_set, mu):
    return links_ref, ((row * SETS + link_set) * MUS + mu) * ENTRIES


def entry(matrices, a, b, c, shape):
    ref, base = matrices
    return jnp.broadcast_to(ref[pl.ds(base + (a * 3 + b) * 2 + c, 1), :], shape)


def transport(matrices, ahead, here):
    forward = [[None] * 3, [None] * 3]
    backward = [[None] * 3, [None] * 3]
    shape = (ahead if ahead is not None else here)[0][0].shape

    def add(total, c, a, value):
        total[c][a] = value if total[c][a] is None else total[c][a] + value

    for a in range(3):
        for b in range(3):
            real = entry(matrices, a, b, 0, shape)
            imag = entry(matrices, a, b, 1, shape)
            if ahead is not None:
                add(forward, 0, a, real * ahead[0][b] - imag * ahead[1][b])
                add(forward, 1, a, real * ahead[1][b] + imag * ahead[0][b])
            if here is not None:
                add(backward, 0, b, real * here[0][a] + imag * here[1][a])
                add(backward, 1, b, real * here[1][a] - imag * here[0][a])
    return forward, backward


def roll(plane, by):
    return pltpu.roll(plane, by % plane.shape[-1], plane.ndim - 1)


def place(rows):
    first = lax.axis_index("gz") * rows
    plane, first_pos = first // BAND, lax.rem(first, BAND)
    return plane, first_pos, lax.rem(plane, 2) == 1, lax.rem(first_pos // rows, 2) == 1


def taper_kernel(rows, source_ref, width_ref, steps_ref, coefs_ref):
    _, first_pos, _, _ = place(rows)
    ones = jnp.ones((8, 128), jnp.float32)
    per_width = ones * width_ref[0].astype(jnp.float32)
    for i in range(rows + 2):
        distance = ones * (first_pos + i - 1 - source_ref[0]).astype(jnp.float32) / per_width
        coefs_ref[i] = 1.0 / (1.0 + distance * distance)
    coefs_ref[rows + 2] = 0.25 / (ones * steps_ref[0].astype(jnp.float32))


def store_z(rows, matrices, row, field, far_ref, near_ref):
    _, _, odd_plane, _ = place(rows)
    _, up = transport(matrices, None, field)
    store_field(far_ref, row, combine(lambda v, h: jnp.where(odd_plane, h, v), field, up))
    store_field(near_ref, row, combine(lambda v, h: jnp.where(odd_plane, v, h), field, up))


def store_t(rows, matrices, field_ref, outer_ref, inner_ref):
    _, _, _, odd_block = place(rows)
    first = load_field(field_ref, 0)
    _, last = transport(matrices, None, load_field(field_ref, rows - 1))
    store_field(outer_ref, 0, combine(lambda p, q: jnp.where(odd_block, q, p), first, last))
    store_field(inner_ref, 0, combine(lambda p, q: jnp.where(odd_block, p, q), first, last))


def begin_kernel(
    rows, adjoint_hbm, links_hbm, far_ref, near_ref, outer_ref, inner_ref, adjoint_ref, links_ref, sems
):
    row_entries = SETS * MUS * ENTRIES
    z_first = (2 * MUS + 2) * ENTRIES
    aligned = z_first // 8 * 8
    copies = [pltpu.make_async_copy(adjoint_hbm, adjoint_ref, sems.at[rows])]
    for row in range(rows):
        part = links_hbm.at[pl.ds(row * row_entries + aligned, row_entries - aligned), :]
        copies.append(pltpu.make_async_copy(part, links_ref.at[row], sems.at[row]))
    for copy in copies:
        copy.start()
    for copy in copies:
        copy.wait()
    for row in range(rows):
        matrices = links_ref.at[row], z_first - aligned
        store_z(rows, matrices, row, load_field(adjoint_ref, row), far_ref, near_ref)
    store_t(rows, (links_ref.at[rows - 1], z_first + ENTRIES - aligned), adjoint_ref, outer_ref, inner_ref)


def start_kernel(rows, link_set, coefs_ref, adjoint_ref, links_ref, sum_ref, start_ref):
    for row in range(rows):
        inside = coefs_ref[row + 1]
        store_field(start_ref, row, combine(lambda v: inside * v, load_field(adjoint_ref, row)))
    local_kernel(rows, link_set, start_ref, links_ref, sum_ref)


def local_kernel(rows, link_set, field_ref, links_ref, sum_ref):
    shape = field_ref.shape[-2:]
    x_pos = lax.broadcasted_iota(jnp.int32, shape, 1) % LX
    at_last = x_pos == LX - 1
    at_first = x_pos == 0

    for row in range(rows):
        here = load_field(field_ref, row)
        ahead = combine(lambda v: jnp.where(at_last, roll(v, LX - 1), roll(v, -1)), here)
        ahead_x, hop = transport(links_at(links_ref, row, link_set, 0), ahead, here)
        total = combine(
            lambda v, f, h: f + jnp.where(at_first, roll(h, 1 - LX), roll(h, 1)) - 8.0 * v, here, ahead_x, hop
        )
        ahead = combine(lambda v: roll(v, -LX), here)
        ahead_y, hop = transport(links_at(links_ref, row, link_set, 1), ahead, here)
        total = combine(lambda s, f, h: s + f + roll(h, LX), total, ahead_y, hop)
        if row > 0:
            total = combine(lambda s, h: s + h, total, earlier)
        if row < rows - 1:
            ahead_t, earlier = transport(links_at(links_ref, row, link_set, 3), load_field(field_ref, row + 1), here)
            total = combine(lambda s, f: s + f, total, ahead_t)
        store_field(sum_ref, row, total)


def arrived_sum(links_ref, link_set, row, rows, arrivals, coefs_ref=None):
    sum_ref, near_ref, far_ref, outer_ref, inner_ref = arrivals
    _, first_pos, odd_plane, odd_block = place(rows)
    far, near = load_field(far_ref, row), load_field(near_ref, row)
    if coefs_ref is not None:
        far, near = (combine(lambda v: coefs_ref[row + 1] * v, f) for f in (far, near))
    above = combine(lambda p, q: jnp.where(odd_plane, p, q), far, near)
    ahead_z, _ = transport(links_at(links_ref, row, link_set, 2), above, None)
    total = combine(
        lambda s, f, p, q: s + f + jnp.where(odd_plane, q, p), load_field(sum_ref, row), ahead_z, far, near
    )
    outer, inner = load_field(outer_ref, 0), load_field(inner_ref, 0)
    if row == 0:
        exists = jnp.where(first_pos != 0, 1.0, 0.0)
        if coefs_ref is not None:
            exists = exists * coefs_ref[0]
        total = combine(lambda s, p, q: s + exists * jnp.where(odd_block, q, p), total, outer, inner)
    if row == rows - 1:
        exists = jnp.where(first_pos != BAND - rows, 1.0, 0.0)
        if coefs_ref is not None:
            exists = exists * coefs_ref[rows + 1]
        later = combine(lambda p, q: exists * jnp.where(odd_block, p, q), outer, inner)
        ahead_t, _ = transport(links_at(links_ref, row, link_set, 3), later, None)
        total = combine(lambda s, f: s + f, total, ahead_t)
    return total


def third_kernel(rows, coefs_ref, links_ref, *refs):
    arrivals, (third_ref, far_ref, near_ref, outer_ref, inner_ref) = refs[:5], refs[5:]
    for row in range(rows):
        inside, eps = coefs_ref[row + 1], coefs_ref[rows + 2]
        total = arrived_sum(links_ref, 2, row, rows, arrivals, coefs_ref)
        third = combine(lambda s: 0.75 * (inside * (eps * s)), total)
        store_field(third_ref, row, third)
        store_z(rows, links_at(links_ref, row, 1, 2), row, third, far_ref, near_ref)
    store_t(rows, links_at(links_ref, rows - 1, 1, 3), third_ref, outer_ref, inner_ref)


def second_kernel(rows, coefs_ref, links_ref, *refs):
    arrivals, (start_ref, third_ref, mixed_ref, far_ref, near_ref, outer_ref, inner_ref, base_ref) = refs[:5], refs[5:]
    for row in range(rows):
        inside, eps = coefs_ref[row + 1], coefs_ref[rows + 2]
        total = arrived_sum(links_ref, 1, row, rows, arrivals)
        third = load_field(third_ref, row)
        second = combine(lambda v, s: v + (8.0 / 9.0) * (inside * (eps * s)), load_field(start_ref, row), total)
        mixed = combine(lambda p, q: 0.25 * p - (2.0 / 9.0) * q, second, third)
        store_field(mixed_ref, row, mixed)
        store_field(base_ref, row, combine(lambda p, q: p + q, second, third))
        store_z(rows, links_at(links_ref, row, 0, 2), row, mixed, far_ref, near_ref)
    store_t(rows, links_at(links_ref, rows - 1, 0, 3), mixed_ref, outer_ref, inner_ref)


def last_kernel(rows, coefs_ref, links_ref, *refs):
    arrivals, (base_ref, out_hbm, out_ref, sems) = refs[:5], refs[5:]
    copies = []
    for row in range(rows):
        inside, eps = coefs_ref[row + 1], coefs_ref[rows + 2]
        total = arrived_sum(links_ref, 0, row, rows, arrivals)
        store_field(out_ref, row, combine(lambda p, s: p + inside * (eps * s), load_field(base_ref, row), total))
        copies.append(pltpu.make_async_copy(out_ref.at[row], out_hbm.at[row], sems.at[row]))
        copies[-1].start()
    for copy in copies:
        copy.wait()


def call(kernel, name, operands, out_shapes, matvecs, space=pltpu.VMEM, scratch=(), out_space=pltpu.VMEM):
    out_spec = pl.BlockSpec(memory_space=out_space)
    return pl.pallas_call(
        kernel,
        name=name,
        out_shape=out_shapes,
        in_specs=[pl.BlockSpec(memory_space=space)] * len(operands),
        out_specs=jax.tree.map(lambda _: out_spec, out_shapes),
        scratch_shapes=scratch,
        cost_estimate=pl.CostEstimate(flops=matvecs * 72 * 1024, bytes_accessed=4096 * 18 * matvecs, transcendentals=0),
        compiler_params=pltpu.CompilerParams(vmem_limit_bytes=16 * 2**20),
    )(*operands)


def body(adjoint, flowed, source_slice, band_width, flow_steps):
    rows = adjoint.shape[0]
    per_plane = BAND // rows
    count = lax.axis_size("gz")
    links = jnp.transpose(flowed, (0, 1, 2, 4, 5, 3, 6)).reshape(-1, flowed.shape[-1])
    whole = jax.ShapeDtypeStruct(adjoint.shape, jnp.float32)
    one_row = jax.ShapeDtypeStruct((1,) + adjoint.shape[1:], jnp.float32)
    coefs_shape = jax.ShapeDtypeStruct((rows + 3,) + adjoint.shape[3:], jnp.float32)

    def in_plane(i, by):
        return i - i % per_plane + (i + by) % per_plane

    def in_line(i, by):
        return (i + by * per_plane) % count

    far_pairs = [(i, in_line(i, 1 if i // per_plane % 2 else -1)) for i in range(count)]
    near_pairs = [(i, in_line(i, -1 if i // per_plane % 2 else 1)) for i in range(count)]
    outer_pairs = [(i, in_plane(i, 1 if i % 2 else -1)) for i in range(count)]
    inner_pairs = [(i, in_plane(i, -1 if i % 2 else 1)) for i in range(count)]

    def sent_on(far, near, outer, inner):
        near = lax.ppermute(near, "gz", near_pairs)
        far = lax.ppermute(far, "gz", far_pairs)
        outer = lax.ppermute(outer, "gz", outer_pairs)
        inner = lax.ppermute(inner, "gz", inner_pairs)
        return near, far, outer, inner

    def local(link_set, field):
        return call(functools.partial(local_kernel, rows, link_set), f"local_{link_set}", (field, links), whole, 22)

    sent = (whole, whole, one_row, one_row)
    copied = SETS * MUS * ENTRIES - (2 * MUS + 2) * ENTRIES // 8 * 8
    sending = call(
        functools.partial(begin_kernel, rows), "begin",
        tuple(pltpu.with_memory_space_constraint(a, pltpu.HBM) for a in (adjoint, links)), sent, 5, pltpu.HBM,
        [
            pltpu.VMEM(adjoint.shape, jnp.float32),
            pltpu.VMEM((rows, copied, flowed.shape[-1]), jnp.float32),
            pltpu.SemaphoreType.DMA((rows + 1,)),
        ],
    )
    arrived = sent_on(*sending)
    coefs = call(
        functools.partial(taper_kernel, rows), "tapers", (source_slice, band_width, flow_steps), coefs_shape, 1,
        pltpu.SMEM,
    )
    total, start = call(
        functools.partial(start_kernel, rows, 2), "start", (coefs, adjoint, links), (whole, whole), 22
    )
    third, *sending = call(
        functools.partial(third_kernel, rows), "third", (coefs, links, total) + arrived, (whole,) + sent, 10
    )
    arrived = sent_on(*sending)
    mixed, *sending, base = call(
        functools.partial(second_kernel, rows), "second", (coefs, links, local(1, third)) + arrived + (start, third),
        (whole,) + sent + (whole,), 10,
    )
    arrived = sent_on(*sending)
    return call(
        functools.partial(last_kernel, rows), "last", (coefs, links, local(0, mixed)) + arrived + (base,), whole, 5,
        scratch=[pltpu.VMEM(adjoint.shape, jnp.float32), pltpu.SemaphoreType.DMA((rows,))], out_space=pltpu.HBM,
    )


def solution(mesh):
    in_specs = (
        P(("cfg", "gz"), None, None, None, None),
        P(("cfg", "gz"), None, None, None, None, None, None),
        P("cfg"),
        P("cfg"),
        P("cfg"),
    )
    out_specs = P(("cfg", "gz"), None, None, None, None)
    return jax.shard_map(body, mesh=mesh, in_specs=in_specs, out_specs=out_specs, check_vma=False)
```

```python
import functools

import jax
import jax.numpy as jnp
from jax import lax
from jax.experimental import pallas as pl
from jax.experimental.pallas import tpu as pltpu
from jax.sharding import PartitionSpec as P

BAND = 32
LX = 8
SETS = 3
MUS = 4
ENTRIES = 18


def load_field(ref, row):
    return [[ref[row, c, a] for a in range(3)] for c in range(2)]


def store_field(ref, row, field):
    for c in range(2):
        for a in range(3):
            ref[row, c, a] = field[c][a]


def combine(function, *fields):
    return [[function(*(f[c][a] for f in fields)) for a in range(3)] for c in range(2)]


def links_at(links_ref, row, link_set, mu):
    return links_ref, ((row * SETS + link_set) * MUS + mu) * ENTRIES


def entry(matrices, a, b, c, shape):
    ref, base = matrices
    return jnp.broadcast_to(ref[pl.ds(base + (a * 3 + b) * 2 + c, 1), :], shape)


def transport(matrices, ahead, here):
    forward = [[None] * 3, [None] * 3]
    backward = [[None] * 3, [None] * 3]
    shape = (ahead if ahead is not None else here)[0][0].shape

    def add(total, c, a, value):
        total[c][a] = value if total[c][a] is None else total[c][a] + value

    for a in range(3):
        for b in range(3):
            real = entry(matrices, a, b, 0, shape)
            imag = entry(matrices, a, b, 1, shape)
            if ahead is not None:
                add(forward, 0, a, real * ahead[0][b] - imag * ahead[1][b])
                add(forward, 1, a, real * ahead[1][b] + imag * ahead[0][b])
            if here is not None:
                add(backward, 0, b, real * here[0][a] + imag * here[1][a])
                add(backward, 1, b, real * here[1][a] - imag * here[0][a])
    return forward, backward


def roll(plane, by):
    return pltpu.roll(plane, by % plane.shape[-1], plane.ndim - 1)


def place(rows):
    first = lax.axis_index("gz") * rows
    plane, first_pos = first // BAND, lax.rem(first, BAND)
    return plane, first_pos, lax.rem(plane, 2) == 1, lax.rem(first_pos // rows, 2) == 1


def taper_kernel(rows, source_ref, width_ref, coefs_ref):
    _, first_pos, _, _ = place(rows)
    ones = jnp.ones((8, 128), jnp.float32)
    per_width = ones * width_ref[0].astype(jnp.float32)
    for i in range(rows + 2):
        distance = ones * (first_pos + i - 1 - source_ref[0]).astype(jnp.float32) / per_width
        coefs_ref[i] = 1.0 / (1.0 + distance * distance)


def eps_kernel(steps_ref, eps_ref):
    eps_ref[...] = 0.25 / (jnp.ones((8, 128), jnp.float32) * steps_ref[0].astype(jnp.float32))


def store_z(rows, matrices, row, field, far_ref, near_ref):
    _, _, odd_plane, _ = place(rows)
    _, up = transport(matrices, None, field)
    store_field(far_ref, row, combine(lambda v, h: jnp.where(odd_plane, h, v), field, up))
    store_field(near_ref, row, combine(lambda v, h: jnp.where(odd_plane, v, h), field, up))


def store_t(rows, matrices, field_ref, outer_ref, inner_ref):
    _, _, _, odd_block = place(rows)
    first = load_field(field_ref, 0)
    _, last = transport(matrices, None, load_field(field_ref, rows - 1))
    store_field(outer_ref, 0, combine(lambda p, q: jnp.where(odd_block, q, p), first, last))
    store_field(inner_ref, 0, combine(lambda p, q: jnp.where(odd_block, p, q), first, last))


def begin_kernel(
    rows, adjoint_hbm, links_hbm, far_ref, near_ref, outer_ref, inner_ref, adjoint_ref, links_ref, sems
):
    row_entries = SETS * MUS * ENTRIES
    z_first = (2 * MUS + 2) * ENTRIES
    aligned = z_first // 8 * 8
    copies = [pltpu.make_async_copy(adjoint_hbm, adjoint_ref, sems.at[rows])]
    for row in range(rows):
        part = links_hbm.at[pl.ds(row * row_entries + aligned, row_entries - aligned), :]
        copies.append(pltpu.make_async_copy(part, links_ref.at[row], sems.at[row]))
    for copy in copies:
        copy.start()
    for copy in copies:
        copy.wait()
    for row in range(rows):
        matrices = links_ref.at[row], z_first - aligned
        store_z(rows, matrices, row, load_field(adjoint_ref, row), far_ref, near_ref)
    store_t(rows, (links_ref.at[rows - 1], z_first + ENTRIES - aligned), adjoint_ref, outer_ref, inner_ref)


def start_kernel(rows, link_set, coefs_ref, adjoint_ref, links_ref, sum_ref, start_ref):
    for row in range(rows):
        inside = coefs_ref[row + 1]
        store_field(start_ref, row, combine(lambda v: inside * v, load_field(adjoint_ref, row)))
    local_kernel(rows, link_set, start_ref, links_ref, sum_ref)


def local_kernel(rows, link_set, field_ref, links_ref, sum_ref):
    shape = field_ref.shape[-2:]
    x_pos = lax.broadcasted_iota(jnp.int32, shape, 1) % LX
    at_last = x_pos == LX - 1
    at_first = x_pos == 0

    for row in range(rows):
        here = load_field(field_ref, row)
        ahead = combine(lambda v: jnp.where(at_last, roll(v, LX - 1), roll(v, -1)), here)
        ahead_x, hop = transport(links_at(links_ref, row, link_set, 0), ahead, here)
        total = combine(
            lambda v, f, h: f + jnp.where(at_first, roll(h, 1 - LX), roll(h, 1)) - 8.0 * v, here, ahead_x, hop
        )
        ahead = combine(lambda v: roll(v, -LX), here)
        ahead_y, hop = transport(links_at(links_ref, row, link_set, 1), ahead, here)
        total = combine(lambda s, f, h: s + f + roll(h, LX), total, ahead_y, hop)
        if row > 0:
            total = combine(lambda s, h: s + h, total, earlier)
        if row < rows - 1:
            ahead_t, earlier = transport(links_at(links_ref, row, link_set, 3), load_field(field_ref, row + 1), here)
            total = combine(lambda s, f: s + f, total, ahead_t)
        store_field(sum_ref, row, total)


def arrived_sum(links_ref, link_set, row, rows, arrivals, coefs_ref=None):
    sum_ref, near_ref, far_ref, outer_ref, inner_ref = arrivals
    _, first_pos, odd_plane, odd_block = place(rows)
    far, near = load_field(far_ref, row), load_field(near_ref, row)
    if coefs_ref is not None:
        far, near = (combine(lambda v: coefs_ref[row + 1] * v, f) for f in (far, near))
    above = combine(lambda p, q: jnp.where(odd_plane, p, q), far, near)
    ahead_z, _ = transport(links_at(links_ref, row, link_set, 2), above, None)
    total = combine(
        lambda s, f, p, q: s + f + jnp.where(odd_plane, q, p), load_field(sum_ref, row), ahead_z, far, near
    )
    outer, inner = load_field(outer_ref, 0), load_field(inner_ref, 0)
    if row == 0:
        exists = jnp.where(first_pos != 0, 1.0, 0.0)
        if coefs_ref is not None:
            exists = exists * coefs_ref[0]
        total = combine(lambda s, p, q: s + exists * jnp.where(odd_block, q, p), total, outer, inner)
    if row == rows - 1:
        exists = jnp.where(first_pos != BAND - rows, 1.0, 0.0)
        if coefs_ref is not None:
            exists = exists * coefs_ref[rows + 1]
        later = combine(lambda p, q: exists * jnp.where(odd_block, p, q), outer, inner)
        ahead_t, _ = transport(links_at(links_ref, row, link_set, 3), later, None)
        total = combine(lambda s, f: s + f, total, ahead_t)
    return total


def third_kernel(rows, coefs_ref, links_ref, *refs):
    arrivals, (third_ref, far_ref, near_ref, outer_ref, inner_ref) = refs[:5], refs[5:]
    for row in range(rows):
        inside = coefs_ref[row + 1]
        total = arrived_sum(links_ref, 2, row, rows, arrivals, coefs_ref)
        third = combine(lambda s: 0.75 * (inside * s), total)
        store_field(third_ref, row, third)
        store_z(rows, links_at(links_ref, row, 1, 2), row, third, far_ref, near_ref)
    store_t(rows, links_at(links_ref, rows - 1, 1, 3), third_ref, outer_ref, inner_ref)


def second_kernel(rows, eps_ref, coefs_ref, links_ref, *refs):
    arrivals, (start_ref, third_ref, mixed_ref, far_ref, near_ref, outer_ref, inner_ref, base_ref) = refs[:5], refs[5:]
    eps = eps_ref[...]
    for row in range(rows):
        inside = coefs_ref[row + 1]
        total = arrived_sum(links_ref, 1, row, rows, arrivals)
        third = combine(lambda v: eps * v, load_field(third_ref, row))
        second = combine(
            lambda v, s: v + (8.0 / 9.0) * (inside * (eps * (eps * s))), load_field(start_ref, row), total
        )
        mixed = combine(lambda p, q: 0.25 * p - (2.0 / 9.0) * q, second, third)
        store_field(mixed_ref, row, mixed)
        store_field(base_ref, row, combine(lambda p, q: p + q, second, third))
        store_z(rows, links_at(links_ref, row, 0, 2), row, mixed, far_ref, near_ref)
    store_t(rows, links_at(links_ref, rows - 1, 0, 3), mixed_ref, outer_ref, inner_ref)


def last_kernel(rows, eps_ref, coefs_ref, links_ref, *refs):
    arrivals, (base_ref, out_hbm, out_ref, sems) = refs[:5], refs[5:]
    copies = []
    for row in range(rows):
        inside, eps = coefs_ref[row + 1], eps_ref[...]
        total = arrived_sum(links_ref, 0, row, rows, arrivals)
        store_field(out_ref, row, combine(lambda p, s: p + inside * (eps * s), load_field(base_ref, row), total))
        copies.append(pltpu.make_async_copy(out_ref.at[row], out_hbm.at[row], sems.at[row]))
        copies[-1].start()
    for copy in copies:
        copy.wait()


def call(kernel, name, operands, out_shapes, matvecs, space=pltpu.VMEM, scratch=(), out_space=pltpu.VMEM):
    out_spec = pl.BlockSpec(memory_space=out_space)
    return pl.pallas_call(
        kernel,
        name=name,
        out_shape=out_shapes,
        in_specs=[pl.BlockSpec(memory_space=space)] * len(operands),
        out_specs=jax.tree.map(lambda _: out_spec, out_shapes),
        scratch_shapes=scratch,
        cost_estimate=pl.CostEstimate(flops=matvecs * 72 * 1024, bytes_accessed=4096 * 18 * matvecs, transcendentals=0),
        compiler_params=pltpu.CompilerParams(vmem_limit_bytes=16 * 2**20),
    )(*operands)


def body(adjoint, flowed, source_slice, band_width, flow_steps):
    rows = adjoint.shape[0]
    per_plane = BAND // rows
    count = lax.axis_size("gz")
    links = jnp.transpose(flowed, (0, 1, 2, 4, 5, 3, 6)).reshape(-1, flowed.shape[-1])
    whole = jax.ShapeDtypeStruct(adjoint.shape, jnp.float32)
    one_row = jax.ShapeDtypeStruct((1,) + adjoint.shape[1:], jnp.float32)
    coefs_shape = jax.ShapeDtypeStruct((rows + 2,) + adjoint.shape[3:], jnp.float32)

    def in_plane(i, by):
        return i - i % per_plane + (i + by) % per_plane

    def in_line(i, by):
        return (i + by * per_plane) % count

    far_pairs = [(i, in_line(i, 1 if i // per_plane % 2 else -1)) for i in range(count)]
    near_pairs = [(i, in_line(i, -1 if i // per_plane % 2 else 1)) for i in range(count)]
    outer_pairs = [(i, in_plane(i, 1 if i % 2 else -1)) for i in range(count)]
    inner_pairs = [(i, in_plane(i, -1 if i % 2 else 1)) for i in range(count)]

    def sent_on(far, near, outer, inner):
        near = lax.ppermute(near, "gz", near_pairs)
        far = lax.ppermute(far, "gz", far_pairs)
        outer = lax.ppermute(outer, "gz", outer_pairs)
        inner = lax.ppermute(inner, "gz", inner_pairs)
        return near, far, outer, inner

    def local(link_set, field):
        return call(functools.partial(local_kernel, rows, link_set), f"local_{link_set}", (field, links), whole, 22)

    sent = (whole, whole, one_row, one_row)
    copied = SETS * MUS * ENTRIES - (2 * MUS + 2) * ENTRIES // 8 * 8
    sending = call(
        functools.partial(begin_kernel, rows), "begin",
        tuple(pltpu.with_memory_space_constraint(a, pltpu.HBM) for a in (adjoint, links)), sent, 5, pltpu.HBM,
        [
            pltpu.VMEM(adjoint.shape, jnp.float32),
            pltpu.VMEM((rows, copied, flowed.shape[-1]), jnp.float32),
            pltpu.SemaphoreType.DMA((rows + 1,)),
        ],
    )
    arrived = sent_on(*sending)
    coefs = call(
        functools.partial(taper_kernel, rows), "tapers", (source_slice, band_width), coefs_shape, 1, pltpu.SMEM
    )
    eps_shape = jax.ShapeDtypeStruct(adjoint.shape[3:], jnp.float32)
    eps = call(eps_kernel, "eps", (flow_steps,), eps_shape, 1, pltpu.SMEM)
    total, start = call(
        functools.partial(start_kernel, rows, 2), "start", (coefs, adjoint, links), (whole, whole), 22
    )
    third, *sending = call(
        functools.partial(third_kernel, rows), "third", (coefs, links, total) + arrived, (whole,) + sent, 10
    )
    arrived = sent_on(*sending)
    mixed, *sending, base = call(
        functools.partial(second_kernel, rows), "second", (eps, coefs, links, local(1, third)) + arrived + (start, third),
        (whole,) + sent + (whole,), 10,
    )
    arrived = sent_on(*sending)
    return call(
        functools.partial(last_kernel, rows), "last", (eps, coefs, links, local(0, mixed)) + arrived + (base,), whole, 5,
        scratch=[pltpu.VMEM(adjoint.shape, jnp.float32), pltpu.SemaphoreType.DMA((rows,))], out_space=pltpu.HBM,
    )


def solution(mesh):
    in_specs = (
        P(("cfg", "gz"), None, None, None, None),
        P(("cfg", "gz"), None, None, None, None, None, None),
        P("cfg"),
        P("cfg"),
        P("cfg"),
    )
    out_specs = P(("cfg", "gz"), None, None, None, None)
    return jax.shard_map(body, mesh=mesh, in_specs=in_specs, out_specs=out_specs, check_vma=False)
```

```python
import functools

import jax
import jax.numpy as jnp
from jax import lax
from jax.experimental import pallas as pl
from jax.experimental.pallas import tpu as pltpu
from jax.sharding import PartitionSpec as P

BAND = 32
LX = 8
SETS = 3
MUS = 4
ENTRIES = 18


def load_field(ref, row):
    return [[ref[row, c, a] for a in range(3)] for c in range(2)]


def store_field(ref, row, field):
    for c in range(2):
        for a in range(3):
            ref[row, c, a] = field[c][a]


def combine(function, *fields):
    return [[function(*(f[c][a] for f in fields)) for a in range(3)] for c in range(2)]


def links_at(links_ref, row, link_set, mu):
    return links_ref, ((row * SETS + link_set) * MUS + mu) * ENTRIES


def entry(matrices, a, b, c, shape):
    ref, base = matrices
    return jnp.broadcast_to(ref[pl.ds(base + (a * 3 + b) * 2 + c, 1), :], shape)


def transport(matrices, ahead, here):
    forward = [[None] * 3, [None] * 3]
    backward = [[None] * 3, [None] * 3]
    shape = (ahead if ahead is not None else here)[0][0].shape

    def add(total, c, a, value):
        total[c][a] = value if total[c][a] is None else total[c][a] + value

    for a in range(3):
        for b in range(3):
            real = entry(matrices, a, b, 0, shape)
            imag = entry(matrices, a, b, 1, shape)
            if ahead is not None:
                add(forward, 0, a, real * ahead[0][b] - imag * ahead[1][b])
                add(forward, 1, a, real * ahead[1][b] + imag * ahead[0][b])
            if here is not None:
                add(backward, 0, b, real * here[0][a] + imag * here[1][a])
                add(backward, 1, b, real * here[1][a] - imag * here[0][a])
    return forward, backward


def roll(plane, by):
    return pltpu.roll(plane, by % plane.shape[-1], plane.ndim - 1)


def place(rows):
    first = lax.axis_index("gz") * rows
    plane, first_pos = first // BAND, lax.rem(first, BAND)
    return plane, first_pos, lax.rem(plane, 2) == 1, lax.rem(first_pos // rows, 2) == 1


def taper_kernel(rows, source_ref, width_ref, coefs_ref):
    _, first_pos, _, _ = place(rows)
    ones = jnp.ones((8, 128), jnp.float32)
    per_width = ones * width_ref[0].astype(jnp.float32)
    for i in range(rows + 2):
        distance = ones * (first_pos + i - 1 - source_ref[0]).astype(jnp.float32) / per_width
        coefs_ref[i] = 1.0 / (1.0 + distance * distance)


def eps_kernel(steps_ref, eps_ref):
    eps_ref[...] = 0.25 / (jnp.ones((8, 128), jnp.float32) * steps_ref[0].astype(jnp.float32))


def store_z(rows, matrices, row, field, far_ref, near_ref):
    _, _, odd_plane, _ = place(rows)
    _, up = transport(matrices, None, field)
    store_field(far_ref, row, combine(lambda v, h: jnp.where(odd_plane, h, v), field, up))
    store_field(near_ref, row, combine(lambda v, h: jnp.where(odd_plane, v, h), field, up))


def store_t(rows, matrices, field_ref, outer_ref, inner_ref):
    _, _, _, odd_block = place(rows)
    first = load_field(field_ref, 0)
    _, last = transport(matrices, None, load_field(field_ref, rows - 1))
    store_field(outer_ref, 0, combine(lambda p, q: jnp.where(odd_block, q, p), first, last))
    store_field(inner_ref, 0, combine(lambda p, q: jnp.where(odd_block, p, q), first, last))


def begin_kernel(
    rows, adjoint_hbm, links_hbm, far_ref, near_ref, outer_ref, inner_ref, adjoint_ref, links_ref, sems
):
    row_entries = SETS * MUS * ENTRIES
    z_first = (2 * MUS + 2) * ENTRIES
    aligned = z_first // 8 * 8
    copies = [pltpu.make_async_copy(adjoint_hbm, adjoint_ref, sems.at[rows])]
    for row in range(rows):
        part = links_hbm.at[pl.ds(row * row_entries + aligned, row_entries - aligned), :]
        copies.append(pltpu.make_async_copy(part, links_ref.at[row], sems.at[row]))
    for copy in copies:
        copy.start()
    for copy in copies:
        copy.wait()
    for row in range(rows):
        matrices = links_ref.at[row], z_first - aligned
        store_z(rows, matrices, row, load_field(adjoint_ref, row), far_ref, near_ref)
    store_t(rows, (links_ref.at[rows - 1], z_first + ENTRIES - aligned), adjoint_ref, outer_ref, inner_ref)


def start_kernel(rows, link_set, coefs_ref, adjoint_ref, links_ref, sum_ref, start_ref):
    for row in range(rows):
        inside = coefs_ref[row + 1]
        store_field(start_ref, row, combine(lambda v: inside * v, load_field(adjoint_ref, row)))
    local_kernel(rows, link_set, start_ref, links_ref, sum_ref)


def local_kernel(rows, link_set, field_ref, links_ref, sum_ref):
    shape = field_ref.shape[-2:]
    x_pos = lax.broadcasted_iota(jnp.int32, shape, 1) % LX
    at_last = x_pos == LX - 1
    at_first = x_pos == 0

    for row in range(rows):
        here = load_field(field_ref, row)
        ahead = combine(lambda v: jnp.where(at_last, roll(v, LX - 1), roll(v, -1)), here)
        ahead_x, hop = transport(links_at(links_ref, row, link_set, 0), ahead, here)
        total = combine(
            lambda v, f, h: f + jnp.where(at_first, roll(h, 1 - LX), roll(h, 1)) - 8.0 * v, here, ahead_x, hop
        )
        ahead = combine(lambda v: roll(v, -LX), here)
        ahead_y, hop = transport(links_at(links_ref, row, link_set, 1), ahead, here)
        total = combine(lambda s, f, h: s + f + roll(h, LX), total, ahead_y, hop)
        if row > 0:
            total = combine(lambda s, h: s + h, total, earlier)
        if row < rows - 1:
            ahead_t, earlier = transport(links_at(links_ref, row, link_set, 3), load_field(field_ref, row + 1), here)
            total = combine(lambda s, f: s + f, total, ahead_t)
        store_field(sum_ref, row, total)


def arrived_sum(links_ref, link_set, row, rows, arrivals, coefs_ref=None):
    sum_ref, near_ref, far_ref, outer_ref, inner_ref = arrivals
    if coefs_ref is not None:
        near_ref, far_ref = far_ref, near_ref
    _, first_pos, odd_plane, odd_block = place(rows)
    far, near = load_field(far_ref, row), load_field(near_ref, row)
    if coefs_ref is not None:
        far, near = (combine(lambda v: coefs_ref[row + 1] * v, f) for f in (far, near))
    above = combine(lambda p, q: jnp.where(odd_plane, p, q), far, near)
    ahead_z, _ = transport(links_at(links_ref, row, link_set, 2), above, None)
    total = combine(
        lambda s, f, p, q: s + f + jnp.where(odd_plane, q, p), load_field(sum_ref, row), ahead_z, far, near
    )
    outer, inner = load_field(outer_ref, 0), load_field(inner_ref, 0)
    if row == 0:
        exists = jnp.where(first_pos != 0, 1.0, 0.0)
        if coefs_ref is not None:
            exists = exists * coefs_ref[0]
        total = combine(lambda s, p, q: s + exists * jnp.where(odd_block, q, p), total, outer, inner)
    if row == rows - 1:
        exists = jnp.where(first_pos != BAND - rows, 1.0, 0.0)
        if coefs_ref is not None:
            exists = exists * coefs_ref[rows + 1]
        later = combine(lambda p, q: exists * jnp.where(odd_block, p, q), outer, inner)
        ahead_t, _ = transport(links_at(links_ref, row, link_set, 3), later, None)
        total = combine(lambda s, f: s + f, total, ahead_t)
    return total


def third_kernel(rows, coefs_ref, links_ref, *refs):
    arrivals, (third_ref, far_ref, near_ref, outer_ref, inner_ref) = refs[:5], refs[5:]
    for row in range(rows):
        inside = coefs_ref[row + 1]
        total = arrived_sum(links_ref, 2, row, rows, arrivals, coefs_ref)
        third = combine(lambda s: 0.75 * (inside * s), total)
        store_field(third_ref, row, third)
        store_z(rows, links_at(links_ref, row, 1, 2), row, third, far_ref, near_ref)
    store_t(rows, links_at(links_ref, rows - 1, 1, 3), third_ref, outer_ref, inner_ref)


def second_kernel(rows, eps_ref, coefs_ref, links_ref, *refs):
    arrivals, (start_ref, third_ref, mixed_ref, far_ref, near_ref, outer_ref, inner_ref, base_ref) = refs[:5], refs[5:]
    eps = eps_ref[...]
    for row in range(rows):
        inside = coefs_ref[row + 1]
        total = arrived_sum(links_ref, 1, row, rows, arrivals)
        third = combine(lambda v: eps * v, load_field(third_ref, row))
        second = combine(
            lambda v, s: v + (8.0 / 9.0) * (inside * (eps * (eps * s))), load_field(start_ref, row), total
        )
        mixed = combine(lambda p, q: 0.25 * p - (2.0 / 9.0) * q, second, third)
        store_field(mixed_ref, row, mixed)
        store_field(base_ref, row, combine(lambda p, q: p + q, second, third))
        store_z(rows, links_at(links_ref, row, 0, 2), row, mixed, far_ref, near_ref)
    store_t(rows, links_at(links_ref, rows - 1, 0, 3), mixed_ref, outer_ref, inner_ref)


def last_kernel(rows, eps_ref, coefs_ref, links_ref, *refs):
    arrivals, (base_ref, out_hbm, out_ref, sems) = refs[:5], refs[5:]
    copies = []
    for row in range(rows):
        inside, eps = coefs_ref[row + 1], eps_ref[...]
        total = arrived_sum(links_ref, 0, row, rows, arrivals)
        store_field(out_ref, row, combine(lambda p, s: p + inside * (eps * s), load_field(base_ref, row), total))
        copies.append(pltpu.make_async_copy(out_ref.at[row], out_hbm.at[row], sems.at[row]))
        copies[-1].start()
    for copy in copies:
        copy.wait()


def call(kernel, name, operands, out_shapes, matvecs, space=pltpu.VMEM, scratch=(), out_space=pltpu.VMEM):
    out_spec = pl.BlockSpec(memory_space=out_space)
    return pl.pallas_call(
        kernel,
        name=name,
        out_shape=out_shapes,
        in_specs=[pl.BlockSpec(memory_space=space)] * len(operands),
        out_specs=jax.tree.map(lambda _: out_spec, out_shapes),
        scratch_shapes=scratch,
        cost_estimate=pl.CostEstimate(flops=matvecs * 72 * 1024, bytes_accessed=4096 * 18 * matvecs, transcendentals=0),
        compiler_params=pltpu.CompilerParams(vmem_limit_bytes=16 * 2**20),
    )(*operands)


def body(adjoint, flowed, source_slice, band_width, flow_steps):
    rows = adjoint.shape[0]
    per_plane = BAND // rows
    count = lax.axis_size("gz")
    links = jnp.transpose(flowed, (0, 1, 2, 4, 5, 3, 6)).reshape(-1, flowed.shape[-1])
    whole = jax.ShapeDtypeStruct(adjoint.shape, jnp.float32)
    one_row = jax.ShapeDtypeStruct((1,) + adjoint.shape[1:], jnp.float32)
    coefs_shape = jax.ShapeDtypeStruct((rows + 2,) + adjoint.shape[3:], jnp.float32)

    def in_plane(i, by):
        return i - i % per_plane + (i + by) % per_plane

    def in_line(i, by):
        return (i + by * per_plane) % count

    far_pairs = [(i, in_line(i, 1 if i // per_plane % 2 else -1)) for i in range(count)]
    near_pairs = [(i, in_line(i, -1 if i // per_plane % 2 else 1)) for i in range(count)]
    outer_pairs = [(i, in_plane(i, 1 if i % 2 else -1)) for i in range(count)]
    inner_pairs = [(i, in_plane(i, -1 if i % 2 else 1)) for i in range(count)]

    def sent_on(far, near, outer, inner, far_first=False):
        near = lax.ppermute(near, "gz", near_pairs)
        far = lax.ppermute(far, "gz", far_pairs)
        outer = lax.ppermute(outer, "gz", outer_pairs)
        inner = lax.ppermute(inner, "gz", inner_pairs)
        return (far, near, outer, inner) if far_first else (near, far, outer, inner)

    def local(link_set, field):
        return call(functools.partial(local_kernel, rows, link_set), f"local_{link_set}", (field, links), whole, 22)

    sent = (whole, whole, one_row, one_row)
    copied = SETS * MUS * ENTRIES - (2 * MUS + 2) * ENTRIES // 8 * 8
    sending = call(
        functools.partial(begin_kernel, rows), "begin",
        tuple(pltpu.with_memory_space_constraint(a, pltpu.HBM) for a in (adjoint, links)), sent, 5, pltpu.HBM,
        [
            pltpu.VMEM(adjoint.shape, jnp.float32),
            pltpu.VMEM((rows, copied, flowed.shape[-1]), jnp.float32),
            pltpu.SemaphoreType.DMA((rows + 1,)),
        ],
    )
    arrived = sent_on(*sending, far_first=True)
    coefs = call(
        functools.partial(taper_kernel, rows), "tapers", (source_slice, band_width), coefs_shape, 1, pltpu.SMEM
    )
    eps_shape = jax.ShapeDtypeStruct(adjoint.shape[3:], jnp.float32)
    eps = call(eps_kernel, "eps", (flow_steps,), eps_shape, 1, pltpu.SMEM)
    total, start = call(
        functools.partial(start_kernel, rows, 2), "start", (coefs, adjoint, links), (whole, whole), 22
    )
    third, *sending = call(
        functools.partial(third_kernel, rows), "third", (coefs, links, total) + arrived, (whole,) + sent, 10
    )
    arrived = sent_on(*sending)
    mixed, *sending, base = call(
        functools.partial(second_kernel, rows), "second", (eps, coefs, links, local(1, third)) + arrived + (start, third),
        (whole,) + sent + (whole,), 10,
    )
    arrived = sent_on(*sending)
    return call(
        functools.partial(last_kernel, rows), "last", (eps, coefs, links, local(0, mixed)) + arrived + (base,), whole, 5,
        scratch=[pltpu.VMEM(adjoint.shape, jnp.float32), pltpu.SemaphoreType.DMA((rows,))], out_space=pltpu.HBM,
    )


def solution(mesh):
    in_specs = (
        P(("cfg", "gz"), None, None, None, None),
        P(("cfg", "gz"), None, None, None, None, None, None),
        P("cfg"),
        P("cfg"),
        P("cfg"),
    )
    out_specs = P(("cfg", "gz"), None, None, None, None)
    return jax.shard_map(body, mesh=mesh, in_specs=in_specs, out_specs=out_specs, check_vma=False)
```

```python
import functools

import jax
import jax.numpy as jnp
from jax import lax
from jax.experimental import pallas as pl
from jax.experimental.pallas import tpu as pltpu
from jax.sharding import PartitionSpec as P

BAND = 32
LX = 8
SETS = 3
MUS = 4
ENTRIES = 18


def load_field(ref, row):
    return [[ref[row, c, a] for a in range(3)] for c in range(2)]


def store_field(ref, row, field):
    for c in range(2):
        for a in range(3):
            ref[row, c, a] = field[c][a]


def combine(function, *fields):
    return [[function(*(f[c][a] for f in fields)) for a in range(3)] for c in range(2)]


def links_at(links_ref, row, link_set, mu):
    return links_ref, ((row * SETS + link_set) * MUS + mu) * ENTRIES


def entry(matrices, a, b, c, shape):
    ref, base = matrices
    return jnp.broadcast_to(ref[pl.ds(base + (a * 3 + b) * 2 + c, 1), :], shape)


def transport(matrices, ahead, here):
    forward = [[None] * 3, [None] * 3]
    backward = [[None] * 3, [None] * 3]
    shape = (ahead if ahead is not None else here)[0][0].shape

    def add(total, c, a, value):
        total[c][a] = value if total[c][a] is None else total[c][a] + value

    for a in range(3):
        for b in range(3):
            real = entry(matrices, a, b, 0, shape)
            imag = entry(matrices, a, b, 1, shape)
            if ahead is not None:
                add(forward, 0, a, real * ahead[0][b] - imag * ahead[1][b])
                add(forward, 1, a, real * ahead[1][b] + imag * ahead[0][b])
            if here is not None:
                add(backward, 0, b, real * here[0][a] + imag * here[1][a])
                add(backward, 1, b, real * here[1][a] - imag * here[0][a])
    return forward, backward


def roll(plane, by):
    return pltpu.roll(plane, by % plane.shape[-1], plane.ndim - 1)


def place(rows):
    first = lax.axis_index("gz") * rows
    plane, first_pos = first // BAND, lax.rem(first, BAND)
    return plane, first_pos, lax.rem(plane, 2) == 1, lax.rem(first_pos // rows, 2) == 1


def taper_kernel(rows, source_ref, width_ref, coefs_ref):
    _, first_pos, _, _ = place(rows)
    ones = jnp.ones((8, 128), jnp.float32)
    per_width = ones * width_ref[0].astype(jnp.float32)
    for i in range(rows + 2):
        distance = ones * (first_pos + i - 1 - source_ref[0]).astype(jnp.float32) / per_width
        coefs_ref[i] = 1.0 / (1.0 + distance * distance)


def eps_kernel(steps_ref, eps_ref):
    eps_ref[...] = 0.25 / (jnp.ones((8, 128), jnp.float32) * steps_ref[0].astype(jnp.float32))


def store_z(rows, matrices, row, field, far_ref, near_ref):
    _, _, odd_plane, _ = place(rows)
    _, up = transport(matrices, None, field)
    store_field(far_ref, row, combine(lambda v, h: jnp.where(odd_plane, h, v), field, up))
    store_field(near_ref, row, combine(lambda v, h: jnp.where(odd_plane, v, h), field, up))


def store_t(rows, matrices, field_ref, outer_ref, inner_ref):
    _, _, _, odd_block = place(rows)
    first = load_field(field_ref, 0)
    _, last = transport(matrices, None, load_field(field_ref, rows - 1))
    store_field(outer_ref, 0, combine(lambda p, q: jnp.where(odd_block, q, p), first, last))
    store_field(inner_ref, 0, combine(lambda p, q: jnp.where(odd_block, p, q), first, last))


def begin_kernel(
    rows, adjoint_hbm, links_hbm, far_ref, near_ref, outer_ref, inner_ref, adjoint_ref, links_ref, sems
):
    row_entries = SETS * MUS * ENTRIES
    z_first = (2 * MUS + 2) * ENTRIES
    aligned = z_first // 8 * 8
    copies = [pltpu.make_async_copy(adjoint_hbm, adjoint_ref, sems.at[rows])]
    for row in range(rows):
        part = links_hbm.at[pl.ds(row * row_entries + aligned, row_entries - aligned), :]
        copies.append(pltpu.make_async_copy(part, links_ref.at[row], sems.at[row]))
    for copy in copies:
        copy.start()
    for copy in copies:
        copy.wait()
    for row in range(rows):
        matrices = links_ref.at[row], z_first - aligned
        store_z(rows, matrices, row, load_field(adjoint_ref, row), far_ref, near_ref)
    store_t(rows, (links_ref.at[rows - 1], z_first + ENTRIES - aligned), adjoint_ref, outer_ref, inner_ref)


def start_kernel(rows, link_set, coefs_ref, adjoint_ref, links_ref, sum_ref, start_ref):
    for row in range(rows):
        inside = coefs_ref[row + 1]
        store_field(start_ref, row, combine(lambda v: inside * v, load_field(adjoint_ref, row)))
    local_kernel(rows, link_set, start_ref, links_ref, sum_ref)


def local_kernel(rows, link_set, field_ref, links_ref, sum_ref):
    shape = field_ref.shape[-2:]
    x_pos = lax.broadcasted_iota(jnp.int32, shape, 1) % LX
    at_last = x_pos == LX - 1
    at_first = x_pos == 0

    for row in range(rows):
        here = load_field(field_ref, row)
        ahead = combine(lambda v: jnp.where(at_last, roll(v, LX - 1), roll(v, -1)), here)
        ahead_x, hop = transport(links_at(links_ref, row, link_set, 0), ahead, here)
        total = combine(
            lambda v, f, h: f + jnp.where(at_first, roll(h, 1 - LX), roll(h, 1)) - 8.0 * v, here, ahead_x, hop
        )
        ahead = combine(lambda v: roll(v, -LX), here)
        ahead_y, hop = transport(links_at(links_ref, row, link_set, 1), ahead, here)
        total = combine(lambda s, f, h: s + f + roll(h, LX), total, ahead_y, hop)
        if row > 0:
            total = combine(lambda s, h: s + h, total, earlier)
        if row < rows - 1:
            ahead_t, earlier = transport(links_at(links_ref, row, link_set, 3), load_field(field_ref, row + 1), here)
            total = combine(lambda s, f: s + f, total, ahead_t)
        store_field(sum_ref, row, total)


def arrived_sum(links_ref, link_set, row, rows, arrivals, coefs_ref=None):
    sum_ref, near_ref, far_ref, outer_ref, inner_ref = arrivals
    _, first_pos, odd_plane, odd_block = place(rows)
    far, near = load_field(far_ref, row), load_field(near_ref, row)
    if coefs_ref is not None:
        far, near = (combine(lambda v: coefs_ref[row + 1] * v, f) for f in (far, near))
    above = combine(lambda p, q: jnp.where(odd_plane, p, q), far, near)
    ahead_z, _ = transport(links_at(links_ref, row, link_set, 2), above, None)
    total = combine(
        lambda s, f, p, q: s + f + jnp.where(odd_plane, q, p), load_field(sum_ref, row), ahead_z, far, near
    )
    outer, inner = load_field(outer_ref, 0), load_field(inner_ref, 0)
    if row == 0:
        exists = jnp.where(first_pos != 0, 1.0, 0.0)
        if coefs_ref is not None:
            exists = exists * coefs_ref[0]
        total = combine(lambda s, p, q: s + exists * jnp.where(odd_block, q, p), total, outer, inner)
    if row == rows - 1:
        exists = jnp.where(first_pos != BAND - rows, 1.0, 0.0)
        if coefs_ref is not None:
            exists = exists * coefs_ref[rows + 1]
        later = combine(lambda p, q: exists * jnp.where(odd_block, p, q), outer, inner)
        ahead_t, _ = transport(links_at(links_ref, row, link_set, 3), later, None)
        total = combine(lambda s, f: s + f, total, ahead_t)
    return total


def third_kernel(rows, coefs_ref, links_ref, *refs):
    arrivals, (third_ref, far_ref, near_ref, outer_ref, inner_ref) = refs[:5], refs[5:]
    for row in range(rows):
        inside = coefs_ref[row + 1]
        total = arrived_sum(links_ref, 2, row, rows, arrivals, coefs_ref)
        third = combine(lambda s: 0.75 * (inside * s), total)
        store_field(third_ref, row, third)
        store_z(rows, links_at(links_ref, row, 1, 2), row, third, far_ref, near_ref)
    store_t(rows, links_at(links_ref, rows - 1, 1, 3), third_ref, outer_ref, inner_ref)


def second_kernel(rows, eps_ref, coefs_ref, links_ref, *refs):
    arrivals, (start_ref, third_ref, mixed_ref, far_ref, near_ref, outer_ref, inner_ref, base_ref) = refs[:5], refs[5:]
    eps = eps_ref[...]
    for row in range(rows):
        inside = coefs_ref[row + 1]
        total = arrived_sum(links_ref, 1, row, rows, arrivals)
        third = combine(lambda v: eps * v, load_field(third_ref, row))
        second = combine(
            lambda v, s: v + (8.0 / 9.0) * (inside * (eps * (eps * s))), load_field(start_ref, row), total
        )
        mixed = combine(lambda p, q: 0.25 * p - (2.0 / 9.0) * q, second, third)
        store_field(mixed_ref, row, mixed)
        store_field(base_ref, row, combine(lambda p, q: p + q, second, third))
        store_z(rows, links_at(links_ref, row, 0, 2), row, mixed, far_ref, near_ref)
    store_t(rows, links_at(links_ref, rows - 1, 0, 3), mixed_ref, outer_ref, inner_ref)


def last_kernel(rows, eps_ref, coefs_ref, links_ref, *refs):
    arrivals, (base_ref, out_hbm, out_ref, sems) = refs[:5], refs[5:]
    copies = []
    for row in range(rows):
        inside, eps = coefs_ref[row + 1], eps_ref[...]
        total = arrived_sum(links_ref, 0, row, rows, arrivals)
        store_field(out_ref, row, combine(lambda p, s: p + inside * (eps * s), load_field(base_ref, row), total))
        copies.append(pltpu.make_async_copy(out_ref.at[row], out_hbm.at[row], sems.at[row]))
        copies[-1].start()
    for copy in copies:
        copy.wait()


def call(kernel, name, operands, out_shapes, matvecs, space=pltpu.VMEM, scratch=(), out_space=pltpu.VMEM):
    out_spec = pl.BlockSpec(memory_space=out_space)
    return pl.pallas_call(
        kernel,
        name=name,
        out_shape=out_shapes,
        in_specs=[pl.BlockSpec(memory_space=space)] * len(operands),
        out_specs=jax.tree.map(lambda _: out_spec, out_shapes),
        scratch_shapes=scratch,
        cost_estimate=pl.CostEstimate(flops=matvecs * 72 * 1024, bytes_accessed=4096 * 18 * matvecs, transcendentals=0),
        compiler_params=pltpu.CompilerParams(vmem_limit_bytes=16 * 2**20),
    )(*operands)


def body(adjoint, flowed, source_slice, band_width, flow_steps):
    rows = adjoint.shape[0]
    per_plane = BAND // rows
    count = lax.axis_size("gz")
    links = jnp.transpose(flowed, (0, 1, 2, 4, 5, 3, 6)).reshape(-1, flowed.shape[-1])
    whole = jax.ShapeDtypeStruct(adjoint.shape, jnp.float32)
    one_row = jax.ShapeDtypeStruct((1,) + adjoint.shape[1:], jnp.float32)
    coefs_shape = jax.ShapeDtypeStruct((rows + 2,) + adjoint.shape[3:], jnp.float32)

    def in_plane(i, by):
        return i - i % per_plane + (i + by) % per_plane

    def in_line(i, by):
        return (i + by * per_plane) % count

    far_pairs = [(i, in_line(i, 1 if i // per_plane % 2 else -1)) for i in range(count)]
    near_pairs = [(i, in_line(i, -1 if i // per_plane % 2 else 1)) for i in range(count)]

    def outer_partner(i):
        block = i % per_plane
        if block in (0, per_plane - 1):
            return in_line(i, -1 if i // per_plane % 2 else 1)
        return in_plane(i, 1 if block % 2 else -1)

    outer_pairs = [(i, outer_partner(i)) for i in range(count)]
    inner_pairs = [(i, in_plane(i, -1 if i % 2 else 1)) for i in range(count)]

    def sent_on(far, near, outer, inner):
        near = lax.ppermute(near, "gz", near_pairs)
        far = lax.ppermute(far, "gz", far_pairs)
        outer = lax.ppermute(outer, "gz", outer_pairs)
        inner = lax.ppermute(inner, "gz", inner_pairs)
        return near, far, outer, inner

    def local(link_set, field):
        return call(functools.partial(local_kernel, rows, link_set), f"local_{link_set}", (field, links), whole, 22)

    sent = (whole, whole, one_row, one_row)
    copied = SETS * MUS * ENTRIES - (2 * MUS + 2) * ENTRIES // 8 * 8
    sending = call(
        functools.partial(begin_kernel, rows), "begin",
        tuple(pltpu.with_memory_space_constraint(a, pltpu.HBM) for a in (adjoint, links)), sent, 5, pltpu.HBM,
        [
            pltpu.VMEM(adjoint.shape, jnp.float32),
            pltpu.VMEM((rows, copied, flowed.shape[-1]), jnp.float32),
            pltpu.SemaphoreType.DMA((rows + 1,)),
        ],
    )
    arrived = sent_on(*sending)
    coefs = call(
        functools.partial(taper_kernel, rows), "tapers", (source_slice, band_width), coefs_shape, 1, pltpu.SMEM
    )
    eps_shape = jax.ShapeDtypeStruct(adjoint.shape[3:], jnp.float32)
    eps = call(eps_kernel, "eps", (flow_steps,), eps_shape, 1, pltpu.SMEM)
    total, start = call(
        functools.partial(start_kernel, rows, 2), "start", (coefs, adjoint, links), (whole, whole), 22
    )
    third, *sending = call(
        functools.partial(third_kernel, rows), "third", (coefs, links, total) + arrived, (whole,) + sent, 10
    )
    arrived = sent_on(*sending)
    mixed, *sending, base = call(
        functools.partial(second_kernel, rows), "second", (eps, coefs, links, local(1, third)) + arrived + (start, third),
        (whole,) + sent + (whole,), 10,
    )
    arrived = sent_on(*sending)
    return call(
        functools.partial(last_kernel, rows), "last", (eps, coefs, links, local(0, mixed)) + arrived + (base,), whole, 5,
        scratch=[pltpu.VMEM(adjoint.shape, jnp.float32), pltpu.SemaphoreType.DMA((rows,))], out_space=pltpu.HBM,
    )


def solution(mesh):
    in_specs = (
        P(("cfg", "gz"), None, None, None, None),
        P(("cfg", "gz"), None, None, None, None, None, None),
        P("cfg"),
        P("cfg"),
        P("cfg"),
    )
    out_specs = P(("cfg", "gz"), None, None, None, None)
    return jax.shard_map(body, mesh=mesh, in_specs=in_specs, out_specs=out_specs, check_vma=False)
```

```python
import functools

import jax
import jax.numpy as jnp
from jax import lax
from jax.experimental import pallas as pl
from jax.experimental.pallas import tpu as pltpu
from jax.sharding import PartitionSpec as P

BAND = 32
LX = 8
SETS = 3
MUS = 4
ENTRIES = 18


def load_field(ref, row):
    return [[ref[row, c, a] for a in range(3)] for c in range(2)]


def store_field(ref, row, field):
    for c in range(2):
        for a in range(3):
            ref[row, c, a] = field[c][a]


def combine(function, *fields):
    return [[function(*(f[c][a] for f in fields)) for a in range(3)] for c in range(2)]


def links_at(links_ref, row, link_set, mu):
    return links_ref, ((row * SETS + link_set) * MUS + mu) * ENTRIES


def entry(matrices, a, b, c, shape):
    ref, base = matrices
    return jnp.broadcast_to(ref[pl.ds(base + (a * 3 + b) * 2 + c, 1), :], shape)


def transport(matrices, ahead, here):
    forward = [[None] * 3, [None] * 3]
    backward = [[None] * 3, [None] * 3]
    shape = (ahead if ahead is not None else here)[0][0].shape

    def add(total, c, a, value):
        total[c][a] = value if total[c][a] is None else total[c][a] + value

    for a in range(3):
        for b in range(3):
            real = entry(matrices, a, b, 0, shape)
            imag = entry(matrices, a, b, 1, shape)
            if ahead is not None:
                add(forward, 0, a, real * ahead[0][b] - imag * ahead[1][b])
                add(forward, 1, a, real * ahead[1][b] + imag * ahead[0][b])
            if here is not None:
                add(backward, 0, b, real * here[0][a] + imag * here[1][a])
                add(backward, 1, b, real * here[1][a] - imag * here[0][a])
    return forward, backward


def roll(plane, by):
    return pltpu.roll(plane, by % plane.shape[-1], plane.ndim - 1)


def place(rows):
    first = lax.axis_index("gz") * rows
    plane, first_pos = first // BAND, lax.rem(first, BAND)
    return plane, first_pos, lax.rem(plane, 2) == 1, lax.rem(first_pos // rows, 2) == 1


def taper_kernel(rows, source_ref, width_ref, coefs_ref):
    _, first_pos, _, _ = place(rows)
    ones = jnp.ones((8, 128), jnp.float32)
    per_width = ones * width_ref[0].astype(jnp.float32)
    for i in range(rows + 2):
        distance = ones * (first_pos + i - 1 - source_ref[0]).astype(jnp.float32) / per_width
        coefs_ref[i] = 1.0 / (1.0 + distance * distance)


def eps_kernel(steps_ref, eps_ref):
    eps_ref[...] = 0.25 / (jnp.ones((8, 128), jnp.float32) * steps_ref[0].astype(jnp.float32))


def store_z(rows, matrices, row, field, far_ref, near_ref):
    _, _, odd_plane, _ = place(rows)
    _, up = transport(matrices, None, field)
    store_field(far_ref, row, combine(lambda v, h: jnp.where(odd_plane, h, v), field, up))
    store_field(near_ref, row, combine(lambda v, h: jnp.where(odd_plane, v, h), field, up))


def store_t(rows, matrices, field_ref, outer_ref, inner_ref):
    _, _, _, odd_block = place(rows)
    first = load_field(field_ref, 0)
    _, last = transport(matrices, None, load_field(field_ref, rows - 1))
    store_field(outer_ref, 0, combine(lambda p, q: jnp.where(odd_block, q, p), first, last))
    store_field(inner_ref, 0, combine(lambda p, q: jnp.where(odd_block, p, q), first, last))


def begin_kernel(
    rows, adjoint_hbm, links_hbm, far_ref, near_ref, outer_ref, inner_ref, adjoint_ref, links_ref, sems
):
    row_entries = SETS * MUS * ENTRIES
    z_first = (2 * MUS + 2) * ENTRIES
    aligned = z_first // 8 * 8
    copies = [pltpu.make_async_copy(adjoint_hbm, adjoint_ref, sems.at[rows])]
    for row in range(rows):
        part = links_hbm.at[pl.ds(row * row_entries + aligned, row_entries - aligned), :]
        copies.append(pltpu.make_async_copy(part, links_ref.at[row], sems.at[row]))
    for copy in copies:
        copy.start()
    for copy in copies:
        copy.wait()
    for row in range(rows):
        matrices = links_ref.at[row], z_first - aligned
        store_z(rows, matrices, row, load_field(adjoint_ref, row), far_ref, near_ref)
    store_t(rows, (links_ref.at[rows - 1], z_first + ENTRIES - aligned), adjoint_ref, outer_ref, inner_ref)


def start_kernel(rows, link_set, coefs_ref, adjoint_ref, links_ref, sum_ref, start_ref):
    for row in range(rows):
        inside = coefs_ref[row + 1]
        store_field(start_ref, row, combine(lambda v: inside * v, load_field(adjoint_ref, row)))
    local_kernel(rows, link_set, start_ref, links_ref, sum_ref)


def local_kernel(rows, link_set, field_ref, links_ref, sum_ref):
    shape = field_ref.shape[-2:]
    x_pos = lax.broadcasted_iota(jnp.int32, shape, 1) % LX
    at_last = x_pos == LX - 1
    at_first = x_pos == 0

    for row in range(rows):
        here = load_field(field_ref, row)
        ahead = combine(lambda v: jnp.where(at_last, roll(v, LX - 1), roll(v, -1)), here)
        ahead_x, hop = transport(links_at(links_ref, row, link_set, 0), ahead, here)
        total = combine(
            lambda v, f, h: f + jnp.where(at_first, roll(h, 1 - LX), roll(h, 1)) - 8.0 * v, here, ahead_x, hop
        )
        ahead = combine(lambda v: roll(v, -LX), here)
        ahead_y, hop = transport(links_at(links_ref, row, link_set, 1), ahead, here)
        total = combine(lambda s, f, h: s + f + roll(h, LX), total, ahead_y, hop)
        if row > 0:
            total = combine(lambda s, h: s + h, total, earlier)
        if row < rows - 1:
            ahead_t, earlier = transport(links_at(links_ref, row, link_set, 3), load_field(field_ref, row + 1), here)
            total = combine(lambda s, f: s + f, total, ahead_t)
        store_field(sum_ref, row, total)


def arrived_sum(links_ref, link_set, row, rows, arrivals, coefs_ref=None):
    sum_ref, near_ref, far_ref, outer_ref, inner_ref = arrivals
    if coefs_ref is None:
        near_ref, far_ref = far_ref, near_ref
    _, first_pos, odd_plane, odd_block = place(rows)
    far, near = load_field(far_ref, row), load_field(near_ref, row)
    if coefs_ref is not None:
        far, near = (combine(lambda v: coefs_ref[row + 1] * v, f) for f in (far, near))
    above = combine(lambda p, q: jnp.where(odd_plane, p, q), far, near)
    ahead_z, _ = transport(links_at(links_ref, row, link_set, 2), above, None)
    total = combine(
        lambda s, f, p, q: s + f + jnp.where(odd_plane, q, p), load_field(sum_ref, row), ahead_z, far, near
    )
    outer, inner = load_field(outer_ref, 0), load_field(inner_ref, 0)
    if row == 0:
        exists = jnp.where(first_pos != 0, 1.0, 0.0)
        if coefs_ref is not None:
            exists = exists * coefs_ref[0]
        total = combine(lambda s, p, q: s + exists * jnp.where(odd_block, q, p), total, outer, inner)
    if row == rows - 1:
        exists = jnp.where(first_pos != BAND - rows, 1.0, 0.0)
        if coefs_ref is not None:
            exists = exists * coefs_ref[rows + 1]
        later = combine(lambda p, q: exists * jnp.where(odd_block, p, q), outer, inner)
        ahead_t, _ = transport(links_at(links_ref, row, link_set, 3), later, None)
        total = combine(lambda s, f: s + f, total, ahead_t)
    return total


def third_kernel(rows, coefs_ref, links_ref, *refs):
    arrivals, (third_ref, far_ref, near_ref, outer_ref, inner_ref) = refs[:5], refs[5:]
    for row in range(rows):
        inside = coefs_ref[row + 1]
        total = arrived_sum(links_ref, 2, row, rows, arrivals, coefs_ref)
        third = combine(lambda s: 0.75 * (inside * s), total)
        store_field(third_ref, row, third)
        store_z(rows, links_at(links_ref, row, 1, 2), row, third, far_ref, near_ref)
    store_t(rows, links_at(links_ref, rows - 1, 1, 3), third_ref, outer_ref, inner_ref)


def second_kernel(rows, eps_ref, coefs_ref, links_ref, *refs):
    arrivals, (start_ref, third_ref, mixed_ref, far_ref, near_ref, outer_ref, inner_ref, base_ref) = refs[:5], refs[5:]
    eps = eps_ref[...]
    for row in range(rows):
        inside = coefs_ref[row + 1]
        total = arrived_sum(links_ref, 1, row, rows, arrivals)
        third = combine(lambda v: eps * v, load_field(third_ref, row))
        second = combine(
            lambda v, s: v + (8.0 / 9.0) * (inside * (eps * (eps * s))), load_field(start_ref, row), total
        )
        mixed = combine(lambda p, q: 0.25 * p - (2.0 / 9.0) * q, second, third)
        store_field(mixed_ref, row, mixed)
        store_field(base_ref, row, combine(lambda p, q: p + q, second, third))
        store_z(rows, links_at(links_ref, row, 0, 2), row, mixed, far_ref, near_ref)
    store_t(rows, links_at(links_ref, rows - 1, 0, 3), mixed_ref, outer_ref, inner_ref)


def last_kernel(rows, eps_ref, coefs_ref, links_ref, *refs):
    arrivals, (base_ref, out_hbm, out_ref, sems) = refs[:5], refs[5:]
    copies = []
    for row in range(rows):
        inside, eps = coefs_ref[row + 1], eps_ref[...]
        total = arrived_sum(links_ref, 0, row, rows, arrivals)
        store_field(out_ref, row, combine(lambda p, s: p + inside * (eps * s), load_field(base_ref, row), total))
        copies.append(pltpu.make_async_copy(out_ref.at[row], out_hbm.at[row], sems.at[row]))
        copies[-1].start()
    for copy in copies:
        copy.wait()


def call(kernel, name, operands, out_shapes, matvecs, space=pltpu.VMEM, scratch=(), out_space=pltpu.VMEM):
    out_spec = pl.BlockSpec(memory_space=out_space)
    return pl.pallas_call(
        kernel,
        name=name,
        out_shape=out_shapes,
        in_specs=[pl.BlockSpec(memory_space=space)] * len(operands),
        out_specs=jax.tree.map(lambda _: out_spec, out_shapes),
        scratch_shapes=scratch,
        cost_estimate=pl.CostEstimate(flops=matvecs * 72 * 1024, bytes_accessed=4096 * 18 * matvecs, transcendentals=0),
        compiler_params=pltpu.CompilerParams(vmem_limit_bytes=16 * 2**20),
    )(*operands)


def body(adjoint, flowed, source_slice, band_width, flow_steps):
    rows = adjoint.shape[0]
    per_plane = BAND // rows
    count = lax.axis_size("gz")
    links = jnp.transpose(flowed, (0, 1, 2, 4, 5, 3, 6)).reshape(-1, flowed.shape[-1])
    whole = jax.ShapeDtypeStruct(adjoint.shape, jnp.float32)
    one_row = jax.ShapeDtypeStruct((1,) + adjoint.shape[1:], jnp.float32)
    coefs_shape = jax.ShapeDtypeStruct((rows + 2,) + adjoint.shape[3:], jnp.float32)

    def in_plane(i, by):
        return i - i % per_plane + (i + by) % per_plane

    def in_line(i, by):
        return (i + by * per_plane) % count

    far_pairs = [(i, in_line(i, 1 if i // per_plane % 2 else -1)) for i in range(count)]
    near_pairs = [(i, in_line(i, -1 if i // per_plane % 2 else 1)) for i in range(count)]
    outer_pairs = [(i, in_plane(i, 1 if i % 2 else -1)) for i in range(count)]
    inner_pairs = [(i, in_plane(i, -1 if i % 2 else 1)) for i in range(count)]

    def sent_on(far, near, outer, inner, far_first=True):
        near = lax.ppermute(near, "gz", near_pairs)
        far = lax.ppermute(far, "gz", far_pairs)
        outer = lax.ppermute(outer, "gz", outer_pairs)
        inner = lax.ppermute(inner, "gz", inner_pairs)
        return (far, near, outer, inner) if far_first else (near, far, outer, inner)

    def local(link_set, field):
        return call(functools.partial(local_kernel, rows, link_set), f"local_{link_set}", (field, links), whole, 22)

    sent = (whole, whole, one_row, one_row)
    copied = SETS * MUS * ENTRIES - (2 * MUS + 2) * ENTRIES // 8 * 8
    sending = call(
        functools.partial(begin_kernel, rows), "begin",
        tuple(pltpu.with_memory_space_constraint(a, pltpu.HBM) for a in (adjoint, links)), sent, 5, pltpu.HBM,
        [
            pltpu.VMEM(adjoint.shape, jnp.float32),
            pltpu.VMEM((rows, copied, flowed.shape[-1]), jnp.float32),
            pltpu.SemaphoreType.DMA((rows + 1,)),
        ],
    )
    arrived = sent_on(*sending, far_first=False)
    coefs = call(
        functools.partial(taper_kernel, rows), "tapers", (source_slice, band_width), coefs_shape, 1, pltpu.SMEM
    )
    eps_shape = jax.ShapeDtypeStruct(adjoint.shape[3:], jnp.float32)
    eps = call(eps_kernel, "eps", (flow_steps,), eps_shape, 1, pltpu.SMEM)
    total, start = call(
        functools.partial(start_kernel, rows, 2), "start", (coefs, adjoint, links), (whole, whole), 22
    )
    third, *sending = call(
        functools.partial(third_kernel, rows), "third", (coefs, links, total) + arrived, (whole,) + sent, 10
    )
    arrived = sent_on(*sending)
    mixed, *sending, base = call(
        functools.partial(second_kernel, rows), "second", (eps, coefs, links, local(1, third)) + arrived + (start, third),
        (whole,) + sent + (whole,), 10,
    )
    arrived = sent_on(*sending)
    return call(
        functools.partial(last_kernel, rows), "last", (eps, coefs, links, local(0, mixed)) + arrived + (base,), whole, 5,
        scratch=[pltpu.VMEM(adjoint.shape, jnp.float32), pltpu.SemaphoreType.DMA((rows,))], out_space=pltpu.HBM,
    )


def solution(mesh):
    in_specs = (
        P(("cfg", "gz"), None, None, None, None),
        P(("cfg", "gz"), None, None, None, None, None, None),
        P("cfg"),
        P("cfg"),
        P("cfg"),
    )
    out_specs = P(("cfg", "gz"), None, None, None, None)
    return jax.shard_map(body, mesh=mesh, in_specs=in_specs, out_specs=out_specs, check_vma=False)
```

```python
import functools

import jax
import jax.numpy as jnp
from jax import lax
from jax.experimental import pallas as pl
from jax.experimental.pallas import tpu as pltpu
from jax.sharding import PartitionSpec as P

BAND = 32
LX = 8
SETS = 3
MUS = 4
ENTRIES = 18


def load_field(ref, row):
    return [[ref[row, c, a] for a in range(3)] for c in range(2)]


def store_field(ref, row, field):
    for c in range(2):
        for a in range(3):
            ref[row, c, a] = field[c][a]


def combine(function, *fields):
    return [[function(*(f[c][a] for f in fields)) for a in range(3)] for c in range(2)]


def links_at(links_ref, row, link_set, mu):
    return links_ref, ((row * SETS + link_set) * MUS + mu) * ENTRIES


def entry(matrices, a, b, c, shape):
    ref, base = matrices
    return jnp.broadcast_to(ref[pl.ds(base + (a * 3 + b) * 2 + c, 1), :], shape)


def transport(matrices, ahead, here):
    forward = [[None] * 3, [None] * 3]
    backward = [[None] * 3, [None] * 3]
    shape = (ahead if ahead is not None else here)[0][0].shape

    def add(total, c, a, value):
        total[c][a] = value if total[c][a] is None else total[c][a] + value

    for a in range(3):
        for b in range(3):
            real = entry(matrices, a, b, 0, shape)
            imag = entry(matrices, a, b, 1, shape)
            if ahead is not None:
                add(forward, 0, a, real * ahead[0][b] - imag * ahead[1][b])
                add(forward, 1, a, real * ahead[1][b] + imag * ahead[0][b])
            if here is not None:
                add(backward, 0, b, real * here[0][a] + imag * here[1][a])
                add(backward, 1, b, real * here[1][a] - imag * here[0][a])
    return forward, backward


def roll(plane, by):
    return pltpu.roll(plane, by % plane.shape[-1], plane.ndim - 1)


def place(rows):
    first = lax.axis_index("gz") * rows
    plane, first_pos = first // BAND, lax.rem(first, BAND)
    return plane, first_pos, lax.rem(plane, 2) == 1, lax.rem(first_pos // rows, 2) == 1


def taper_kernel(rows, source_ref, width_ref, coefs_ref):
    _, first_pos, _, _ = place(rows)
    ones = jnp.ones((8, 128), jnp.float32)
    per_width = ones * width_ref[0].astype(jnp.float32)
    for i in range(rows + 2):
        distance = ones * (first_pos + i - 1 - source_ref[0]).astype(jnp.float32) / per_width
        coefs_ref[i] = 1.0 / (1.0 + distance * distance)


def eps_kernel(steps_ref, eps_ref):
    eps_ref[...] = 0.25 / (jnp.ones((8, 128), jnp.float32) * steps_ref[0].astype(jnp.float32))


def store_z(rows, matrices, row, field, far_ref, near_ref):
    _, _, odd_plane, _ = place(rows)
    _, up = transport(matrices, None, field)
    store_field(far_ref, row, combine(lambda v, h: jnp.where(odd_plane, h, v), field, up))
    store_field(near_ref, row, combine(lambda v, h: jnp.where(odd_plane, v, h), field, up))


def store_t(rows, matrices, field_ref, outer_ref, inner_ref):
    _, _, _, odd_block = place(rows)
    first = load_field(field_ref, 0)
    _, last = transport(matrices, None, load_field(field_ref, rows - 1))
    store_field(outer_ref, 0, combine(lambda p, q: jnp.where(odd_block, q, p), first, last))
    store_field(inner_ref, 0, combine(lambda p, q: jnp.where(odd_block, p, q), first, last))


def begin_kernel(
    rows, adjoint_hbm, links_hbm, far_ref, near_ref, outer_ref, inner_ref, adjoint_ref, links_ref, sems
):
    row_entries = SETS * MUS * ENTRIES
    z_first = (2 * MUS + 2) * ENTRIES
    aligned = z_first // 8 * 8
    copies = [pltpu.make_async_copy(adjoint_hbm, adjoint_ref, sems.at[rows])]
    for row in range(rows):
        part = links_hbm.at[pl.ds(row * row_entries + aligned, row_entries - aligned), :]
        copies.append(pltpu.make_async_copy(part, links_ref.at[row], sems.at[row]))
    for copy in copies:
        copy.start()
    for copy in copies:
        copy.wait()
    for row in range(rows):
        matrices = links_ref.at[row], z_first - aligned
        store_z(rows, matrices, row, load_field(adjoint_ref, row), far_ref, near_ref)
    store_t(rows, (links_ref.at[rows - 1], z_first + ENTRIES - aligned), adjoint_ref, outer_ref, inner_ref)


def start_kernel(rows, link_set, coefs_ref, adjoint_ref, links_ref, sum_ref, start_ref):
    for row in range(rows):
        inside = coefs_ref[row + 1]
        store_field(start_ref, row, combine(lambda v: inside * v, load_field(adjoint_ref, row)))
    local_kernel(rows, link_set, start_ref, links_ref, sum_ref)


def local_kernel(rows, link_set, field_ref, links_ref, sum_ref):
    shape = field_ref.shape[-2:]
    x_pos = lax.broadcasted_iota(jnp.int32, shape, 1) % LX
    at_last = x_pos == LX - 1
    at_first = x_pos == 0

    for row in range(rows):
        here = load_field(field_ref, row)
        ahead = combine(lambda v: jnp.where(at_last, roll(v, LX - 1), roll(v, -1)), here)
        ahead_x, hop = transport(links_at(links_ref, row, link_set, 0), ahead, here)
        total = combine(
            lambda v, f, h: f + jnp.where(at_first, roll(h, 1 - LX), roll(h, 1)) - 8.0 * v, here, ahead_x, hop
        )
        ahead = combine(lambda v: roll(v, -LX), here)
        ahead_y, hop = transport(links_at(links_ref, row, link_set, 1), ahead, here)
        total = combine(lambda s, f, h: s + f + roll(h, LX), total, ahead_y, hop)
        if row > 0:
            total = combine(lambda s, h: s + h, total, earlier)
        if row < rows - 1:
            ahead_t, earlier = transport(links_at(links_ref, row, link_set, 3), load_field(field_ref, row + 1), here)
            total = combine(lambda s, f: s + f, total, ahead_t)
        store_field(sum_ref, row, total)


def arrived_sum(links_ref, link_set, row, rows, arrivals, coefs_ref=None):
    sum_ref, near_ref, far_ref, outer_ref, inner_ref = arrivals
    if link_set == 1:
        near_ref, far_ref = far_ref, near_ref
    _, first_pos, odd_plane, odd_block = place(rows)
    far, near = load_field(far_ref, row), load_field(near_ref, row)
    if coefs_ref is not None:
        far, near = (combine(lambda v: coefs_ref[row + 1] * v, f) for f in (far, near))
    above = combine(lambda p, q: jnp.where(odd_plane, p, q), far, near)
    ahead_z, _ = transport(links_at(links_ref, row, link_set, 2), above, None)
    total = combine(
        lambda s, f, p, q: s + f + jnp.where(odd_plane, q, p), load_field(sum_ref, row), ahead_z, far, near
    )
    outer, inner = load_field(outer_ref, 0), load_field(inner_ref, 0)
    if row == 0:
        exists = jnp.where(first_pos != 0, 1.0, 0.0)
        if coefs_ref is not None:
            exists = exists * coefs_ref[0]
        total = combine(lambda s, p, q: s + exists * jnp.where(odd_block, q, p), total, outer, inner)
    if row == rows - 1:
        exists = jnp.where(first_pos != BAND - rows, 1.0, 0.0)
        if coefs_ref is not None:
            exists = exists * coefs_ref[rows + 1]
        later = combine(lambda p, q: exists * jnp.where(odd_block, p, q), outer, inner)
        ahead_t, _ = transport(links_at(links_ref, row, link_set, 3), later, None)
        total = combine(lambda s, f: s + f, total, ahead_t)
    return total


def third_kernel(rows, coefs_ref, links_ref, *refs):
    arrivals, (third_ref, far_ref, near_ref, outer_ref, inner_ref) = refs[:5], refs[5:]
    for row in range(rows):
        inside = coefs_ref[row + 1]
        total = arrived_sum(links_ref, 2, row, rows, arrivals, coefs_ref)
        third = combine(lambda s: 0.75 * (inside * s), total)
        store_field(third_ref, row, third)
        store_z(rows, links_at(links_ref, row, 1, 2), row, third, far_ref, near_ref)
    store_t(rows, links_at(links_ref, rows - 1, 1, 3), third_ref, outer_ref, inner_ref)


def second_kernel(rows, eps_ref, coefs_ref, links_ref, *refs):
    arrivals, (start_ref, third_ref, mixed_ref, far_ref, near_ref, outer_ref, inner_ref, base_ref) = refs[:5], refs[5:]
    eps = eps_ref[...]
    for row in range(rows):
        inside = coefs_ref[row + 1]
        total = arrived_sum(links_ref, 1, row, rows, arrivals)
        third = combine(lambda v: eps * v, load_field(third_ref, row))
        second = combine(
            lambda v, s: v + (8.0 / 9.0) * (inside * (eps * (eps * s))), load_field(start_ref, row), total
        )
        mixed = combine(lambda p, q: 0.25 * p - (2.0 / 9.0) * q, second, third)
        store_field(mixed_ref, row, mixed)
        store_field(base_ref, row, combine(lambda p, q: p + q, second, third))
        store_z(rows, links_at(links_ref, row, 0, 2), row, mixed, far_ref, near_ref)
    store_t(rows, links_at(links_ref, rows - 1, 0, 3), mixed_ref, outer_ref, inner_ref)


def last_kernel(rows, eps_ref, coefs_ref, links_ref, *refs):
    arrivals, (base_ref, out_hbm, out_ref, sems) = refs[:5], refs[5:]
    copies = []
    for row in range(rows):
        inside, eps = coefs_ref[row + 1], eps_ref[...]
        total = arrived_sum(links_ref, 0, row, rows, arrivals)
        store_field(out_ref, row, combine(lambda p, s: p + inside * (eps * s), load_field(base_ref, row), total))
        copies.append(pltpu.make_async_copy(out_ref.at[row], out_hbm.at[row], sems.at[row]))
        copies[-1].start()
    for copy in copies:
        copy.wait()


def call(kernel, name, operands, out_shapes, matvecs, space=pltpu.VMEM, scratch=(), out_space=pltpu.VMEM):
    out_spec = pl.BlockSpec(memory_space=out_space)
    return pl.pallas_call(
        kernel,
        name=name,
        out_shape=out_shapes,
        in_specs=[pl.BlockSpec(memory_space=space)] * len(operands),
        out_specs=jax.tree.map(lambda _: out_spec, out_shapes),
        scratch_shapes=scratch,
        cost_estimate=pl.CostEstimate(flops=matvecs * 72 * 1024, bytes_accessed=4096 * 18 * matvecs, transcendentals=0),
        compiler_params=pltpu.CompilerParams(vmem_limit_bytes=16 * 2**20),
    )(*operands)


def body(adjoint, flowed, source_slice, band_width, flow_steps):
    rows = adjoint.shape[0]
    per_plane = BAND // rows
    count = lax.axis_size("gz")
    links = jnp.transpose(flowed, (0, 1, 2, 4, 5, 3, 6)).reshape(-1, flowed.shape[-1])
    whole = jax.ShapeDtypeStruct(adjoint.shape, jnp.float32)
    one_row = jax.ShapeDtypeStruct((1,) + adjoint.shape[1:], jnp.float32)
    coefs_shape = jax.ShapeDtypeStruct((rows + 2,) + adjoint.shape[3:], jnp.float32)

    def in_plane(i, by):
        return i - i % per_plane + (i + by) % per_plane

    def in_line(i, by):
        return (i + by * per_plane) % count

    far_pairs = [(i, in_line(i, 1 if i // per_plane % 2 else -1)) for i in range(count)]
    near_pairs = [(i, in_line(i, -1 if i // per_plane % 2 else 1)) for i in range(count)]
    outer_pairs = [(i, in_plane(i, 1 if i % 2 else -1)) for i in range(count)]
    inner_pairs = [(i, in_plane(i, -1 if i % 2 else 1)) for i in range(count)]

    def sent_on(far, near, outer, inner, far_first=False):
        near = lax.ppermute(near, "gz", near_pairs)
        far = lax.ppermute(far, "gz", far_pairs)
        outer = lax.ppermute(outer, "gz", outer_pairs)
        inner = lax.ppermute(inner, "gz", inner_pairs)
        return (far, near, outer, inner) if far_first else (near, far, outer, inner)

    def local(link_set, field):
        return call(functools.partial(local_kernel, rows, link_set), f"local_{link_set}", (field, links), whole, 22)

    sent = (whole, whole, one_row, one_row)
    copied = SETS * MUS * ENTRIES - (2 * MUS + 2) * ENTRIES // 8 * 8
    sending = call(
        functools.partial(begin_kernel, rows), "begin",
        tuple(pltpu.with_memory_space_constraint(a, pltpu.HBM) for a in (adjoint, links)), sent, 5, pltpu.HBM,
        [
            pltpu.VMEM(adjoint.shape, jnp.float32),
            pltpu.VMEM((rows, copied, flowed.shape[-1]), jnp.float32),
            pltpu.SemaphoreType.DMA((rows + 1,)),
        ],
    )
    arrived = sent_on(*sending)
    coefs = call(
        functools.partial(taper_kernel, rows), "tapers", (source_slice, band_width), coefs_shape, 1, pltpu.SMEM
    )
    eps_shape = jax.ShapeDtypeStruct(adjoint.shape[3:], jnp.float32)
    eps = call(eps_kernel, "eps", (flow_steps,), eps_shape, 1, pltpu.SMEM)
    total, start = call(
        functools.partial(start_kernel, rows, 2), "start", (coefs, adjoint, links), (whole, whole), 22
    )
    third, *sending = call(
        functools.partial(third_kernel, rows), "third", (coefs, links, total) + arrived, (whole,) + sent, 10
    )
    arrived = sent_on(*sending, far_first=True)
    mixed, *sending, base = call(
        functools.partial(second_kernel, rows), "second", (eps, coefs, links, local(1, third)) + arrived + (start, third),
        (whole,) + sent + (whole,), 10,
    )
    arrived = sent_on(*sending)
    return call(
        functools.partial(last_kernel, rows), "last", (eps, coefs, links, local(0, mixed)) + arrived + (base,), whole, 5,
        scratch=[pltpu.VMEM(adjoint.shape, jnp.float32), pltpu.SemaphoreType.DMA((rows,))], out_space=pltpu.HBM,
    )


def solution(mesh):
    in_specs = (
        P(("cfg", "gz"), None, None, None, None),
        P(("cfg", "gz"), None, None, None, None, None, None),
        P("cfg"),
        P("cfg"),
        P("cfg"),
    )
    out_specs = P(("cfg", "gz"), None, None, None, None)
    return jax.shard_map(body, mesh=mesh, in_specs=in_specs, out_specs=out_specs, check_vma=False)
```

```python
import functools

import jax
import jax.numpy as jnp
from jax import lax
from jax.experimental import pallas as pl
from jax.experimental.pallas import tpu as pltpu
from jax.sharding import PartitionSpec as P

BAND = 32
LX = 8
SETS = 3
MUS = 4
ENTRIES = 18


def load_field(ref, row):
    return [[ref[row, c, a] for a in range(3)] for c in range(2)]


def store_field(ref, row, field):
    for c in range(2):
        for a in range(3):
            ref[row, c, a] = field[c][a]


def combine(function, *fields):
    return [[function(*(f[c][a] for f in fields)) for a in range(3)] for c in range(2)]


def links_at(links_ref, row, link_set, mu):
    return links_ref, ((row * SETS + link_set) * MUS + mu) * ENTRIES


def entry(matrices, a, b, c, shape):
    ref, base = matrices
    return jnp.broadcast_to(ref[pl.ds(base + (a * 3 + b) * 2 + c, 1), :], shape)


def transport(matrices, ahead, here):
    forward = [[None] * 3, [None] * 3]
    backward = [[None] * 3, [None] * 3]
    shape = (ahead if ahead is not None else here)[0][0].shape

    def add(total, c, a, value):
        total[c][a] = value if total[c][a] is None else total[c][a] + value

    for a in range(3):
        for b in range(3):
            real = entry(matrices, a, b, 0, shape)
            imag = entry(matrices, a, b, 1, shape)
            if ahead is not None:
                add(forward, 0, a, real * ahead[0][b] - imag * ahead[1][b])
                add(forward, 1, a, real * ahead[1][b] + imag * ahead[0][b])
            if here is not None:
                add(backward, 0, b, real * here[0][a] + imag * here[1][a])
                add(backward, 1, b, real * here[1][a] - imag * here[0][a])
    return forward, backward


def roll(plane, by):
    return pltpu.roll(plane, by % plane.shape[-1], plane.ndim - 1)


def place(rows):
    first = lax.axis_index("gz") * rows
    plane, first_pos = first // BAND, lax.rem(first, BAND)
    return plane, first_pos, lax.rem(plane, 2) == 1, lax.rem(first_pos // rows, 2) == 1


def taper_kernel(rows, source_ref, width_ref, coefs_ref):
    _, first_pos, _, _ = place(rows)
    ones = jnp.ones((8, 128), jnp.float32)
    per_width = ones * width_ref[0].astype(jnp.float32)
    for i in range(rows + 2):
        distance = ones * (first_pos + i - 1 - source_ref[0]).astype(jnp.float32) / per_width
        coefs_ref[i] = 1.0 / (1.0 + distance * distance)


def eps_kernel(steps_ref, eps_ref):
    eps_ref[...] = 0.25 / (jnp.ones((8, 128), jnp.float32) * steps_ref[0].astype(jnp.float32))


def store_z(rows, matrices, row, field, far_ref, near_ref):
    _, _, odd_plane, _ = place(rows)
    _, up = transport(matrices, None, field)
    store_field(far_ref, row, combine(lambda v, h: jnp.where(odd_plane, h, v), field, up))
    store_field(near_ref, row, combine(lambda v, h: jnp.where(odd_plane, v, h), field, up))


def store_t(rows, matrices, field_ref, outer_ref, inner_ref):
    _, _, _, odd_block = place(rows)
    first = load_field(field_ref, 0)
    _, last = transport(matrices, None, load_field(field_ref, rows - 1))
    store_field(outer_ref, 0, combine(lambda p, q: jnp.where(odd_block, q, p), first, last))
    store_field(inner_ref, 0, combine(lambda p, q: jnp.where(odd_block, p, q), first, last))


def begin_kernel(
    rows, adjoint_hbm, links_hbm, far_ref, near_ref, outer_ref, inner_ref, adjoint_ref, links_ref, sems
):
    z_first = (2 * MUS + 2) * ENTRIES
    aligned = z_first // 8 * 8
    part = links_hbm.at[:, pl.ds(aligned, SETS * MUS * ENTRIES - aligned), :]
    copies = [pltpu.make_async_copy(part, links_ref, sems.at[rows])]
    for row in range(rows):
        copies.append(pltpu.make_async_copy(adjoint_hbm.at[row], adjoint_ref.at[row], sems.at[row]))
    for copy in copies:
        copy.start()
    copies[0].wait()
    for row in range(rows):
        copies[row + 1].wait()
        matrices = links_ref.at[row], z_first - aligned
        store_z(rows, matrices, row, load_field(adjoint_ref, row), far_ref, near_ref)
    store_t(rows, (links_ref.at[rows - 1], z_first + ENTRIES - aligned), adjoint_ref, outer_ref, inner_ref)


def start_kernel(rows, link_set, coefs_ref, adjoint_ref, links_ref, sum_ref, start_ref):
    for row in range(rows):
        inside = coefs_ref[row + 1]
        store_field(start_ref, row, combine(lambda v: inside * v, load_field(adjoint_ref, row)))
    local_kernel(rows, link_set, start_ref, links_ref, sum_ref)


def local_kernel(rows, link_set, field_ref, links_ref, sum_ref):
    shape = field_ref.shape[-2:]
    x_pos = lax.broadcasted_iota(jnp.int32, shape, 1) % LX
    at_last = x_pos == LX - 1
    at_first = x_pos == 0

    for row in range(rows):
        here = load_field(field_ref, row)
        ahead = combine(lambda v: jnp.where(at_last, roll(v, LX - 1), roll(v, -1)), here)
        ahead_x, hop = transport(links_at(links_ref, row, link_set, 0), ahead, here)
        total = combine(
            lambda v, f, h: f + jnp.where(at_first, roll(h, 1 - LX), roll(h, 1)) - 8.0 * v, here, ahead_x, hop
        )
        ahead = combine(lambda v: roll(v, -LX), here)
        ahead_y, hop = transport(links_at(links_ref, row, link_set, 1), ahead, here)
        total = combine(lambda s, f, h: s + f + roll(h, LX), total, ahead_y, hop)
        if row > 0:
            total = combine(lambda s, h: s + h, total, earlier)
        if row < rows - 1:
            ahead_t, earlier = transport(links_at(links_ref, row, link_set, 3), load_field(field_ref, row + 1), here)
            total = combine(lambda s, f: s + f, total, ahead_t)
        store_field(sum_ref, row, total)


def arrived_sum(links_ref, link_set, row, rows, arrivals, coefs_ref=None):
    sum_ref, near_ref, far_ref, outer_ref, inner_ref = arrivals
    _, first_pos, odd_plane, odd_block = place(rows)
    far, near = load_field(far_ref, row), load_field(near_ref, row)
    if coefs_ref is not None:
        far, near = (combine(lambda v: coefs_ref[row + 1] * v, f) for f in (far, near))
    above = combine(lambda p, q: jnp.where(odd_plane, p, q), far, near)
    ahead_z, _ = transport(links_at(links_ref, row, link_set, 2), above, None)
    total = combine(
        lambda s, f, p, q: s + f + jnp.where(odd_plane, q, p), load_field(sum_ref, row), ahead_z, far, near
    )
    outer, inner = load_field(outer_ref, 0), load_field(inner_ref, 0)
    if row == 0:
        exists = jnp.where(first_pos != 0, 1.0, 0.0)
        if coefs_ref is not None:
            exists = exists * coefs_ref[0]
        total = combine(lambda s, p, q: s + exists * jnp.where(odd_block, q, p), total, outer, inner)
    if row == rows - 1:
        exists = jnp.where(first_pos != BAND - rows, 1.0, 0.0)
        if coefs_ref is not None:
            exists = exists * coefs_ref[rows + 1]
        later = combine(lambda p, q: exists * jnp.where(odd_block, p, q), outer, inner)
        ahead_t, _ = transport(links_at(links_ref, row, link_set, 3), later, None)
        total = combine(lambda s, f: s + f, total, ahead_t)
    return total


def third_kernel(rows, coefs_ref, links_ref, *refs):
    arrivals, (third_ref, far_ref, near_ref, outer_ref, inner_ref) = refs[:5], refs[5:]
    for row in range(rows):
        inside = coefs_ref[row + 1]
        total = arrived_sum(links_ref, 2, row, rows, arrivals, coefs_ref)
        third = combine(lambda s: 0.75 * (inside * s), total)
        store_field(third_ref, row, third)
        store_z(rows, links_at(links_ref, row, 1, 2), row, third, far_ref, near_ref)
    store_t(rows, links_at(links_ref, rows - 1, 1, 3), third_ref, outer_ref, inner_ref)


def second_kernel(rows, eps_ref, coefs_ref, links_ref, *refs):
    arrivals, (start_ref, third_ref, mixed_ref, far_ref, near_ref, outer_ref, inner_ref, base_ref) = refs[:5], refs[5:]
    eps = eps_ref[...]
    for row in range(rows):
        inside = coefs_ref[row + 1]
        total = arrived_sum(links_ref, 1, row, rows, arrivals)
        third = combine(lambda v: eps * v, load_field(third_ref, row))
        second = combine(
            lambda v, s: v + (8.0 / 9.0) * (inside * (eps * (eps * s))), load_field(start_ref, row), total
        )
        mixed = combine(lambda p, q: 0.25 * p - (2.0 / 9.0) * q, second, third)
        store_field(mixed_ref, row, mixed)
        store_field(base_ref, row, combine(lambda p, q: p + q, second, third))
        store_z(rows, links_at(links_ref, row, 0, 2), row, mixed, far_ref, near_ref)
    store_t(rows, links_at(links_ref, rows - 1, 0, 3), mixed_ref, outer_ref, inner_ref)


def last_kernel(rows, eps_ref, coefs_ref, links_ref, *refs):
    arrivals, (base_ref, out_hbm, out_ref, sems) = refs[:5], refs[5:]
    copies = []
    for row in range(rows):
        inside, eps = coefs_ref[row + 1], eps_ref[...]
        total = arrived_sum(links_ref, 0, row, rows, arrivals)
        store_field(out_ref, row, combine(lambda p, s: p + inside * (eps * s), load_field(base_ref, row), total))
        copies.append(pltpu.make_async_copy(out_ref.at[row], out_hbm.at[row], sems.at[row]))
        copies[-1].start()
    for copy in copies:
        copy.wait()


def call(kernel, name, operands, out_shapes, matvecs, space=pltpu.VMEM, scratch=(), out_space=pltpu.VMEM):
    out_spec = pl.BlockSpec(memory_space=out_space)
    return pl.pallas_call(
        kernel,
        name=name,
        out_shape=out_shapes,
        in_specs=[pl.BlockSpec(memory_space=space)] * len(operands),
        out_specs=jax.tree.map(lambda _: out_spec, out_shapes),
        scratch_shapes=scratch,
        cost_estimate=pl.CostEstimate(flops=matvecs * 72 * 1024, bytes_accessed=4096 * 18 * matvecs, transcendentals=0),
        compiler_params=pltpu.CompilerParams(vmem_limit_bytes=16 * 2**20),
    )(*operands)


def body(adjoint, flowed, source_slice, band_width, flow_steps):
    rows = adjoint.shape[0]
    per_plane = BAND // rows
    count = lax.axis_size("gz")
    links = jnp.transpose(flowed, (0, 1, 2, 4, 5, 3, 6)).reshape(-1, flowed.shape[-1])
    whole = jax.ShapeDtypeStruct(adjoint.shape, jnp.float32)
    one_row = jax.ShapeDtypeStruct((1,) + adjoint.shape[1:], jnp.float32)
    coefs_shape = jax.ShapeDtypeStruct((rows + 2,) + adjoint.shape[3:], jnp.float32)

    def in_plane(i, by):
        return i - i % per_plane + (i + by) % per_plane

    def in_line(i, by):
        return (i + by * per_plane) % count

    far_pairs = [(i, in_line(i, 1 if i // per_plane % 2 else -1)) for i in range(count)]
    near_pairs = [(i, in_line(i, -1 if i // per_plane % 2 else 1)) for i in range(count)]
    outer_pairs = [(i, in_plane(i, 1 if i % 2 else -1)) for i in range(count)]
    inner_pairs = [(i, in_plane(i, -1 if i % 2 else 1)) for i in range(count)]

    def sent_on(far, near, outer, inner):
        near = lax.ppermute(near, "gz", near_pairs)
        far = lax.ppermute(far, "gz", far_pairs)
        outer = lax.ppermute(outer, "gz", outer_pairs)
        inner = lax.ppermute(inner, "gz", inner_pairs)
        return near, far, outer, inner

    def local(link_set, field):
        return call(functools.partial(local_kernel, rows, link_set), f"local_{link_set}", (field, links), whole, 22)

    sent = (whole, whole, one_row, one_row)
    copied = SETS * MUS * ENTRIES - (2 * MUS + 2) * ENTRIES // 8 * 8
    sending = call(
        functools.partial(begin_kernel, rows), "begin",
        tuple(
            pltpu.with_memory_space_constraint(a, pltpu.HBM)
            for a in (adjoint, links.reshape(rows, -1, flowed.shape[-1]))
        ), sent, 5, pltpu.HBM,
        [
            pltpu.VMEM(adjoint.shape, jnp.float32),
            pltpu.VMEM((rows, copied, flowed.shape[-1]), jnp.float32),
            pltpu.SemaphoreType.DMA((rows + 1,)),
        ],
    )
    arrived = sent_on(*sending)
    coefs = call(
        functools.partial(taper_kernel, rows), "tapers", (source_slice, band_width), coefs_shape, 1, pltpu.SMEM
    )
    eps_shape = jax.ShapeDtypeStruct(adjoint.shape[3:], jnp.float32)
    eps = call(eps_kernel, "eps", (flow_steps,), eps_shape, 1, pltpu.SMEM)
    total, start = call(
        functools.partial(start_kernel, rows, 2), "start", (coefs, adjoint, links), (whole, whole), 22
    )
    third, *sending = call(
        functools.partial(third_kernel, rows), "third", (coefs, links, total) + arrived, (whole,) + sent, 10
    )
    arrived = sent_on(*sending)
    mixed, *sending, base = call(
        functools.partial(second_kernel, rows), "second", (eps, coefs, links, local(1, third)) + arrived + (start, third),
        (whole,) + sent + (whole,), 10,
    )
    arrived = sent_on(*sending)
    return call(
        functools.partial(last_kernel, rows), "last", (eps, coefs, links, local(0, mixed)) + arrived + (base,), whole, 5,
        scratch=[pltpu.VMEM(adjoint.shape, jnp.float32), pltpu.SemaphoreType.DMA((rows,))], out_space=pltpu.HBM,
    )


def solution(mesh):
    in_specs = (
        P(("cfg", "gz"), None, None, None, None),
        P(("cfg", "gz"), None, None, None, None, None, None),
        P("cfg"),
        P("cfg"),
        P("cfg"),
    )
    out_specs = P(("cfg", "gz"), None, None, None, None)
    return jax.shard_map(body, mesh=mesh, in_specs=in_specs, out_specs=out_specs, check_vma=False)
```

```python
import functools

import jax
import jax.numpy as jnp
from jax import lax
from jax.experimental import pallas as pl
from jax.experimental.pallas import tpu as pltpu
from jax.sharding import PartitionSpec as P

BAND = 32
LX = 8
SETS = 3
MUS = 4
ENTRIES = 18


def load_field(ref, row):
    return [[ref[row, c, a] for a in range(3)] for c in range(2)]


def store_field(ref, row, field):
    for c in range(2):
        for a in range(3):
            ref[row, c, a] = field[c][a]


def combine(function, *fields):
    return [[function(*(f[c][a] for f in fields)) for a in range(3)] for c in range(2)]


def links_at(links_ref, row, link_set, mu):
    return links_ref, ((row * SETS + link_set) * MUS + mu) * ENTRIES


def entry(matrices, a, b, c, shape):
    ref, base = matrices
    return jnp.broadcast_to(ref[pl.ds(base + (a * 3 + b) * 2 + c, 1), :], shape)


def transport(matrices, ahead, here):
    forward = [[None] * 3, [None] * 3]
    backward = [[None] * 3, [None] * 3]
    shape = (ahead if ahead is not None else here)[0][0].shape

    def add(total, c, a, value):
        total[c][a] = value if total[c][a] is None else total[c][a] + value

    for a in range(3):
        for b in range(3):
            real = entry(matrices, a, b, 0, shape)
            imag = entry(matrices, a, b, 1, shape)
            if ahead is not None:
                add(forward, 0, a, real * ahead[0][b] - imag * ahead[1][b])
                add(forward, 1, a, real * ahead[1][b] + imag * ahead[0][b])
            if here is not None:
                add(backward, 0, b, real * here[0][a] + imag * here[1][a])
                add(backward, 1, b, real * here[1][a] - imag * here[0][a])
    return forward, backward


def roll(plane, by):
    return pltpu.roll(plane, by % plane.shape[-1], plane.ndim - 1)


def place(rows):
    first = lax.axis_index("gz") * rows
    plane, first_pos = first // BAND, lax.rem(first, BAND)
    return plane, first_pos, lax.rem(plane, 2) == 1, lax.rem(first_pos // rows, 2) == 1


def taper_kernel(rows, source_ref, width_ref, coefs_ref):
    _, first_pos, _, _ = place(rows)
    ones = jnp.ones((8, 128), jnp.float32)
    per_width = ones * width_ref[0].astype(jnp.float32)
    for i in range(rows + 2):
        distance = ones * (first_pos + i - 1 - source_ref[0]).astype(jnp.float32) / per_width
        coefs_ref[i] = 1.0 / (1.0 + distance * distance)


def eps_kernel(steps_ref, eps_ref):
    eps_ref[...] = 0.25 / (jnp.ones((8, 128), jnp.float32) * steps_ref[0].astype(jnp.float32))


def store_z(rows, matrices, row, field, far_ref, near_ref):
    _, _, odd_plane, _ = place(rows)
    _, up = transport(matrices, None, field)
    store_field(far_ref, row, combine(lambda v, h: jnp.where(odd_plane, h, v), field, up))
    store_field(near_ref, row, combine(lambda v, h: jnp.where(odd_plane, v, h), field, up))


def store_up_and_down(matrices, row, field, up_ref, down_ref):
    _, up = transport(matrices, None, field)
    store_field(up_ref, row, up)
    store_field(down_ref, row, field)


def store_t(rows, matrices, field_ref, outer_ref, inner_ref):
    _, _, _, odd_block = place(rows)
    first = load_field(field_ref, 0)
    _, last = transport(matrices, None, load_field(field_ref, rows - 1))
    store_field(outer_ref, 0, combine(lambda p, q: jnp.where(odd_block, q, p), first, last))
    store_field(inner_ref, 0, combine(lambda p, q: jnp.where(odd_block, p, q), first, last))


def begin_kernel(
    rows, adjoint_hbm, links_hbm, up_ref, down_ref, outer_ref, inner_ref, adjoint_ref, links_ref, sems
):
    row_entries = SETS * MUS * ENTRIES
    z_first = (2 * MUS + 2) * ENTRIES
    aligned = z_first // 8 * 8
    copies = [pltpu.make_async_copy(adjoint_hbm, adjoint_ref, sems.at[rows])]
    for row in range(rows):
        part = links_hbm.at[pl.ds(row * row_entries + aligned, row_entries - aligned), :]
        copies.append(pltpu.make_async_copy(part, links_ref.at[row], sems.at[row]))
    for copy in copies:
        copy.start()
    for copy in copies:
        copy.wait()
    for row in range(rows):
        matrices = links_ref.at[row], z_first - aligned
        store_up_and_down(matrices, row, load_field(adjoint_ref, row), up_ref, down_ref)
    store_t(rows, (links_ref.at[rows - 1], z_first + ENTRIES - aligned), adjoint_ref, outer_ref, inner_ref)


def start_kernel(rows, link_set, coefs_ref, adjoint_ref, links_ref, sum_ref, start_ref):
    for row in range(rows):
        inside = coefs_ref[row + 1]
        store_field(start_ref, row, combine(lambda v: inside * v, load_field(adjoint_ref, row)))
    local_kernel(rows, link_set, start_ref, links_ref, sum_ref)


def local_kernel(rows, link_set, field_ref, links_ref, sum_ref):
    shape = field_ref.shape[-2:]
    x_pos = lax.broadcasted_iota(jnp.int32, shape, 1) % LX
    at_last = x_pos == LX - 1
    at_first = x_pos == 0

    for row in range(rows):
        here = load_field(field_ref, row)
        ahead = combine(lambda v: jnp.where(at_last, roll(v, LX - 1), roll(v, -1)), here)
        ahead_x, hop = transport(links_at(links_ref, row, link_set, 0), ahead, here)
        total = combine(
            lambda v, f, h: f + jnp.where(at_first, roll(h, 1 - LX), roll(h, 1)) - 8.0 * v, here, ahead_x, hop
        )
        ahead = combine(lambda v: roll(v, -LX), here)
        ahead_y, hop = transport(links_at(links_ref, row, link_set, 1), ahead, here)
        total = combine(lambda s, f, h: s + f + roll(h, LX), total, ahead_y, hop)
        if row > 0:
            total = combine(lambda s, h: s + h, total, earlier)
        if row < rows - 1:
            ahead_t, earlier = transport(links_at(links_ref, row, link_set, 3), load_field(field_ref, row + 1), here)
            total = combine(lambda s, f: s + f, total, ahead_t)
        store_field(sum_ref, row, total)


def arrived_sum(links_ref, link_set, row, rows, arrivals, coefs_ref=None):
    sum_ref, one_ref, two_ref, outer_ref, inner_ref = arrivals
    _, first_pos, odd_plane, odd_block = place(rows)
    one, two = load_field(one_ref, row), load_field(two_ref, row)
    if coefs_ref is not None:
        below, above = (combine(lambda v: coefs_ref[row + 1] * v, f) for f in (one, two))
    else:
        below = combine(lambda near, far: jnp.where(odd_plane, near, far), one, two)
        above = combine(lambda near, far: jnp.where(odd_plane, far, near), one, two)
    ahead_z, _ = transport(links_at(links_ref, row, link_set, 2), above, None)
    total = combine(lambda s, f, h: s + f + h, load_field(sum_ref, row), ahead_z, below)
    outer, inner = load_field(outer_ref, 0), load_field(inner_ref, 0)
    if row == 0:
        exists = jnp.where(first_pos != 0, 1.0, 0.0)
        if coefs_ref is not None:
            exists = exists * coefs_ref[0]
        total = combine(lambda s, p, q: s + exists * jnp.where(odd_block, q, p), total, outer, inner)
    if row == rows - 1:
        exists = jnp.where(first_pos != BAND - rows, 1.0, 0.0)
        if coefs_ref is not None:
            exists = exists * coefs_ref[rows + 1]
        later = combine(lambda p, q: exists * jnp.where(odd_block, p, q), outer, inner)
        ahead_t, _ = transport(links_at(links_ref, row, link_set, 3), later, None)
        total = combine(lambda s, f: s + f, total, ahead_t)
    return total


def third_kernel(rows, coefs_ref, links_ref, *refs):
    arrivals, (third_ref, far_ref, near_ref, outer_ref, inner_ref) = refs[:5], refs[5:]
    for row in range(rows):
        inside = coefs_ref[row + 1]
        total = arrived_sum(links_ref, 2, row, rows, arrivals, coefs_ref)
        third = combine(lambda s: 0.75 * (inside * s), total)
        store_field(third_ref, row, third)
        store_z(rows, links_at(links_ref, row, 1, 2), row, third, far_ref, near_ref)
    store_t(rows, links_at(links_ref, rows - 1, 1, 3), third_ref, outer_ref, inner_ref)


def second_kernel(rows, eps_ref, coefs_ref, links_ref, *refs):
    arrivals, (start_ref, third_ref, mixed_ref, far_ref, near_ref, outer_ref, inner_ref, base_ref) = refs[:5], refs[5:]
    eps = eps_ref[...]
    for row in range(rows):
        inside = coefs_ref[row + 1]
        total = arrived_sum(links_ref, 1, row, rows, arrivals)
        third = combine(lambda v: eps * v, load_field(third_ref, row))
        second = combine(
            lambda v, s: v + (8.0 / 9.0) * (inside * (eps * (eps * s))), load_field(start_ref, row), total
        )
        mixed = combine(lambda p, q: 0.25 * p - (2.0 / 9.0) * q, second, third)
        store_field(mixed_ref, row, mixed)
        store_field(base_ref, row, combine(lambda p, q: p + q, second, third))
        store_z(rows, links_at(links_ref, row, 0, 2), row, mixed, far_ref, near_ref)
    store_t(rows, links_at(links_ref, rows - 1, 0, 3), mixed_ref, outer_ref, inner_ref)


def last_kernel(rows, eps_ref, coefs_ref, links_ref, *refs):
    arrivals, (base_ref, out_hbm, out_ref, sems) = refs[:5], refs[5:]
    copies = []
    for row in range(rows):
        inside, eps = coefs_ref[row + 1], eps_ref[...]
        total = arrived_sum(links_ref, 0, row, rows, arrivals)
        store_field(out_ref, row, combine(lambda p, s: p + inside * (eps * s), load_field(base_ref, row), total))
        copies.append(pltpu.make_async_copy(out_ref.at[row], out_hbm.at[row], sems.at[row]))
        copies[-1].start()
    for copy in copies:
        copy.wait()


def call(kernel, name, operands, out_shapes, matvecs, space=pltpu.VMEM, scratch=(), out_space=pltpu.VMEM):
    out_spec = pl.BlockSpec(memory_space=out_space)
    return pl.pallas_call(
        kernel,
        name=name,
        out_shape=out_shapes,
        in_specs=[pl.BlockSpec(memory_space=space)] * len(operands),
        out_specs=jax.tree.map(lambda _: out_spec, out_shapes),
        scratch_shapes=scratch,
        cost_estimate=pl.CostEstimate(flops=matvecs * 72 * 1024, bytes_accessed=4096 * 18 * matvecs, transcendentals=0),
        compiler_params=pltpu.CompilerParams(vmem_limit_bytes=16 * 2**20),
    )(*operands)


def body(adjoint, flowed, source_slice, band_width, flow_steps):
    rows = adjoint.shape[0]
    per_plane = BAND // rows
    count = lax.axis_size("gz")
    links = jnp.transpose(flowed, (0, 1, 2, 4, 5, 3, 6)).reshape(-1, flowed.shape[-1])
    whole = jax.ShapeDtypeStruct(adjoint.shape, jnp.float32)
    one_row = jax.ShapeDtypeStruct((1,) + adjoint.shape[1:], jnp.float32)
    coefs_shape = jax.ShapeDtypeStruct((rows + 2,) + adjoint.shape[3:], jnp.float32)

    def in_plane(i, by):
        return i - i % per_plane + (i + by) % per_plane

    def in_line(i, by):
        return (i + by * per_plane) % count

    far_pairs = [(i, in_line(i, 1 if i // per_plane % 2 else -1)) for i in range(count)]
    near_pairs = [(i, in_line(i, -1 if i // per_plane % 2 else 1)) for i in range(count)]
    outer_pairs = [(i, in_plane(i, 1 if i % 2 else -1)) for i in range(count)]
    inner_pairs = [(i, in_plane(i, -1 if i % 2 else 1)) for i in range(count)]

    up_pairs = [(i, in_line(i, 1)) for i in range(count)]
    down_pairs = [(i, in_line(i, -1)) for i in range(count)]

    def sent_on(far, near, outer, inner):
        near = lax.ppermute(near, "gz", near_pairs)
        far = lax.ppermute(far, "gz", far_pairs)
        outer = lax.ppermute(outer, "gz", outer_pairs)
        inner = lax.ppermute(inner, "gz", inner_pairs)
        return near, far, outer, inner

    def shifted_on(up, down, outer, inner):
        below = lax.ppermute(up, "gz", up_pairs)
        above = lax.ppermute(down, "gz", down_pairs)
        outer = lax.ppermute(outer, "gz", outer_pairs)
        inner = lax.ppermute(inner, "gz", inner_pairs)
        return below, above, outer, inner

    def local(link_set, field):
        return call(functools.partial(local_kernel, rows, link_set), f"local_{link_set}", (field, links), whole, 22)

    sent = (whole, whole, one_row, one_row)
    copied = SETS * MUS * ENTRIES - (2 * MUS + 2) * ENTRIES // 8 * 8
    sending = call(
        functools.partial(begin_kernel, rows), "begin",
        tuple(pltpu.with_memory_space_constraint(a, pltpu.HBM) for a in (adjoint, links)), sent, 5, pltpu.HBM,
        [
            pltpu.VMEM(adjoint.shape, jnp.float32),
            pltpu.VMEM((rows, copied, flowed.shape[-1]), jnp.float32),
            pltpu.SemaphoreType.DMA((rows + 1,)),
        ],
    )
    arrived = shifted_on(*sending)
    coefs = call(
        functools.partial(taper_kernel, rows), "tapers", (source_slice, band_width), coefs_shape, 1, pltpu.SMEM
    )
    eps_shape = jax.ShapeDtypeStruct(adjoint.shape[3:], jnp.float32)
    eps = call(eps_kernel, "eps", (flow_steps,), eps_shape, 1, pltpu.SMEM)
    total, start = call(
        functools.partial(start_kernel, rows, 2), "start", (coefs, adjoint, links), (whole, whole), 22
    )
    third, *sending = call(
        functools.partial(third_kernel, rows), "third", (coefs, links, total) + arrived, (whole,) + sent, 10
    )
    arrived = sent_on(*sending)
    mixed, *sending, base = call(
        functools.partial(second_kernel, rows), "second", (eps, coefs, links, local(1, third)) + arrived + (start, third),
        (whole,) + sent + (whole,), 10,
    )
    arrived = sent_on(*sending)
    return call(
        functools.partial(last_kernel, rows), "last", (eps, coefs, links, local(0, mixed)) + arrived + (base,), whole, 5,
        scratch=[pltpu.VMEM(adjoint.shape, jnp.float32), pltpu.SemaphoreType.DMA((rows,))], out_space=pltpu.HBM,
    )


def solution(mesh):
    in_specs = (
        P(("cfg", "gz"), None, None, None, None),
        P(("cfg", "gz"), None, None, None, None, None, None),
        P("cfg"),
        P("cfg"),
        P("cfg"),
    )
    out_specs = P(("cfg", "gz"), None, None, None, None)
    return jax.shard_map(body, mesh=mesh, in_specs=in_specs, out_specs=out_specs, check_vma=False)
```

```python
import functools

import jax
import jax.numpy as jnp
from jax import lax
from jax.experimental import pallas as pl
from jax.experimental.pallas import tpu as pltpu
from jax.sharding import PartitionSpec as P

BAND = 32
LX = 8
SETS = 3
MUS = 4
ENTRIES = 18


def load_field(ref, row):
    return [[ref[row, c, a] for a in range(3)] for c in range(2)]


def store_field(ref, row, field):
    for c in range(2):
        for a in range(3):
            ref[row, c, a] = field[c][a]


def combine(function, *fields):
    return [[function(*(f[c][a] for f in fields)) for a in range(3)] for c in range(2)]


def links_at(links_ref, row, link_set, mu):
    return links_ref, ((row * SETS + link_set) * MUS + mu) * ENTRIES


def entry(matrices, a, b, c, shape):
    ref, base = matrices
    return jnp.broadcast_to(ref[pl.ds(base + (a * 3 + b) * 2 + c, 1), :], shape)


def transport(matrices, ahead, here):
    forward = [[None] * 3, [None] * 3]
    backward = [[None] * 3, [None] * 3]
    shape = (ahead if ahead is not None else here)[0][0].shape

    def add(total, c, a, value):
        total[c][a] = value if total[c][a] is None else total[c][a] + value

    for a in range(3):
        for b in range(3):
            real = entry(matrices, a, b, 0, shape)
            imag = entry(matrices, a, b, 1, shape)
            if ahead is not None:
                add(forward, 0, a, real * ahead[0][b] - imag * ahead[1][b])
                add(forward, 1, a, real * ahead[1][b] + imag * ahead[0][b])
            if here is not None:
                add(backward, 0, b, real * here[0][a] + imag * here[1][a])
                add(backward, 1, b, real * here[1][a] - imag * here[0][a])
    return forward, backward


def roll(plane, by):
    return pltpu.roll(plane, by % plane.shape[-1], plane.ndim - 1)


def place(rows):
    first = lax.axis_index("gz") * rows
    plane, first_pos = first // BAND, lax.rem(first, BAND)
    return plane, first_pos, lax.rem(plane, 2) == 1, lax.rem(first_pos // rows, 2) == 1


def taper_kernel(rows, source_ref, width_ref, coefs_ref):
    _, first_pos, _, _ = place(rows)
    ones = jnp.ones((8, 128), jnp.float32)
    per_width = ones * width_ref[0].astype(jnp.float32)
    for i in range(rows + 2):
        distance = ones * (first_pos + i - 1 - source_ref[0]).astype(jnp.float32) / per_width
        coefs_ref[i] = 1.0 / (1.0 + distance * distance)


def eps_kernel(steps_ref, eps_ref):
    eps_ref[...] = 0.25 / (jnp.ones((8, 128), jnp.float32) * steps_ref[0].astype(jnp.float32))


def store_z(rows, matrices, row, field, far_ref, near_ref):
    _, _, odd_plane, _ = place(rows)
    _, up = transport(matrices, None, field)
    store_field(far_ref, row, combine(lambda v, h: jnp.where(odd_plane, h, v), field, up))
    store_field(near_ref, row, combine(lambda v, h: jnp.where(odd_plane, v, h), field, up))


def store_up_and_down(matrices, row, field, up_ref, down_ref):
    _, up = transport(matrices, None, field)
    store_field(up_ref, row, up)
    store_field(down_ref, row, field)


def store_t(rows, matrices, field_ref, outer_ref, inner_ref):
    _, _, _, odd_block = place(rows)
    first = load_field(field_ref, 0)
    _, last = transport(matrices, None, load_field(field_ref, rows - 1))
    store_field(outer_ref, 0, combine(lambda p, q: jnp.where(odd_block, q, p), first, last))
    store_field(inner_ref, 0, combine(lambda p, q: jnp.where(odd_block, p, q), first, last))


def begin_kernel(
    rows, adjoint_hbm, links_hbm, up_ref, down_ref, outer_ref, inner_ref, adjoint_ref, links_ref, sems
):
    row_entries = SETS * MUS * ENTRIES
    z_first = (2 * MUS + 2) * ENTRIES
    aligned = z_first // 8 * 8
    copies = [pltpu.make_async_copy(adjoint_hbm, adjoint_ref, sems.at[rows])]
    for row in range(rows):
        part = links_hbm.at[pl.ds(row * row_entries + aligned, row_entries - aligned), :]
        copies.append(pltpu.make_async_copy(part, links_ref.at[row], sems.at[row]))
    for copy in copies:
        copy.start()
    for copy in copies:
        copy.wait()
    for row in range(rows):
        matrices = links_ref.at[row], z_first - aligned
        store_up_and_down(matrices, row, load_field(adjoint_ref, row), up_ref, down_ref)
    store_t(rows, (links_ref.at[rows - 1], z_first + ENTRIES - aligned), adjoint_ref, outer_ref, inner_ref)


def start_kernel(rows, link_set, coefs_ref, adjoint_ref, links_ref, sum_ref, start_ref):
    for row in range(rows):
        inside = coefs_ref[row + 1]
        store_field(start_ref, row, combine(lambda v: inside * v, load_field(adjoint_ref, row)))
    local_kernel(rows, link_set, start_ref, links_ref, sum_ref)


def local_kernel(rows, link_set, field_ref, links_ref, sum_ref):
    shape = field_ref.shape[-2:]
    x_pos = lax.broadcasted_iota(jnp.int32, shape, 1) % LX
    at_last = x_pos == LX - 1
    at_first = x_pos == 0

    for row in range(rows):
        here = load_field(field_ref, row)
        ahead = combine(lambda v: jnp.where(at_last, roll(v, LX - 1), roll(v, -1)), here)
        ahead_x, hop = transport(links_at(links_ref, row, link_set, 0), ahead, here)
        total = combine(
            lambda v, f, h: f + jnp.where(at_first, roll(h, 1 - LX), roll(h, 1)) - 8.0 * v, here, ahead_x, hop
        )
        ahead = combine(lambda v: roll(v, -LX), here)
        ahead_y, hop = transport(links_at(links_ref, row, link_set, 1), ahead, here)
        total = combine(lambda s, f, h: s + f + roll(h, LX), total, ahead_y, hop)
        if row > 0:
            total = combine(lambda s, h: s + h, total, earlier)
        if row < rows - 1:
            ahead_t, earlier = transport(links_at(links_ref, row, link_set, 3), load_field(field_ref, row + 1), here)
            total = combine(lambda s, f: s + f, total, ahead_t)
        store_field(sum_ref, row, total)


def arrived_sum(links_ref, link_set, row, rows, arrivals, coefs_ref=None):
    sum_ref, one_ref, two_ref, outer_ref, inner_ref = arrivals
    if link_set == 1:
        one_ref, two_ref = two_ref, one_ref
    _, first_pos, odd_plane, odd_block = place(rows)
    one, two = load_field(one_ref, row), load_field(two_ref, row)
    if coefs_ref is not None:
        below, above = (combine(lambda v: coefs_ref[row + 1] * v, f) for f in (one, two))
    else:
        below = combine(lambda near, far: jnp.where(odd_plane, near, far), one, two)
        above = combine(lambda near, far: jnp.where(odd_plane, far, near), one, two)
    ahead_z, _ = transport(links_at(links_ref, row, link_set, 2), above, None)
    total = combine(lambda s, f, h: s + f + h, load_field(sum_ref, row), ahead_z, below)
    outer, inner = load_field(outer_ref, 0), load_field(inner_ref, 0)
    if row == 0:
        exists = jnp.where(first_pos != 0, 1.0, 0.0)
        if coefs_ref is not None:
            exists = exists * coefs_ref[0]
        total = combine(lambda s, p, q: s + exists * jnp.where(odd_block, q, p), total, outer, inner)
    if row == rows - 1:
        exists = jnp.where(first_pos != BAND - rows, 1.0, 0.0)
        if coefs_ref is not None:
            exists = exists * coefs_ref[rows + 1]
        later = combine(lambda p, q: exists * jnp.where(odd_block, p, q), outer, inner)
        ahead_t, _ = transport(links_at(links_ref, row, link_set, 3), later, None)
        total = combine(lambda s, f: s + f, total, ahead_t)
    return total


def third_kernel(rows, coefs_ref, links_ref, *refs):
    arrivals, (third_ref, far_ref, near_ref, outer_ref, inner_ref) = refs[:5], refs[5:]
    for row in range(rows):
        inside = coefs_ref[row + 1]
        total = arrived_sum(links_ref, 2, row, rows, arrivals, coefs_ref)
        third = combine(lambda s: 0.75 * (inside * s), total)
        store_field(third_ref, row, third)
        store_z(rows, links_at(links_ref, row, 1, 2), row, third, far_ref, near_ref)
    store_t(rows, links_at(links_ref, rows - 1, 1, 3), third_ref, outer_ref, inner_ref)


def second_kernel(rows, eps_ref, coefs_ref, links_ref, *refs):
    arrivals, (start_ref, third_ref, mixed_ref, far_ref, near_ref, outer_ref, inner_ref, base_ref) = refs[:5], refs[5:]
    eps = eps_ref[...]
    for row in range(rows):
        inside = coefs_ref[row + 1]
        total = arrived_sum(links_ref, 1, row, rows, arrivals)
        third = combine(lambda v: eps * v, load_field(third_ref, row))
        second = combine(
            lambda v, s: v + (8.0 / 9.0) * (inside * (eps * (eps * s))), load_field(start_ref, row), total
        )
        mixed = combine(lambda p, q: 0.25 * p - (2.0 / 9.0) * q, second, third)
        store_field(mixed_ref, row, mixed)
        store_field(base_ref, row, combine(lambda p, q: p + q, second, third))
        store_z(rows, links_at(links_ref, row, 0, 2), row, mixed, far_ref, near_ref)
    store_t(rows, links_at(links_ref, rows - 1, 0, 3), mixed_ref, outer_ref, inner_ref)


def last_kernel(rows, eps_ref, coefs_ref, links_ref, *refs):
    arrivals, (base_ref, out_hbm, out_ref, sems) = refs[:5], refs[5:]
    copies = []
    for row in range(rows):
        inside, eps = coefs_ref[row + 1], eps_ref[...]
        total = arrived_sum(links_ref, 0, row, rows, arrivals)
        store_field(out_ref, row, combine(lambda p, s: p + inside * (eps * s), load_field(base_ref, row), total))
        copies.append(pltpu.make_async_copy(out_ref.at[row], out_hbm.at[row], sems.at[row]))
        copies[-1].start()
    for copy in copies:
        copy.wait()


def call(kernel, name, operands, out_shapes, matvecs, space=pltpu.VMEM, scratch=(), out_space=pltpu.VMEM):
    out_spec = pl.BlockSpec(memory_space=out_space)
    return pl.pallas_call(
        kernel,
        name=name,
        out_shape=out_shapes,
        in_specs=[pl.BlockSpec(memory_space=space)] * len(operands),
        out_specs=jax.tree.map(lambda _: out_spec, out_shapes),
        scratch_shapes=scratch,
        cost_estimate=pl.CostEstimate(flops=matvecs * 72 * 1024, bytes_accessed=4096 * 18 * matvecs, transcendentals=0),
        compiler_params=pltpu.CompilerParams(vmem_limit_bytes=16 * 2**20),
    )(*operands)


def body(adjoint, flowed, source_slice, band_width, flow_steps):
    rows = adjoint.shape[0]
    per_plane = BAND // rows
    count = lax.axis_size("gz")
    links = jnp.transpose(flowed, (0, 1, 2, 4, 5, 3, 6)).reshape(-1, flowed.shape[-1])
    whole = jax.ShapeDtypeStruct(adjoint.shape, jnp.float32)
    one_row = jax.ShapeDtypeStruct((1,) + adjoint.shape[1:], jnp.float32)
    coefs_shape = jax.ShapeDtypeStruct((rows + 2,) + adjoint.shape[3:], jnp.float32)

    def in_plane(i, by):
        return i - i % per_plane + (i + by) % per_plane

    def in_line(i, by):
        return (i + by * per_plane) % count

    far_pairs = [(i, in_line(i, 1 if i // per_plane % 2 else -1)) for i in range(count)]
    near_pairs = [(i, in_line(i, -1 if i // per_plane % 2 else 1)) for i in range(count)]
    outer_pairs = [(i, in_plane(i, 1 if i % 2 else -1)) for i in range(count)]
    inner_pairs = [(i, in_plane(i, -1 if i % 2 else 1)) for i in range(count)]

    up_pairs = [(i, in_line(i, 1)) for i in range(count)]
    down_pairs = [(i, in_line(i, -1)) for i in range(count)]

    def sent_on(far, near, outer, inner, far_first):
        near = lax.ppermute(near, "gz", near_pairs)
        far = lax.ppermute(far, "gz", far_pairs)
        outer = lax.ppermute(outer, "gz", outer_pairs)
        inner = lax.ppermute(inner, "gz", inner_pairs)
        return (far, near, outer, inner) if far_first else (near, far, outer, inner)

    def shifted_on(up, down, outer, inner):
        below = lax.ppermute(up, "gz", up_pairs)
        above = lax.ppermute(down, "gz", down_pairs)
        outer = lax.ppermute(outer, "gz", outer_pairs)
        inner = lax.ppermute(inner, "gz", inner_pairs)
        return below, above, outer, inner

    def local(link_set, field):
        return call(functools.partial(local_kernel, rows, link_set), f"local_{link_set}", (field, links), whole, 22)

    sent = (whole, whole, one_row, one_row)
    copied = SETS * MUS * ENTRIES - (2 * MUS + 2) * ENTRIES // 8 * 8
    sending = call(
        functools.partial(begin_kernel, rows), "begin",
        tuple(pltpu.with_memory_space_constraint(a, pltpu.HBM) for a in (adjoint, links)), sent, 5, pltpu.HBM,
        [
            pltpu.VMEM(adjoint.shape, jnp.float32),
            pltpu.VMEM((rows, copied, flowed.shape[-1]), jnp.float32),
            pltpu.SemaphoreType.DMA((rows + 1,)),
        ],
    )
    arrived = shifted_on(*sending)
    coefs = call(
        functools.partial(taper_kernel, rows), "tapers", (source_slice, band_width), coefs_shape, 1, pltpu.SMEM
    )
    eps_shape = jax.ShapeDtypeStruct(adjoint.shape[3:], jnp.float32)
    eps = call(eps_kernel, "eps", (flow_steps,), eps_shape, 1, pltpu.SMEM)
    total, start = call(
        functools.partial(start_kernel, rows, 2), "start", (coefs, adjoint, links), (whole, whole), 22
    )
    third, *sending = call(
        functools.partial(third_kernel, rows), "third", (coefs, links, total) + arrived, (whole,) + sent, 10
    )
    arrived = sent_on(*sending, far_first=True)
    mixed, *sending, base = call(
        functools.partial(second_kernel, rows), "second", (eps, coefs, links, local(1, third)) + arrived + (start, third),
        (whole,) + sent + (whole,), 10,
    )
    arrived = sent_on(*sending, far_first=False)
    return call(
        functools.partial(last_kernel, rows), "last", (eps, coefs, links, local(0, mixed)) + arrived + (base,), whole, 5,
        scratch=[pltpu.VMEM(adjoint.shape, jnp.float32), pltpu.SemaphoreType.DMA((rows,))], out_space=pltpu.HBM,
    )


def solution(mesh):
    in_specs = (
        P(("cfg", "gz"), None, None, None, None),
        P(("cfg", "gz"), None, None, None, None, None, None),
        P("cfg"),
        P("cfg"),
        P("cfg"),
    )
    out_specs = P(("cfg", "gz"), None, None, None, None)
    return jax.shard_map(body, mesh=mesh, in_specs=in_specs, out_specs=out_specs, check_vma=False)
```

```python
import functools

import jax
import jax.numpy as jnp
from jax import lax
from jax.experimental import pallas as pl
from jax.experimental.pallas import tpu as pltpu
from jax.sharding import PartitionSpec as P

BAND = 32
LX = 8
SETS = 3
MUS = 4
ENTRIES = 18


def load_field(ref, row):
    return [[ref[row, c, a] for a in range(3)] for c in range(2)]


def store_field(ref, row, field):
    for c in range(2):
        for a in range(3):
            ref[row, c, a] = field[c][a]


def combine(function, *fields):
    return [[function(*(f[c][a] for f in fields)) for a in range(3)] for c in range(2)]


def links_at(links_ref, row, link_set, mu):
    return links_ref, ((row * SETS + link_set) * MUS + mu) * ENTRIES


def entry(matrices, a, b, c, shape):
    ref, base = matrices
    return jnp.broadcast_to(ref[pl.ds(base + (a * 3 + b) * 2 + c, 1), :], shape)


def transport(matrices, ahead, here):
    forward = [[None] * 3, [None] * 3]
    backward = [[None] * 3, [None] * 3]
    shape = (ahead if ahead is not None else here)[0][0].shape

    def add(total, c, a, value):
        total[c][a] = value if total[c][a] is None else total[c][a] + value

    for a in range(3):
        for b in range(3):
            real = entry(matrices, a, b, 0, shape)
            imag = entry(matrices, a, b, 1, shape)
            if ahead is not None:
                add(forward, 0, a, real * ahead[0][b] - imag * ahead[1][b])
                add(forward, 1, a, real * ahead[1][b] + imag * ahead[0][b])
            if here is not None:
                add(backward, 0, b, real * here[0][a] + imag * here[1][a])
                add(backward, 1, b, real * here[1][a] - imag * here[0][a])
    return forward, backward


def roll(plane, by):
    return pltpu.roll(plane, by % plane.shape[-1], plane.ndim - 1)


def place(rows):
    first = lax.axis_index("gz") * rows
    plane, first_pos = first // BAND, lax.rem(first, BAND)
    return plane, first_pos, lax.rem(plane, 2) == 1, lax.rem(first_pos // rows, 2) == 1


def taper_kernel(rows, source_ref, width_ref, coefs_ref):
    _, first_pos, _, _ = place(rows)
    ones = jnp.ones((8, 128), jnp.float32)
    per_width = ones * width_ref[0].astype(jnp.float32)
    for i in range(rows + 2):
        distance = ones * (first_pos + i - 1 - source_ref[0]).astype(jnp.float32) / per_width
        coefs_ref[i] = 1.0 / (1.0 + distance * distance)


def eps_kernel(steps_ref, eps_ref):
    eps_ref[...] = 0.25 / (jnp.ones((8, 128), jnp.float32) * steps_ref[0].astype(jnp.float32))


def store_z(rows, matrices, row, field, far_ref, near_ref):
    _, _, odd_plane, _ = place(rows)
    _, up = transport(matrices, None, field)
    store_field(far_ref, row, combine(lambda v, h: jnp.where(odd_plane, h, v), field, up))
    store_field(near_ref, row, combine(lambda v, h: jnp.where(odd_plane, v, h), field, up))


def store_up_and_down(matrices, row, field, up_ref, down_ref):
    _, up = transport(matrices, None, field)
    store_field(up_ref, row, up)
    store_field(down_ref, row, field)


def store_t(rows, matrices, field_ref, outer_ref, inner_ref):
    _, _, _, odd_block = place(rows)
    first = load_field(field_ref, 0)
    _, last = transport(matrices, None, load_field(field_ref, rows - 1))
    store_field(outer_ref, 0, combine(lambda p, q: jnp.where(odd_block, q, p), first, last))
    store_field(inner_ref, 0, combine(lambda p, q: jnp.where(odd_block, p, q), first, last))


def begin_kernel(
    rows, adjoint_hbm, links_hbm, up_ref, down_ref, outer_ref, inner_ref, adjoint_ref, links_ref, sems
):
    row_entries = SETS * MUS * ENTRIES
    z_first = (2 * MUS + 2) * ENTRIES
    aligned = z_first // 8 * 8
    copies = [pltpu.make_async_copy(adjoint_hbm, adjoint_ref, sems.at[rows])]
    for row in range(rows):
        part = links_hbm.at[pl.ds(row * row_entries + aligned, row_entries - aligned), :]
        copies.append(pltpu.make_async_copy(part, links_ref.at[row], sems.at[row]))
    for copy in copies:
        copy.start()
    for copy in copies:
        copy.wait()
    for row in range(rows):
        matrices = links_ref.at[row], z_first - aligned
        store_up_and_down(matrices, row, load_field(adjoint_ref, row), up_ref, down_ref)
    store_t(rows, (links_ref.at[rows - 1], z_first + ENTRIES - aligned), adjoint_ref, outer_ref, inner_ref)


def start_kernel(rows, link_set, coefs_ref, adjoint_ref, links_ref, sum_ref, start_ref):
    for row in range(rows):
        inside = coefs_ref[row + 1]
        store_field(start_ref, row, combine(lambda v: inside * v, load_field(adjoint_ref, row)))
    local_kernel(rows, link_set, start_ref, links_ref, sum_ref)


def local_kernel(rows, link_set, field_ref, links_ref, sum_ref):
    shape = field_ref.shape[-2:]
    x_pos = lax.broadcasted_iota(jnp.int32, shape, 1) % LX
    at_last = x_pos == LX - 1
    at_first = x_pos == 0

    for row in range(rows):
        here = load_field(field_ref, row)
        ahead = combine(lambda v: jnp.where(at_last, roll(v, LX - 1), roll(v, -1)), here)
        ahead_x, hop = transport(links_at(links_ref, row, link_set, 0), ahead, here)
        total = combine(
            lambda v, f, h: f + jnp.where(at_first, roll(h, 1 - LX), roll(h, 1)) - 8.0 * v, here, ahead_x, hop
        )
        ahead = combine(lambda v: roll(v, -LX), here)
        ahead_y, hop = transport(links_at(links_ref, row, link_set, 1), ahead, here)
        total = combine(lambda s, f, h: s + f + roll(h, LX), total, ahead_y, hop)
        if row > 0:
            total = combine(lambda s, h: s + h, total, earlier)
        if row < rows - 1:
            ahead_t, earlier = transport(links_at(links_ref, row, link_set, 3), load_field(field_ref, row + 1), here)
            total = combine(lambda s, f: s + f, total, ahead_t)
        store_field(sum_ref, row, total)


def arrived_sum(links_ref, link_set, row, rows, arrivals, coefs_ref=None):
    sum_ref, one_ref, two_ref, outer_ref, inner_ref = arrivals
    if link_set == 0:
        one_ref, two_ref = two_ref, one_ref
    _, first_pos, odd_plane, odd_block = place(rows)
    one, two = load_field(one_ref, row), load_field(two_ref, row)
    if coefs_ref is not None:
        below, above = (combine(lambda v: coefs_ref[row + 1] * v, f) for f in (one, two))
    else:
        below = combine(lambda near, far: jnp.where(odd_plane, near, far), one, two)
        above = combine(lambda near, far: jnp.where(odd_plane, far, near), one, two)
    ahead_z, _ = transport(links_at(links_ref, row, link_set, 2), above, None)
    total = combine(lambda s, f, h: s + f + h, load_field(sum_ref, row), ahead_z, below)
    outer, inner = load_field(outer_ref, 0), load_field(inner_ref, 0)
    if row == 0:
        exists = jnp.where(first_pos != 0, 1.0, 0.0)
        if coefs_ref is not None:
            exists = exists * coefs_ref[0]
        total = combine(lambda s, p, q: s + exists * jnp.where(odd_block, q, p), total, outer, inner)
    if row == rows - 1:
        exists = jnp.where(first_pos != BAND - rows, 1.0, 0.0)
        if coefs_ref is not None:
            exists = exists * coefs_ref[rows + 1]
        later = combine(lambda p, q: exists * jnp.where(odd_block, p, q), outer, inner)
        ahead_t, _ = transport(links_at(links_ref, row, link_set, 3), later, None)
        total = combine(lambda s, f: s + f, total, ahead_t)
    return total


def third_kernel(rows, coefs_ref, links_ref, *refs):
    arrivals, (third_ref, far_ref, near_ref, outer_ref, inner_ref) = refs[:5], refs[5:]
    for row in range(rows):
        inside = coefs_ref[row + 1]
        total = arrived_sum(links_ref, 2, row, rows, arrivals, coefs_ref)
        third = combine(lambda s: 0.75 * (inside * s), total)
        store_field(third_ref, row, third)
        store_z(rows, links_at(links_ref, row, 1, 2), row, third, far_ref, near_ref)
    store_t(rows, links_at(links_ref, rows - 1, 1, 3), third_ref, outer_ref, inner_ref)


def second_kernel(rows, eps_ref, coefs_ref, links_ref, *refs):
    arrivals, (start_ref, third_ref, mixed_ref, far_ref, near_ref, outer_ref, inner_ref, base_ref) = refs[:5], refs[5:]
    eps = eps_ref[...]
    for row in range(rows):
        inside = coefs_ref[row + 1]
        total = arrived_sum(links_ref, 1, row, rows, arrivals)
        third = combine(lambda v: eps * v, load_field(third_ref, row))
        second = combine(
            lambda v, s: v + (8.0 / 9.0) * (inside * (eps * (eps * s))), load_field(start_ref, row), total
        )
        mixed = combine(lambda p, q: 0.25 * p - (2.0 / 9.0) * q, second, third)
        store_field(mixed_ref, row, mixed)
        store_field(base_ref, row, combine(lambda p, q: p + q, second, third))
        store_z(rows, links_at(links_ref, row, 0, 2), row, mixed, far_ref, near_ref)
    store_t(rows, links_at(links_ref, rows - 1, 0, 3), mixed_ref, outer_ref, inner_ref)


def last_kernel(rows, eps_ref, coefs_ref, links_ref, *refs):
    arrivals, (base_ref, out_hbm, out_ref, sems) = refs[:5], refs[5:]
    copies = []
    for row in range(rows):
        inside, eps = coefs_ref[row + 1], eps_ref[...]
        total = arrived_sum(links_ref, 0, row, rows, arrivals)
        store_field(out_ref, row, combine(lambda p, s: p + inside * (eps * s), load_field(base_ref, row), total))
        copies.append(pltpu.make_async_copy(out_ref.at[row], out_hbm.at[row], sems.at[row]))
        copies[-1].start()
    for copy in copies:
        copy.wait()


def call(kernel, name, operands, out_shapes, matvecs, space=pltpu.VMEM, scratch=(), out_space=pltpu.VMEM):
    out_spec = pl.BlockSpec(memory_space=out_space)
    return pl.pallas_call(
        kernel,
        name=name,
        out_shape=out_shapes,
        in_specs=[pl.BlockSpec(memory_space=space)] * len(operands),
        out_specs=jax.tree.map(lambda _: out_spec, out_shapes),
        scratch_shapes=scratch,
        cost_estimate=pl.CostEstimate(flops=matvecs * 72 * 1024, bytes_accessed=4096 * 18 * matvecs, transcendentals=0),
        compiler_params=pltpu.CompilerParams(vmem_limit_bytes=16 * 2**20),
    )(*operands)


def body(adjoint, flowed, source_slice, band_width, flow_steps):
    rows = adjoint.shape[0]
    per_plane = BAND // rows
    count = lax.axis_size("gz")
    links = jnp.transpose(flowed, (0, 1, 2, 4, 5, 3, 6)).reshape(-1, flowed.shape[-1])
    whole = jax.ShapeDtypeStruct(adjoint.shape, jnp.float32)
    one_row = jax.ShapeDtypeStruct((1,) + adjoint.shape[1:], jnp.float32)
    coefs_shape = jax.ShapeDtypeStruct((rows + 2,) + adjoint.shape[3:], jnp.float32)

    def in_plane(i, by):
        return i - i % per_plane + (i + by) % per_plane

    def in_line(i, by):
        return (i + by * per_plane) % count

    far_pairs = [(i, in_line(i, 1 if i // per_plane % 2 else -1)) for i in range(count)]
    near_pairs = [(i, in_line(i, -1 if i // per_plane % 2 else 1)) for i in range(count)]
    outer_pairs = [(i, in_plane(i, 1 if i % 2 else -1)) for i in range(count)]
    inner_pairs = [(i, in_plane(i, -1 if i % 2 else 1)) for i in range(count)]

    up_pairs = [(i, in_line(i, 1)) for i in range(count)]
    down_pairs = [(i, in_line(i, -1)) for i in range(count)]

    def sent_on(far, near, outer, inner, far_first):
        near = lax.ppermute(near, "gz", near_pairs)
        far = lax.ppermute(far, "gz", far_pairs)
        outer = lax.ppermute(outer, "gz", outer_pairs)
        inner = lax.ppermute(inner, "gz", inner_pairs)
        return (far, near, outer, inner) if far_first else (near, far, outer, inner)

    def shifted_on(up, down, outer, inner):
        below = lax.ppermute(up, "gz", up_pairs)
        above = lax.ppermute(down, "gz", down_pairs)
        outer = lax.ppermute(outer, "gz", outer_pairs)
        inner = lax.ppermute(inner, "gz", inner_pairs)
        return below, above, outer, inner

    def local(link_set, field):
        return call(functools.partial(local_kernel, rows, link_set), f"local_{link_set}", (field, links), whole, 22)

    sent = (whole, whole, one_row, one_row)
    copied = SETS * MUS * ENTRIES - (2 * MUS + 2) * ENTRIES // 8 * 8
    sending = call(
        functools.partial(begin_kernel, rows), "begin",
        tuple(pltpu.with_memory_space_constraint(a, pltpu.HBM) for a in (adjoint, links)), sent, 5, pltpu.HBM,
        [
            pltpu.VMEM(adjoint.shape, jnp.float32),
            pltpu.VMEM((rows, copied, flowed.shape[-1]), jnp.float32),
            pltpu.SemaphoreType.DMA((rows + 1,)),
        ],
    )
    arrived = shifted_on(*sending)
    coefs = call(
        functools.partial(taper_kernel, rows), "tapers", (source_slice, band_width), coefs_shape, 1, pltpu.SMEM
    )
    eps_shape = jax.ShapeDtypeStruct(adjoint.shape[3:], jnp.float32)
    eps = call(eps_kernel, "eps", (flow_steps,), eps_shape, 1, pltpu.SMEM)
    total, start = call(
        functools.partial(start_kernel, rows, 2), "start", (coefs, adjoint, links), (whole, whole), 22
    )
    third, *sending = call(
        functools.partial(third_kernel, rows), "third", (coefs, links, total) + arrived, (whole,) + sent, 10
    )
    arrived = sent_on(*sending, far_first=False)
    mixed, *sending, base = call(
        functools.partial(second_kernel, rows), "second", (eps, coefs, links, local(1, third)) + arrived + (start, third),
        (whole,) + sent + (whole,), 10,
    )
    arrived = sent_on(*sending, far_first=True)
    return call(
        functools.partial(last_kernel, rows), "last", (eps, coefs, links, local(0, mixed)) + arrived + (base,), whole, 5,
        scratch=[pltpu.VMEM(adjoint.shape, jnp.float32), pltpu.SemaphoreType.DMA((rows,))], out_space=pltpu.HBM,
    )


def solution(mesh):
    in_specs = (
        P(("cfg", "gz"), None, None, None, None),
        P(("cfg", "gz"), None, None, None, None, None, None),
        P("cfg"),
        P("cfg"),
        P("cfg"),
    )
    out_specs = P(("cfg", "gz"), None, None, None, None)
    return jax.shard_map(body, mesh=mesh, in_specs=in_specs, out_specs=out_specs, check_vma=False)
```

```python
import functools

import jax
import jax.numpy as jnp
from jax import lax
from jax.experimental import pallas as pl
from jax.experimental.pallas import tpu as pltpu
from jax.sharding import PartitionSpec as P

BAND = 32
LX = 8
SETS = 3
MUS = 4
ENTRIES = 18


def load_field(ref, row):
    return [[ref[row, c, a] for a in range(3)] for c in range(2)]


def store_field(ref, row, field):
    for c in range(2):
        for a in range(3):
            ref[row, c, a] = field[c][a]


def combine(function, *fields):
    return [[function(*(f[c][a] for f in fields)) for a in range(3)] for c in range(2)]


def links_at(links_ref, row, link_set, mu):
    return links_ref, ((row * SETS + link_set) * MUS + mu) * ENTRIES


def entry(matrices, a, b, c, shape):
    ref, base = matrices
    return jnp.broadcast_to(ref[pl.ds(base + (a * 3 + b) * 2 + c, 1), :], shape)


def transport(matrices, ahead, here):
    forward = [[None] * 3, [None] * 3]
    backward = [[None] * 3, [None] * 3]
    shape = (ahead if ahead is not None else here)[0][0].shape

    def add(total, c, a, value):
        total[c][a] = value if total[c][a] is None else total[c][a] + value

    for a in range(3):
        for b in range(3):
            real = entry(matrices, a, b, 0, shape)
            imag = entry(matrices, a, b, 1, shape)
            if ahead is not None:
                add(forward, 0, a, real * ahead[0][b] - imag * ahead[1][b])
                add(forward, 1, a, real * ahead[1][b] + imag * ahead[0][b])
            if here is not None:
                add(backward, 0, b, real * here[0][a] + imag * here[1][a])
                add(backward, 1, b, real * here[1][a] - imag * here[0][a])
    return forward, backward


def roll(plane, by):
    return pltpu.roll(plane, by % plane.shape[-1], plane.ndim - 1)


def place(rows):
    first = lax.axis_index("gz") * rows
    plane, first_pos = first // BAND, lax.rem(first, BAND)
    return plane, first_pos, lax.rem(plane, 2) == 1, lax.rem(first_pos // rows, 2) == 1


def taper_kernel(rows, source_ref, width_ref, coefs_ref):
    _, first_pos, _, _ = place(rows)
    ones = jnp.ones((8, 128), jnp.float32)
    per_width = ones * width_ref[0].astype(jnp.float32)
    for i in range(rows + 2):
        distance = ones * (first_pos + i - 1 - source_ref[0]).astype(jnp.float32) / per_width
        coefs_ref[i] = 1.0 / (1.0 + distance * distance)


def eps_kernel(steps_ref, eps_ref):
    eps_ref[...] = 0.25 / (jnp.ones((8, 128), jnp.float32) * steps_ref[0].astype(jnp.float32))


def store_z(rows, matrices, row, field, far_ref, near_ref):
    _, _, odd_plane, _ = place(rows)
    _, up = transport(matrices, None, field)
    store_field(far_ref, row, combine(lambda v, h: jnp.where(odd_plane, h, v), field, up))
    store_field(near_ref, row, combine(lambda v, h: jnp.where(odd_plane, v, h), field, up))


def store_up_and_down(matrices, row, field, up_ref, down_ref):
    _, up = transport(matrices, None, field)
    store_field(up_ref, row, up)
    store_field(down_ref, row, field)


def store_t(rows, matrices, field_ref, outer_ref, inner_ref):
    _, _, _, odd_block = place(rows)
    first = load_field(field_ref, 0)
    _, last = transport(matrices, None, load_field(field_ref, rows - 1))
    store_field(outer_ref, 0, combine(lambda p, q: jnp.where(odd_block, q, p), first, last))
    store_field(inner_ref, 0, combine(lambda p, q: jnp.where(odd_block, p, q), first, last))


def begin_kernel(
    rows, adjoint_hbm, links_hbm, up_ref, down_ref, outer_ref, inner_ref, adjoint_ref, links_ref, sems
):
    row_entries = SETS * MUS * ENTRIES
    z_first = (2 * MUS + 2) * ENTRIES
    aligned = z_first // 8 * 8
    copies = [pltpu.make_async_copy(adjoint_hbm, adjoint_ref, sems.at[rows])]
    for row in range(rows):
        part = links_hbm.at[pl.ds(row * row_entries + aligned, row_entries - aligned), :]
        copies.append(pltpu.make_async_copy(part, links_ref.at[row], sems.at[row]))
    for copy in copies:
        copy.start()
    for copy in copies:
        copy.wait()
    for row in range(rows):
        matrices = links_ref.at[row], z_first - aligned
        store_up_and_down(matrices, row, load_field(adjoint_ref, row), up_ref, down_ref)
    store_t(rows, (links_ref.at[rows - 1], z_first + ENTRIES - aligned), adjoint_ref, outer_ref, inner_ref)


def start_kernel(rows, link_set, coefs_ref, adjoint_ref, links_ref, sum_ref, start_ref):
    for row in range(rows):
        inside = coefs_ref[row + 1]
        store_field(start_ref, row, combine(lambda v: inside * v, load_field(adjoint_ref, row)))
    local_kernel(rows, link_set, start_ref, links_ref, sum_ref)


def local_kernel(rows, link_set, field_ref, links_ref, sum_ref):
    shape = field_ref.shape[-2:]
    x_pos = lax.broadcasted_iota(jnp.int32, shape, 1) % LX
    at_last = x_pos == LX - 1
    at_first = x_pos == 0

    for row in range(rows):
        here = load_field(field_ref, row)
        ahead = combine(lambda v: jnp.where(at_last, roll(v, LX - 1), roll(v, -1)), here)
        ahead_x, hop = transport(links_at(links_ref, row, link_set, 0), ahead, here)
        total = combine(
            lambda v, f, h: f + jnp.where(at_first, roll(h, 1 - LX), roll(h, 1)) - 8.0 * v, here, ahead_x, hop
        )
        ahead = combine(lambda v: roll(v, -LX), here)
        ahead_y, hop = transport(links_at(links_ref, row, link_set, 1), ahead, here)
        total = combine(lambda s, f, h: s + f + roll(h, LX), total, ahead_y, hop)
        if row > 0:
            total = combine(lambda s, h: s + h, total, earlier)
        if row < rows - 1:
            ahead_t, earlier = transport(links_at(links_ref, row, link_set, 3), load_field(field_ref, row + 1), here)
            total = combine(lambda s, f: s + f, total, ahead_t)
        store_field(sum_ref, row, total)


def arrived_sum(links_ref, link_set, row, rows, arrivals, coefs_ref=None):
    sum_ref, one_ref, two_ref, outer_ref, inner_ref = arrivals
    if link_set == 0:
        one_ref, two_ref = two_ref, one_ref
    _, first_pos, odd_plane, odd_block = place(rows)
    one, two = load_field(one_ref, row), load_field(two_ref, row)
    if coefs_ref is not None:
        outer_ref, inner_ref = inner_ref, outer_ref
        below, above = (combine(lambda v: coefs_ref[row + 1] * v, f) for f in (one, two))
    else:
        below = combine(lambda near, far: jnp.where(odd_plane, near, far), one, two)
        above = combine(lambda near, far: jnp.where(odd_plane, far, near), one, two)
    ahead_z, _ = transport(links_at(links_ref, row, link_set, 2), above, None)
    total = combine(lambda s, f, h: s + f + h, load_field(sum_ref, row), ahead_z, below)
    outer, inner = load_field(outer_ref, 0), load_field(inner_ref, 0)
    if row == 0:
        exists = jnp.where(first_pos != 0, 1.0, 0.0)
        if coefs_ref is not None:
            exists = exists * coefs_ref[0]
        total = combine(lambda s, p, q: s + exists * jnp.where(odd_block, q, p), total, outer, inner)
    if row == rows - 1:
        exists = jnp.where(first_pos != BAND - rows, 1.0, 0.0)
        if coefs_ref is not None:
            exists = exists * coefs_ref[rows + 1]
        later = combine(lambda p, q: exists * jnp.where(odd_block, p, q), outer, inner)
        ahead_t, _ = transport(links_at(links_ref, row, link_set, 3), later, None)
        total = combine(lambda s, f: s + f, total, ahead_t)
    return total


def third_kernel(rows, coefs_ref, links_ref, *refs):
    arrivals, (third_ref, far_ref, near_ref, outer_ref, inner_ref) = refs[:5], refs[5:]
    for row in range(rows):
        inside = coefs_ref[row + 1]
        total = arrived_sum(links_ref, 2, row, rows, arrivals, coefs_ref)
        third = combine(lambda s: 0.75 * (inside * s), total)
        store_field(third_ref, row, third)
        store_z(rows, links_at(links_ref, row, 1, 2), row, third, far_ref, near_ref)
    store_t(rows, links_at(links_ref, rows - 1, 1, 3), third_ref, outer_ref, inner_ref)


def second_kernel(rows, eps_ref, coefs_ref, links_ref, *refs):
    arrivals, (start_ref, third_ref, mixed_ref, far_ref, near_ref, outer_ref, inner_ref, base_ref) = refs[:5], refs[5:]
    eps = eps_ref[...]
    for row in range(rows):
        inside = coefs_ref[row + 1]
        total = arrived_sum(links_ref, 1, row, rows, arrivals)
        third = combine(lambda v: eps * v, load_field(third_ref, row))
        second = combine(
            lambda v, s: v + (8.0 / 9.0) * (inside * (eps * (eps * s))), load_field(start_ref, row), total
        )
        mixed = combine(lambda p, q: 0.25 * p - (2.0 / 9.0) * q, second, third)
        store_field(mixed_ref, row, mixed)
        store_field(base_ref, row, combine(lambda p, q: p + q, second, third))
        store_z(rows, links_at(links_ref, row, 0, 2), row, mixed, far_ref, near_ref)
    store_t(rows, links_at(links_ref, rows - 1, 0, 3), mixed_ref, outer_ref, inner_ref)


def last_kernel(rows, eps_ref, coefs_ref, links_ref, *refs):
    arrivals, (base_ref, out_hbm, out_ref, sems) = refs[:5], refs[5:]
    copies = []
    for row in range(rows):
        inside, eps = coefs_ref[row + 1], eps_ref[...]
        total = arrived_sum(links_ref, 0, row, rows, arrivals)
        store_field(out_ref, row, combine(lambda p, s: p + inside * (eps * s), load_field(base_ref, row), total))
        copies.append(pltpu.make_async_copy(out_ref.at[row], out_hbm.at[row], sems.at[row]))
        copies[-1].start()
    for copy in copies:
        copy.wait()


def call(kernel, name, operands, out_shapes, matvecs, space=pltpu.VMEM, scratch=(), out_space=pltpu.VMEM):
    out_spec = pl.BlockSpec(memory_space=out_space)
    return pl.pallas_call(
        kernel,
        name=name,
        out_shape=out_shapes,
        in_specs=[pl.BlockSpec(memory_space=space)] * len(operands),
        out_specs=jax.tree.map(lambda _: out_spec, out_shapes),
        scratch_shapes=scratch,
        cost_estimate=pl.CostEstimate(flops=matvecs * 72 * 1024, bytes_accessed=4096 * 18 * matvecs, transcendentals=0),
        compiler_params=pltpu.CompilerParams(vmem_limit_bytes=16 * 2**20),
    )(*operands)


def body(adjoint, flowed, source_slice, band_width, flow_steps):
    rows = adjoint.shape[0]
    per_plane = BAND // rows
    count = lax.axis_size("gz")
    links = jnp.transpose(flowed, (0, 1, 2, 4, 5, 3, 6)).reshape(-1, flowed.shape[-1])
    whole = jax.ShapeDtypeStruct(adjoint.shape, jnp.float32)
    one_row = jax.ShapeDtypeStruct((1,) + adjoint.shape[1:], jnp.float32)
    coefs_shape = jax.ShapeDtypeStruct((rows + 2,) + adjoint.shape[3:], jnp.float32)

    def in_plane(i, by):
        return i - i % per_plane + (i + by) % per_plane

    def in_line(i, by):
        return (i + by * per_plane) % count

    far_pairs = [(i, in_line(i, 1 if i // per_plane % 2 else -1)) for i in range(count)]
    near_pairs = [(i, in_line(i, -1 if i // per_plane % 2 else 1)) for i in range(count)]
    outer_pairs = [(i, in_plane(i, 1 if i % 2 else -1)) for i in range(count)]
    inner_pairs = [(i, in_plane(i, -1 if i % 2 else 1)) for i in range(count)]

    up_pairs = [(i, in_line(i, 1)) for i in range(count)]
    down_pairs = [(i, in_line(i, -1)) for i in range(count)]

    def sent_on(far, near, outer, inner, far_first):
        near = lax.ppermute(near, "gz", near_pairs)
        far = lax.ppermute(far, "gz", far_pairs)
        outer = lax.ppermute(outer, "gz", outer_pairs)
        inner = lax.ppermute(inner, "gz", inner_pairs)
        return (far, near, outer, inner) if far_first else (near, far, outer, inner)

    def shifted_on(up, down, outer, inner):
        below = lax.ppermute(up, "gz", up_pairs)
        above = lax.ppermute(down, "gz", down_pairs)
        outer = lax.ppermute(outer, "gz", outer_pairs)
        inner = lax.ppermute(inner, "gz", inner_pairs)
        return below, above, inner, outer

    def local(link_set, field):
        return call(functools.partial(local_kernel, rows, link_set), f"local_{link_set}", (field, links), whole, 22)

    sent = (whole, whole, one_row, one_row)
    copied = SETS * MUS * ENTRIES - (2 * MUS + 2) * ENTRIES // 8 * 8
    sending = call(
        functools.partial(begin_kernel, rows), "begin",
        tuple(pltpu.with_memory_space_constraint(a, pltpu.HBM) for a in (adjoint, links)), sent, 5, pltpu.HBM,
        [
            pltpu.VMEM(adjoint.shape, jnp.float32),
            pltpu.VMEM((rows, copied, flowed.shape[-1]), jnp.float32),
            pltpu.SemaphoreType.DMA((rows + 1,)),
        ],
    )
    arrived = shifted_on(*sending)
    coefs = call(
        functools.partial(taper_kernel, rows), "tapers", (source_slice, band_width), coefs_shape, 1, pltpu.SMEM
    )
    eps_shape = jax.ShapeDtypeStruct(adjoint.shape[3:], jnp.float32)
    eps = call(eps_kernel, "eps", (flow_steps,), eps_shape, 1, pltpu.SMEM)
    total, start = call(
        functools.partial(start_kernel, rows, 2), "start", (coefs, adjoint, links), (whole, whole), 22
    )
    third, *sending = call(
        functools.partial(third_kernel, rows), "third", (coefs, links, total) + arrived, (whole,) + sent, 10
    )
    arrived = sent_on(*sending, far_first=False)
    mixed, *sending, base = call(
        functools.partial(second_kernel, rows), "second", (eps, coefs, links, local(1, third)) + arrived + (start, third),
        (whole,) + sent + (whole,), 10,
    )
    arrived = sent_on(*sending, far_first=True)
    return call(
        functools.partial(last_kernel, rows), "last", (eps, coefs, links, local(0, mixed)) + arrived + (base,), whole, 5,
        scratch=[pltpu.VMEM(adjoint.shape, jnp.float32), pltpu.SemaphoreType.DMA((rows,))], out_space=pltpu.HBM,
    )


def solution(mesh):
    in_specs = (
        P(("cfg", "gz"), None, None, None, None),
        P(("cfg", "gz"), None, None, None, None, None, None),
        P("cfg"),
        P("cfg"),
        P("cfg"),
    )
    out_specs = P(("cfg", "gz"), None, None, None, None)
    return jax.shard_map(body, mesh=mesh, in_specs=in_specs, out_specs=out_specs, check_vma=False)
```

```python
import functools

import jax
import jax.numpy as jnp
from jax import lax
from jax.experimental import pallas as pl
from jax.experimental.pallas import tpu as pltpu
from jax.sharding import PartitionSpec as P

BAND = 32
LX = 8
SETS = 3
MUS = 4
ENTRIES = 18


def load_field(ref, row):
    return [[ref[row, c, a] for a in range(3)] for c in range(2)]


def store_field(ref, row, field):
    for c in range(2):
        for a in range(3):
            ref[row, c, a] = field[c][a]


def combine(function, *fields):
    return [[function(*(f[c][a] for f in fields)) for a in range(3)] for c in range(2)]


def links_at(links_ref, row, link_set, mu):
    return links_ref, ((row * SETS + link_set) * MUS + mu) * ENTRIES


def entry(matrices, a, b, c, shape):
    ref, base = matrices
    return jnp.broadcast_to(ref[pl.ds(base + (a * 3 + b) * 2 + c, 1), :], shape)


def transport(matrices, ahead, here):
    forward = [[None] * 3, [None] * 3]
    backward = [[None] * 3, [None] * 3]
    shape = (ahead if ahead is not None else here)[0][0].shape

    def add(total, c, a, value):
        total[c][a] = value if total[c][a] is None else total[c][a] + value

    for a in range(3):
        for b in range(3):
            real = entry(matrices, a, b, 0, shape)
            imag = entry(matrices, a, b, 1, shape)
            if ahead is not None:
                add(forward, 0, a, real * ahead[0][b] - imag * ahead[1][b])
                add(forward, 1, a, real * ahead[1][b] + imag * ahead[0][b])
            if here is not None:
                add(backward, 0, b, real * here[0][a] + imag * here[1][a])
                add(backward, 1, b, real * here[1][a] - imag * here[0][a])
    return forward, backward


def roll(plane, by):
    return pltpu.roll(plane, by % plane.shape[-1], plane.ndim - 1)


def place(rows):
    first = lax.axis_index("gz") * rows
    plane, first_pos = first // BAND, lax.rem(first, BAND)
    return plane, first_pos, lax.rem(plane, 2) == 1, lax.rem(first_pos // rows, 2) == 1


def taper_kernel(rows, source_ref, width_ref, coefs_ref):
    _, first_pos, _, _ = place(rows)
    ones = jnp.ones((8, 128), jnp.float32)
    per_width = ones * width_ref[0].astype(jnp.float32)
    for i in range(rows + 2):
        distance = ones * (first_pos + i - 1 - source_ref[0]).astype(jnp.float32) / per_width
        coefs_ref[i] = 1.0 / (1.0 + distance * distance)


def eps_kernel(steps_ref, eps_ref):
    eps_ref[...] = 0.25 / (jnp.ones((8, 128), jnp.float32) * steps_ref[0].astype(jnp.float32))


def store_z(rows, matrices, row, field, far_ref, near_ref):
    _, _, odd_plane, _ = place(rows)
    _, up = transport(matrices, None, field)
    store_field(far_ref, row, combine(lambda v, h: jnp.where(odd_plane, h, v), field, up))
    store_field(near_ref, row, combine(lambda v, h: jnp.where(odd_plane, v, h), field, up))


def store_up_and_down(matrices, row, field, up_ref, down_ref):
    _, up = transport(matrices, None, field)
    store_field(up_ref, row, up)
    store_field(down_ref, row, field)


def store_t(rows, matrices, field_ref, outer_ref, inner_ref):
    _, _, _, odd_block = place(rows)
    first = load_field(field_ref, 0)
    _, last = transport(matrices, None, load_field(field_ref, rows - 1))
    store_field(outer_ref, 0, combine(lambda p, q: jnp.where(odd_block, q, p), first, last))
    store_field(inner_ref, 0, combine(lambda p, q: jnp.where(odd_block, p, q), first, last))


def begin_kernel(
    rows, adjoint_hbm, links_hbm, up_ref, down_ref, outer_ref, inner_ref, adjoint_ref, links_ref, sems
):
    row_entries = SETS * MUS * ENTRIES
    z_first = (2 * MUS + 2) * ENTRIES
    aligned = z_first // 8 * 8
    copies = [pltpu.make_async_copy(adjoint_hbm, adjoint_ref, sems.at[rows])]
    for row in range(rows):
        part = links_hbm.at[pl.ds(row * row_entries + aligned, row_entries - aligned), :]
        copies.append(pltpu.make_async_copy(part, links_ref.at[row], sems.at[row]))
    for copy in copies:
        copy.start()
    for copy in copies:
        copy.wait()
    for row in range(rows):
        matrices = links_ref.at[row], z_first - aligned
        store_up_and_down(matrices, row, load_field(adjoint_ref, row), up_ref, down_ref)
    store_t(rows, (links_ref.at[rows - 1], z_first + ENTRIES - aligned), adjoint_ref, outer_ref, inner_ref)


def start_kernel(rows, link_set, coefs_ref, adjoint_ref, links_ref, sum_ref, start_ref):
    for row in range(rows):
        inside = coefs_ref[row + 1]
        store_field(start_ref, row, combine(lambda v: inside * v, load_field(adjoint_ref, row)))
    local_kernel(rows, link_set, start_ref, links_ref, sum_ref)


def local_kernel(rows, link_set, field_ref, links_ref, sum_ref):
    shape = field_ref.shape[-2:]
    x_pos = lax.broadcasted_iota(jnp.int32, shape, 1) % LX
    at_last = x_pos == LX - 1
    at_first = x_pos == 0

    for row in range(rows):
        here = load_field(field_ref, row)
        ahead = combine(lambda v: jnp.where(at_last, roll(v, LX - 1), roll(v, -1)), here)
        ahead_x, hop = transport(links_at(links_ref, row, link_set, 0), ahead, here)
        total = combine(
            lambda v, f, h: f + jnp.where(at_first, roll(h, 1 - LX), roll(h, 1)) - 8.0 * v, here, ahead_x, hop
        )
        ahead = combine(lambda v: roll(v, -LX), here)
        ahead_y, hop = transport(links_at(links_ref, row, link_set, 1), ahead, here)
        total = combine(lambda s, f, h: s + f + roll(h, LX), total, ahead_y, hop)
        if row > 0:
            total = combine(lambda s, h: s + h, total, earlier)
        if row < rows - 1:
            ahead_t, earlier = transport(links_at(links_ref, row, link_set, 3), load_field(field_ref, row + 1), here)
            total = combine(lambda s, f: s + f, total, ahead_t)
        store_field(sum_ref, row, total)


def arrived_sum(links_ref, link_set, row, rows, arrivals, coefs_ref=None):
    sum_ref, one_ref, two_ref, outer_ref, inner_ref = arrivals
    if coefs_ref is None:
        one_ref, two_ref = two_ref, one_ref
    _, first_pos, odd_plane, odd_block = place(rows)
    one, two = load_field(one_ref, row), load_field(two_ref, row)
    if coefs_ref is not None:
        below, above = (combine(lambda v: coefs_ref[row + 1] * v, f) for f in (one, two))
    else:
        below = combine(lambda near, far: jnp.where(odd_plane, near, far), one, two)
        above = combine(lambda near, far: jnp.where(odd_plane, far, near), one, two)
    ahead_z, _ = transport(links_at(links_ref, row, link_set, 2), above, None)
    total = combine(lambda s, f, h: s + f + h, load_field(sum_ref, row), ahead_z, below)
    outer, inner = load_field(outer_ref, 0), load_field(inner_ref, 0)
    if row == 0:
        exists = jnp.where(first_pos != 0, 1.0, 0.0)
        if coefs_ref is not None:
            exists = exists * coefs_ref[0]
        total = combine(lambda s, p, q: s + exists * jnp.where(odd_block, q, p), total, outer, inner)
    if row == rows - 1:
        exists = jnp.where(first_pos != BAND - rows, 1.0, 0.0)
        if coefs_ref is not None:
            exists = exists * coefs_ref[rows + 1]
        later = combine(lambda p, q: exists * jnp.where(odd_block, p, q), outer, inner)
        ahead_t, _ = transport(links_at(links_ref, row, link_set, 3), later, None)
        total = combine(lambda s, f: s + f, total, ahead_t)
    return total


def third_kernel(rows, coefs_ref, links_ref, *refs):
    arrivals, (third_ref, far_ref, near_ref, outer_ref, inner_ref) = refs[:5], refs[5:]
    for row in range(rows):
        inside = coefs_ref[row + 1]
        total = arrived_sum(links_ref, 2, row, rows, arrivals, coefs_ref)
        third = combine(lambda s: 0.75 * (inside * s), total)
        store_field(third_ref, row, third)
        store_z(rows, links_at(links_ref, row, 1, 2), row, third, far_ref, near_ref)
    store_t(rows, links_at(links_ref, rows - 1, 1, 3), third_ref, outer_ref, inner_ref)


def second_kernel(rows, eps_ref, coefs_ref, links_ref, *refs):
    arrivals, (start_ref, third_ref, mixed_ref, far_ref, near_ref, outer_ref, inner_ref, base_ref) = refs[:5], refs[5:]
    eps = eps_ref[...]
    for row in range(rows):
        inside = coefs_ref[row + 1]
        total = arrived_sum(links_ref, 1, row, rows, arrivals)
        third = combine(lambda v: eps * v, load_field(third_ref, row))
        second = combine(
            lambda v, s: v + (8.0 / 9.0) * (inside * (eps * (eps * s))), load_field(start_ref, row), total
        )
        mixed = combine(lambda p, q: 0.25 * p - (2.0 / 9.0) * q, second, third)
        store_field(mixed_ref, row, mixed)
        store_field(base_ref, row, combine(lambda p, q: p + q, second, third))
        store_z(rows, links_at(links_ref, row, 0, 2), row, mixed, far_ref, near_ref)
    store_t(rows, links_at(links_ref, rows - 1, 0, 3), mixed_ref, outer_ref, inner_ref)


def last_kernel(rows, eps_ref, coefs_ref, links_ref, *refs):
    arrivals, (base_ref, out_hbm, out_ref, sems) = refs[:5], refs[5:]
    copies = []
    for row in range(rows):
        inside, eps = coefs_ref[row + 1], eps_ref[...]
        total = arrived_sum(links_ref, 0, row, rows, arrivals)
        store_field(out_ref, row, combine(lambda p, s: p + inside * (eps * s), load_field(base_ref, row), total))
        copies.append(pltpu.make_async_copy(out_ref.at[row], out_hbm.at[row], sems.at[row]))
        copies[-1].start()
    for copy in copies:
        copy.wait()


def call(kernel, name, operands, out_shapes, matvecs, space=pltpu.VMEM, scratch=(), out_space=pltpu.VMEM):
    out_spec = pl.BlockSpec(memory_space=out_space)
    return pl.pallas_call(
        kernel,
        name=name,
        out_shape=out_shapes,
        in_specs=[pl.BlockSpec(memory_space=space)] * len(operands),
        out_specs=jax.tree.map(lambda _: out_spec, out_shapes),
        scratch_shapes=scratch,
        cost_estimate=pl.CostEstimate(flops=matvecs * 72 * 1024, bytes_accessed=4096 * 18 * matvecs, transcendentals=0),
        compiler_params=pltpu.CompilerParams(vmem_limit_bytes=16 * 2**20),
    )(*operands)


def body(adjoint, flowed, source_slice, band_width, flow_steps):
    rows = adjoint.shape[0]
    per_plane = BAND // rows
    count = lax.axis_size("gz")
    links = jnp.transpose(flowed, (0, 1, 2, 4, 5, 3, 6)).reshape(-1, flowed.shape[-1])
    whole = jax.ShapeDtypeStruct(adjoint.shape, jnp.float32)
    one_row = jax.ShapeDtypeStruct((1,) + adjoint.shape[1:], jnp.float32)
    coefs_shape = jax.ShapeDtypeStruct((rows + 2,) + adjoint.shape[3:], jnp.float32)

    def in_plane(i, by):
        return i - i % per_plane + (i + by) % per_plane

    def in_line(i, by):
        return (i + by * per_plane) % count

    far_pairs = [(i, in_line(i, 1 if i // per_plane % 2 else -1)) for i in range(count)]
    near_pairs = [(i, in_line(i, -1 if i // per_plane % 2 else 1)) for i in range(count)]
    outer_pairs = [(i, in_plane(i, 1 if i % 2 else -1)) for i in range(count)]
    inner_pairs = [(i, in_plane(i, -1 if i % 2 else 1)) for i in range(count)]

    up_pairs = [(i, in_line(i, 1)) for i in range(count)]
    down_pairs = [(i, in_line(i, -1)) for i in range(count)]

    def sent_on(far, near, outer, inner):
        near = lax.ppermute(near, "gz", near_pairs)
        far = lax.ppermute(far, "gz", far_pairs)
        outer = lax.ppermute(outer, "gz", outer_pairs)
        inner = lax.ppermute(inner, "gz", inner_pairs)
        return far, near, outer, inner

    def shifted_on(up, down, outer, inner):
        below = lax.ppermute(up, "gz", up_pairs)
        above = lax.ppermute(down, "gz", down_pairs)
        outer = lax.ppermute(outer, "gz", outer_pairs)
        inner = lax.ppermute(inner, "gz", inner_pairs)
        return below, above, outer, inner

    def local(link_set, field):
        return call(functools.partial(local_kernel, rows, link_set), f"local_{link_set}", (field, links), whole, 22)

    sent = (whole, whole, one_row, one_row)
    copied = SETS * MUS * ENTRIES - (2 * MUS + 2) * ENTRIES // 8 * 8
    sending = call(
        functools.partial(begin_kernel, rows), "begin",
        tuple(pltpu.with_memory_space_constraint(a, pltpu.HBM) for a in (adjoint, links)), sent, 5, pltpu.HBM,
        [
            pltpu.VMEM(adjoint.shape, jnp.float32),
            pltpu.VMEM((rows, copied, flowed.shape[-1]), jnp.float32),
            pltpu.SemaphoreType.DMA((rows + 1,)),
        ],
    )
    arrived = shifted_on(*sending)
    coefs = call(
        functools.partial(taper_kernel, rows), "tapers", (source_slice, band_width), coefs_shape, 1, pltpu.SMEM
    )
    eps_shape = jax.ShapeDtypeStruct(adjoint.shape[3:], jnp.float32)
    eps = call(eps_kernel, "eps", (flow_steps,), eps_shape, 1, pltpu.SMEM)
    total, start = call(
        functools.partial(start_kernel, rows, 2), "start", (coefs, adjoint, links), (whole, whole), 22
    )
    third, *sending = call(
        functools.partial(third_kernel, rows), "third", (coefs, links, total) + arrived, (whole,) + sent, 10
    )
    arrived = sent_on(*sending)
    mixed, *sending, base = call(
        functools.partial(second_kernel, rows), "second", (eps, coefs, links, local(1, third)) + arrived + (start, third),
        (whole,) + sent + (whole,), 10,
    )
    arrived = sent_on(*sending)
    return call(
        functools.partial(last_kernel, rows), "last", (eps, coefs, links, local(0, mixed)) + arrived + (base,), whole, 5,
        scratch=[pltpu.VMEM(adjoint.shape, jnp.float32), pltpu.SemaphoreType.DMA((rows,))], out_space=pltpu.HBM,
    )


def solution(mesh):
    in_specs = (
        P(("cfg", "gz"), None, None, None, None),
        P(("cfg", "gz"), None, None, None, None, None, None),
        P("cfg"),
        P("cfg"),
        P("cfg"),
    )
    out_specs = P(("cfg", "gz"), None, None, None, None)
    return jax.shard_map(body, mesh=mesh, in_specs=in_specs, out_specs=out_specs, check_vma=False)
```

```python
import functools

import jax
import jax.numpy as jnp
from jax import lax
from jax.experimental import pallas as pl
from jax.experimental.pallas import tpu as pltpu
from jax.sharding import PartitionSpec as P

BAND = 32
LX = 8
SETS = 3
MUS = 4
ENTRIES = 18


def load_field(ref, row):
    return [[ref[row, c, a] for a in range(3)] for c in range(2)]


def store_field(ref, row, field):
    for c in range(2):
        for a in range(3):
            ref[row, c, a] = field[c][a]


def combine(function, *fields):
    return [[function(*(f[c][a] for f in fields)) for a in range(3)] for c in range(2)]


def links_at(links_ref, row, link_set, mu):
    return links_ref, ((row * SETS + link_set) * MUS + mu) * ENTRIES


def entry(matrices, a, b, c, shape):
    ref, base = matrices
    return jnp.broadcast_to(ref[pl.ds(base + (a * 3 + b) * 2 + c, 1), :], shape)


def transport(matrices, ahead, here):
    forward = [[None] * 3, [None] * 3]
    backward = [[None] * 3, [None] * 3]
    shape = (ahead if ahead is not None else here)[0][0].shape

    def add(total, c, a, value):
        total[c][a] = value if total[c][a] is None else total[c][a] + value

    for a in range(3):
        for b in range(3):
            real = entry(matrices, a, b, 0, shape)
            imag = entry(matrices, a, b, 1, shape)
            if ahead is not None:
                add(forward, 0, a, real * ahead[0][b] - imag * ahead[1][b])
                add(forward, 1, a, real * ahead[1][b] + imag * ahead[0][b])
            if here is not None:
                add(backward, 0, b, real * here[0][a] + imag * here[1][a])
                add(backward, 1, b, real * here[1][a] - imag * here[0][a])
    return forward, backward


def roll(plane, by):
    return pltpu.roll(plane, by % plane.shape[-1], plane.ndim - 1)


def place(rows):
    first = lax.axis_index("gz") * rows
    plane, first_pos = first // BAND, lax.rem(first, BAND)
    return plane, first_pos, lax.rem(plane, 2) == 1, lax.rem(first_pos // rows, 2) == 1


def taper_kernel(rows, source_ref, width_ref, coefs_ref):
    _, first_pos, _, _ = place(rows)
    ones = jnp.ones((8, 128), jnp.float32)
    per_width = ones * width_ref[0].astype(jnp.float32)
    for i in range(rows + 2):
        distance = ones * (first_pos + i - 1 - source_ref[0]).astype(jnp.float32) / per_width
        coefs_ref[i] = 1.0 / (1.0 + distance * distance)


def eps_kernel(steps_ref, eps_ref):
    eps_ref[...] = 0.25 / (jnp.ones((8, 128), jnp.float32) * steps_ref[0].astype(jnp.float32))


def store_z(rows, matrices, row, field, far_ref, near_ref):
    _, _, odd_plane, _ = place(rows)
    _, up = transport(matrices, None, field)
    store_field(far_ref, row, combine(lambda v, h: jnp.where(odd_plane, h, v), field, up))
    store_field(near_ref, row, combine(lambda v, h: jnp.where(odd_plane, v, h), field, up))


def store_up_and_down(matrices, row, field, up_ref, down_ref):
    _, up = transport(matrices, None, field)
    store_field(up_ref, row, up)
    store_field(down_ref, row, field)


def store_t(rows, matrices, field_ref, outer_ref, inner_ref):
    _, _, _, odd_block = place(rows)
    first = load_field(field_ref, 0)
    _, last = transport(matrices, None, load_field(field_ref, rows - 1))
    store_field(outer_ref, 0, combine(lambda p, q: jnp.where(odd_block, q, p), first, last))
    store_field(inner_ref, 0, combine(lambda p, q: jnp.where(odd_block, p, q), first, last))


def begin_kernel(
    rows, adjoint_hbm, links_hbm, up_ref, down_ref, outer_ref, inner_ref, adjoint_ref, links_ref, sems
):
    row_entries = SETS * MUS * ENTRIES
    z_first = (2 * MUS + 2) * ENTRIES
    aligned = z_first // 8 * 8
    copies = [pltpu.make_async_copy(adjoint_hbm, adjoint_ref, sems.at[rows])]
    for row in range(rows):
        part = links_hbm.at[pl.ds(row * row_entries + aligned, row_entries - aligned), :]
        copies.append(pltpu.make_async_copy(part, links_ref.at[row], sems.at[row]))
    for copy in copies:
        copy.start()
    for copy in copies:
        copy.wait()
    for row in range(rows):
        matrices = links_ref.at[row], z_first - aligned
        store_up_and_down(matrices, row, load_field(adjoint_ref, row), up_ref, down_ref)
    store_t(rows, (links_ref.at[rows - 1], z_first + ENTRIES - aligned), adjoint_ref, outer_ref, inner_ref)


def start_kernel(rows, link_set, coefs_ref, adjoint_ref, links_ref, sum_ref, start_ref):
    for row in range(rows):
        inside = coefs_ref[row + 1]
        store_field(start_ref, row, combine(lambda v: inside * v, load_field(adjoint_ref, row)))
    local_kernel(rows, link_set, start_ref, links_ref, sum_ref)


def local_kernel(rows, link_set, field_ref, links_ref, sum_ref):
    shape = field_ref.shape[-2:]
    x_pos = lax.broadcasted_iota(jnp.int32, shape, 1) % LX
    at_last = x_pos == LX - 1
    at_first = x_pos == 0

    for row in range(rows):
        here = load_field(field_ref, row)
        ahead = combine(lambda v: jnp.where(at_last, roll(v, LX - 1), roll(v, -1)), here)
        ahead_x, hop = transport(links_at(links_ref, row, link_set, 0), ahead, here)
        total = combine(
            lambda v, f, h: f + jnp.where(at_first, roll(h, 1 - LX), roll(h, 1)) - 8.0 * v, here, ahead_x, hop
        )
        ahead = combine(lambda v: roll(v, -LX), here)
        ahead_y, hop = transport(links_at(links_ref, row, link_set, 1), ahead, here)
        total = combine(lambda s, f, h: s + f + roll(h, LX), total, ahead_y, hop)
        if row > 0:
            total = combine(lambda s, h: s + h, total, earlier)
        if row < rows - 1:
            ahead_t, earlier = transport(links_at(links_ref, row, link_set, 3), load_field(field_ref, row + 1), here)
            total = combine(lambda s, f: s + f, total, ahead_t)
        store_field(sum_ref, row, total)


def arrived_sum(links_ref, link_set, row, rows, arrivals, coefs_ref=None):
    sum_ref, one_ref, two_ref, outer_ref, inner_ref = arrivals
    _, _, odd_plane, _ = place(rows)
    one, two = load_field(one_ref, row), load_field(two_ref, row)
    if coefs_ref is not None:
        below, above = (combine(lambda v: coefs_ref[row + 1] * v, f) for f in (one, two))
    else:
        below = combine(lambda near, far: jnp.where(odd_plane, near, far), one, two)
        above = combine(lambda near, far: jnp.where(odd_plane, far, near), one, two)
    ahead_z, _ = transport(links_at(links_ref, row, link_set, 2), above, None)
    total = combine(lambda s, f, h: s + f + h, load_field(sum_ref, row), ahead_z, below)
    return with_edges(links_ref, link_set, row, rows, total, outer_ref, inner_ref, coefs_ref)


def with_edges(links_ref, link_set, row, rows, total, outer_ref, inner_ref, coefs_ref=None):
    _, first_pos, _, odd_block = place(rows)
    outer, inner = load_field(outer_ref, 0), load_field(inner_ref, 0)
    if row == 0:
        exists = jnp.where(first_pos != 0, 1.0, 0.0)
        if coefs_ref is not None:
            exists = exists * coefs_ref[0]
        total = combine(lambda s, p, q: s + exists * jnp.where(odd_block, q, p), total, outer, inner)
    if row == rows - 1:
        exists = jnp.where(first_pos != BAND - rows, 1.0, 0.0)
        if coefs_ref is not None:
            exists = exists * coefs_ref[rows + 1]
        later = combine(lambda p, q: exists * jnp.where(odd_block, p, q), outer, inner)
        ahead_t, _ = transport(links_at(links_ref, row, link_set, 3), later, None)
        total = combine(lambda s, f: s + f, total, ahead_t)
    return total


def third_kernel(rows, coefs_ref, links_ref, *refs):
    arrivals, (third_ref, far_ref, near_ref, outer_ref, inner_ref) = refs[:5], refs[5:]
    for row in range(rows):
        inside = coefs_ref[row + 1]
        total = arrived_sum(links_ref, 2, row, rows, arrivals, coefs_ref)
        third = combine(lambda s: 0.75 * (inside * s), total)
        store_field(third_ref, row, third)
        store_z(rows, links_at(links_ref, row, 1, 2), row, third, far_ref, near_ref)
    store_t(rows, links_at(links_ref, rows - 1, 1, 3), third_ref, outer_ref, inner_ref)


def second_kernel(rows, eps_ref, coefs_ref, links_ref, *refs):
    arrivals, (start_ref, third_ref, mixed_ref, far_ref, near_ref, outer_ref, inner_ref, base_ref) = refs[:5], refs[5:]
    eps = eps_ref[...]
    for row in range(rows):
        inside = coefs_ref[row + 1]
        total = arrived_sum(links_ref, 1, row, rows, arrivals)
        third = combine(lambda v: eps * v, load_field(third_ref, row))
        second = combine(
            lambda v, s: v + (8.0 / 9.0) * (inside * (eps * (eps * s))), load_field(start_ref, row), total
        )
        mixed = combine(lambda p, q: 0.25 * p - (2.0 / 9.0) * q, second, third)
        store_field(mixed_ref, row, mixed)
        store_field(base_ref, row, combine(lambda p, q: p + q, second, third))
        store_z(rows, links_at(links_ref, row, 0, 2), row, mixed, far_ref, near_ref)
    store_t(rows, links_at(links_ref, rows - 1, 0, 3), mixed_ref, outer_ref, inner_ref)


def z_term(links_ref, row, field, from_above):
    ahead, _ = transport(links_at(links_ref, row, 0, 2), field, None)
    return combine(lambda f, h: jnp.where(from_above, f, h), ahead, field)


def partial_kernel(
    rows, eps_ref, coefs_ref, links_ref, sum_ref, far_ref, outer_ref, inner_ref, base_ref, partial_ref
):
    _, _, odd_plane, _ = place(rows)
    for row in range(rows):
        inside, eps = coefs_ref[row + 1], eps_ref[...]
        far = z_term(links_ref, row, load_field(far_ref, row), odd_plane)
        total = combine(lambda s, f: s + f, load_field(sum_ref, row), far)
        total = with_edges(links_ref, 0, row, rows, total, outer_ref, inner_ref)
        store_field(
            partial_ref, row, combine(lambda p, s: p + inside * (eps * s), load_field(base_ref, row), total)
        )


def last_kernel(rows, eps_ref, coefs_ref, links_ref, near_ref, partial_ref, out_hbm, out_ref, sems):
    _, _, odd_plane, _ = place(rows)
    copies = []
    for row in range(rows):
        inside, eps = coefs_ref[row + 1], eps_ref[...]
        near = z_term(links_ref, row, load_field(near_ref, row), ~odd_plane)
        store_field(out_ref, row, combine(lambda p, s: p + inside * (eps * s), load_field(partial_ref, row), near))
        copies.append(pltpu.make_async_copy(out_ref.at[row], out_hbm.at[row], sems.at[row]))
        copies[-1].start()
    for copy in copies:
        copy.wait()


def call(kernel, name, operands, out_shapes, matvecs, space=pltpu.VMEM, scratch=(), out_space=pltpu.VMEM):
    out_spec = pl.BlockSpec(memory_space=out_space)
    return pl.pallas_call(
        kernel,
        name=name,
        out_shape=out_shapes,
        in_specs=[pl.BlockSpec(memory_space=space)] * len(operands),
        out_specs=jax.tree.map(lambda _: out_spec, out_shapes),
        scratch_shapes=scratch,
        cost_estimate=pl.CostEstimate(flops=matvecs * 72 * 1024, bytes_accessed=4096 * 18 * matvecs, transcendentals=0),
        compiler_params=pltpu.CompilerParams(vmem_limit_bytes=16 * 2**20),
    )(*operands)


def body(adjoint, flowed, source_slice, band_width, flow_steps):
    rows = adjoint.shape[0]
    per_plane = BAND // rows
    count = lax.axis_size("gz")
    links = jnp.transpose(flowed, (0, 1, 2, 4, 5, 3, 6)).reshape(-1, flowed.shape[-1])
    whole = jax.ShapeDtypeStruct(adjoint.shape, jnp.float32)
    one_row = jax.ShapeDtypeStruct((1,) + adjoint.shape[1:], jnp.float32)
    coefs_shape = jax.ShapeDtypeStruct((rows + 2,) + adjoint.shape[3:], jnp.float32)

    def in_plane(i, by):
        return i - i % per_plane + (i + by) % per_plane

    def in_line(i, by):
        return (i + by * per_plane) % count

    far_pairs = [(i, in_line(i, 1 if i // per_plane % 2 else -1)) for i in range(count)]
    near_pairs = [(i, in_line(i, -1 if i // per_plane % 2 else 1)) for i in range(count)]
    outer_pairs = [(i, in_plane(i, 1 if i % 2 else -1)) for i in range(count)]
    inner_pairs = [(i, in_plane(i, -1 if i % 2 else 1)) for i in range(count)]

    up_pairs = [(i, in_line(i, 1)) for i in range(count)]
    down_pairs = [(i, in_line(i, -1)) for i in range(count)]

    def sent_on(far, near, outer, inner, far_first):
        near = lax.ppermute(near, "gz", near_pairs)
        far = lax.ppermute(far, "gz", far_pairs)
        outer = lax.ppermute(outer, "gz", outer_pairs)
        inner = lax.ppermute(inner, "gz", inner_pairs)
        return (far, near, outer, inner) if far_first else (near, far, outer, inner)

    def shifted_on(up, down, outer, inner):
        below = lax.ppermute(up, "gz", up_pairs)
        above = lax.ppermute(down, "gz", down_pairs)
        outer = lax.ppermute(outer, "gz", outer_pairs)
        inner = lax.ppermute(inner, "gz", inner_pairs)
        return below, above, outer, inner

    def local(link_set, field):
        return call(functools.partial(local_kernel, rows, link_set), f"local_{link_set}", (field, links), whole, 22)

    sent = (whole, whole, one_row, one_row)
    copied = SETS * MUS * ENTRIES - (2 * MUS + 2) * ENTRIES // 8 * 8
    sending = call(
        functools.partial(begin_kernel, rows), "begin",
        tuple(pltpu.with_memory_space_constraint(a, pltpu.HBM) for a in (adjoint, links)), sent, 5, pltpu.HBM,
        [
            pltpu.VMEM(adjoint.shape, jnp.float32),
            pltpu.VMEM((rows, copied, flowed.shape[-1]), jnp.float32),
            pltpu.SemaphoreType.DMA((rows + 1,)),
        ],
    )
    arrived = shifted_on(*sending)
    coefs = call(
        functools.partial(taper_kernel, rows), "tapers", (source_slice, band_width), coefs_shape, 1, pltpu.SMEM
    )
    eps_shape = jax.ShapeDtypeStruct(adjoint.shape[3:], jnp.float32)
    eps = call(eps_kernel, "eps", (flow_steps,), eps_shape, 1, pltpu.SMEM)
    total, start = call(
        functools.partial(start_kernel, rows, 2), "start", (coefs, adjoint, links), (whole, whole), 22
    )
    third, *sending = call(
        functools.partial(third_kernel, rows), "third", (coefs, links, total) + arrived, (whole,) + sent, 10
    )
    arrived = sent_on(*sending, far_first=False)
    mixed, *sending, base = call(
        functools.partial(second_kernel, rows), "second", (eps, coefs, links, local(1, third)) + arrived + (start, third),
        (whole,) + sent + (whole,), 10,
    )
    far, near, outer, inner = sent_on(*sending, far_first=True)
    partial = call(
        functools.partial(partial_kernel, rows), "partial",
        (eps, coefs, links, local(0, mixed), far, outer, inner, base), whole, 5,
    )
    return call(
        functools.partial(last_kernel, rows), "last", (eps, coefs, links, near, partial), whole, 4,
        scratch=[pltpu.VMEM(adjoint.shape, jnp.float32), pltpu.SemaphoreType.DMA((rows,))], out_space=pltpu.HBM,
    )


def solution(mesh):
    in_specs = (
        P(("cfg", "gz"), None, None, None, None),
        P(("cfg", "gz"), None, None, None, None, None, None),
        P("cfg"),
        P("cfg"),
        P("cfg"),
    )
    out_specs = P(("cfg", "gz"), None, None, None, None)
    return jax.shard_map(body, mesh=mesh, in_specs=in_specs, out_specs=out_specs, check_vma=False)
```

```python
import functools

import jax
import jax.numpy as jnp
from jax import lax
from jax.experimental import pallas as pl
from jax.experimental.pallas import tpu as pltpu
from jax.sharding import PartitionSpec as P

BAND = 32
LX = 8
SETS = 3
MUS = 4
ENTRIES = 18


def load_field(ref, row):
    return [[ref[row, c, a] for a in range(3)] for c in range(2)]


def store_field(ref, row, field):
    for c in range(2):
        for a in range(3):
            ref[row, c, a] = field[c][a]


def combine(function, *fields):
    return [[function(*(f[c][a] for f in fields)) for a in range(3)] for c in range(2)]


def links_at(links_ref, row, link_set, mu):
    return links_ref, ((row * SETS + link_set) * MUS + mu) * ENTRIES


def entry(matrices, a, b, c, shape):
    ref, base = matrices
    return jnp.broadcast_to(ref[pl.ds(base + (a * 3 + b) * 2 + c, 1), :], shape)


def transport(matrices, ahead, here):
    forward = [[None] * 3, [None] * 3]
    backward = [[None] * 3, [None] * 3]
    shape = (ahead if ahead is not None else here)[0][0].shape

    def add(total, c, a, value):
        total[c][a] = value if total[c][a] is None else total[c][a] + value

    for a in range(3):
        for b in range(3):
            real = entry(matrices, a, b, 0, shape)
            imag = entry(matrices, a, b, 1, shape)
            if ahead is not None:
                add(forward, 0, a, real * ahead[0][b] - imag * ahead[1][b])
                add(forward, 1, a, real * ahead[1][b] + imag * ahead[0][b])
            if here is not None:
                add(backward, 0, b, real * here[0][a] + imag * here[1][a])
                add(backward, 1, b, real * here[1][a] - imag * here[0][a])
    return forward, backward


def roll(plane, by):
    return pltpu.roll(plane, by % plane.shape[-1], plane.ndim - 1)


def place(rows):
    first = lax.axis_index("gz") * rows
    plane, first_pos = first // BAND, lax.rem(first, BAND)
    return plane, first_pos, lax.rem(plane, 2) == 1, lax.rem(first_pos // rows, 2) == 1


def taper_kernel(rows, source_ref, width_ref, coefs_ref):
    _, first_pos, _, _ = place(rows)
    ones = jnp.ones((8, 128), jnp.float32)
    per_width = ones * width_ref[0].astype(jnp.float32)
    for i in range(rows + 2):
        distance = ones * (first_pos + i - 1 - source_ref[0]).astype(jnp.float32) / per_width
        coefs_ref[i] = 1.0 / (1.0 + distance * distance)


def eps_kernel(steps_ref, eps_ref):
    eps_ref[...] = 0.25 / (jnp.ones((8, 128), jnp.float32) * steps_ref[0].astype(jnp.float32))


def store_z(rows, matrices, row, field, far_ref, near_ref):
    _, _, odd_plane, _ = place(rows)
    _, up = transport(matrices, None, field)
    store_field(far_ref, row, combine(lambda v, h: jnp.where(odd_plane, h, v), field, up))
    store_field(near_ref, row, combine(lambda v, h: jnp.where(odd_plane, v, h), field, up))


def store_up_and_down(matrices, row, field, up_ref, down_ref):
    _, up = transport(matrices, None, field)
    store_field(up_ref, row, up)
    store_field(down_ref, row, field)


def store_t(rows, matrices, field_ref, outer_ref, inner_ref):
    _, _, _, odd_block = place(rows)
    first = load_field(field_ref, 0)
    _, last = transport(matrices, None, load_field(field_ref, rows - 1))
    store_field(outer_ref, 0, combine(lambda p, q: jnp.where(odd_block, q, p), first, last))
    store_field(inner_ref, 0, combine(lambda p, q: jnp.where(odd_block, p, q), first, last))


def begin_kernel(
    rows, adjoint_hbm, links_hbm, up_ref, down_ref, outer_ref, inner_ref, adjoint_ref, links_ref, sems
):
    row_entries = SETS * MUS * ENTRIES
    z_first = (2 * MUS + 2) * ENTRIES
    aligned = z_first // 8 * 8
    copies = [pltpu.make_async_copy(adjoint_hbm, adjoint_ref, sems.at[rows])]
    for row in range(rows):
        part = links_hbm.at[pl.ds(row * row_entries + aligned, row_entries - aligned), :]
        copies.append(pltpu.make_async_copy(part, links_ref.at[row], sems.at[row]))
    for copy in copies:
        copy.start()
    for copy in copies:
        copy.wait()
    for row in range(rows):
        matrices = links_ref.at[row], z_first - aligned
        store_up_and_down(matrices, row, load_field(adjoint_ref, row), up_ref, down_ref)
    store_t(rows, (links_ref.at[rows - 1], z_first + ENTRIES - aligned), adjoint_ref, outer_ref, inner_ref)


def start_kernel(rows, link_set, coefs_ref, adjoint_ref, links_ref, sum_ref, start_ref):
    for row in range(rows):
        inside = coefs_ref[row + 1]
        store_field(start_ref, row, combine(lambda v: inside * v, load_field(adjoint_ref, row)))
    local_kernel(rows, link_set, start_ref, links_ref, sum_ref)


def local_kernel(rows, link_set, field_ref, links_ref, sum_ref):
    shape = field_ref.shape[-2:]
    x_pos = lax.broadcasted_iota(jnp.int32, shape, 1) % LX
    at_last = x_pos == LX - 1
    at_first = x_pos == 0

    for row in range(rows):
        here = load_field(field_ref, row)
        ahead = combine(lambda v: jnp.where(at_last, roll(v, LX - 1), roll(v, -1)), here)
        ahead_x, hop = transport(links_at(links_ref, row, link_set, 0), ahead, here)
        total = combine(
            lambda v, f, h: f + jnp.where(at_first, roll(h, 1 - LX), roll(h, 1)) - 8.0 * v, here, ahead_x, hop
        )
        ahead = combine(lambda v: roll(v, -LX), here)
        ahead_y, hop = transport(links_at(links_ref, row, link_set, 1), ahead, here)
        total = combine(lambda s, f, h: s + f + roll(h, LX), total, ahead_y, hop)
        if row > 0:
            total = combine(lambda s, h: s + h, total, earlier)
        if row < rows - 1:
            ahead_t, earlier = transport(links_at(links_ref, row, link_set, 3), load_field(field_ref, row + 1), here)
            total = combine(lambda s, f: s + f, total, ahead_t)
        store_field(sum_ref, row, total)


def arrived_sum(links_ref, link_set, row, rows, arrivals, coefs_ref=None):
    sum_ref, one_ref, two_ref, outer_ref, inner_ref = arrivals
    _, _, odd_plane, _ = place(rows)
    one, two = load_field(one_ref, row), load_field(two_ref, row)
    if coefs_ref is not None:
        below, above = (combine(lambda v: coefs_ref[row + 1] * v, f) for f in (one, two))
    else:
        below = combine(lambda near, far: jnp.where(odd_plane, near, far), one, two)
        above = combine(lambda near, far: jnp.where(odd_plane, far, near), one, two)
    ahead_z, _ = transport(links_at(links_ref, row, link_set, 2), above, None)
    total = combine(lambda s, f, h: s + f + h, load_field(sum_ref, row), ahead_z, below)
    return with_edges(links_ref, link_set, row, rows, total, outer_ref, inner_ref, coefs_ref)


def with_edges(links_ref, link_set, row, rows, total, outer_ref, inner_ref, coefs_ref=None):
    _, first_pos, _, odd_block = place(rows)
    outer, inner = load_field(outer_ref, 0), load_field(inner_ref, 0)
    if row == 0:
        exists = jnp.where(first_pos != 0, 1.0, 0.0)
        if coefs_ref is not None:
            exists = exists * coefs_ref[0]
        total = combine(lambda s, p, q: s + exists * jnp.where(odd_block, q, p), total, outer, inner)
    if row == rows - 1:
        exists = jnp.where(first_pos != BAND - rows, 1.0, 0.0)
        if coefs_ref is not None:
            exists = exists * coefs_ref[rows + 1]
        later = combine(lambda p, q: exists * jnp.where(odd_block, p, q), outer, inner)
        ahead_t, _ = transport(links_at(links_ref, row, link_set, 3), later, None)
        total = combine(lambda s, f: s + f, total, ahead_t)
    return total


def third_kernel(rows, coefs_ref, links_ref, *refs):
    arrivals, (third_ref, far_ref, near_ref, outer_ref, inner_ref) = refs[:5], refs[5:]
    for row in range(rows):
        inside = coefs_ref[row + 1]
        total = arrived_sum(links_ref, 2, row, rows, arrivals, coefs_ref)
        third = combine(lambda s: 0.75 * (inside * s), total)
        store_field(third_ref, row, third)
        store_z(rows, links_at(links_ref, row, 1, 2), row, third, far_ref, near_ref)
    store_t(rows, links_at(links_ref, rows - 1, 1, 3), third_ref, outer_ref, inner_ref)


def z_term(links_ref, link_set, row, field, from_above):
    ahead, _ = transport(links_at(links_ref, row, link_set, 2), field, None)
    return combine(lambda f, h: jnp.where(from_above, f, h), ahead, field)


def waiting_kernel(rows, links_ref, sum_ref, near_ref, outer_ref, inner_ref, total_ref):
    _, _, odd_plane, _ = place(rows)
    for row in range(rows):
        near = z_term(links_ref, 1, row, load_field(near_ref, row), ~odd_plane)
        total = combine(lambda s, f: s + f, load_field(sum_ref, row), near)
        store_field(total_ref, row, with_edges(links_ref, 1, row, rows, total, outer_ref, inner_ref))


def second_kernel(rows, eps_ref, coefs_ref, links_ref, *refs):
    total_ref, came_ref, start_ref, third_ref, mixed_ref, far_ref, near_ref, outer_ref, inner_ref, base_ref = refs
    _, _, odd_plane, _ = place(rows)
    eps = eps_ref[...]
    for row in range(rows):
        inside = coefs_ref[row + 1]
        far = z_term(links_ref, 1, row, load_field(came_ref, row), odd_plane)
        total = combine(lambda s, f: s + f, load_field(total_ref, row), far)
        third = combine(lambda v: eps * v, load_field(third_ref, row))
        second = combine(
            lambda v, s: v + (8.0 / 9.0) * (inside * (eps * (eps * s))), load_field(start_ref, row), total
        )
        mixed = combine(lambda p, q: 0.25 * p - (2.0 / 9.0) * q, second, third)
        store_field(mixed_ref, row, mixed)
        store_field(base_ref, row, combine(lambda p, q: p + q, second, third))
        store_z(rows, links_at(links_ref, row, 0, 2), row, mixed, far_ref, near_ref)
    store_t(rows, links_at(links_ref, rows - 1, 0, 3), mixed_ref, outer_ref, inner_ref)


def partial_kernel(
    rows, eps_ref, coefs_ref, links_ref, sum_ref, far_ref, outer_ref, inner_ref, base_ref, partial_ref
):
    _, _, odd_plane, _ = place(rows)
    for row in range(rows):
        inside, eps = coefs_ref[row + 1], eps_ref[...]
        far = z_term(links_ref, 0, row, load_field(far_ref, row), odd_plane)
        total = combine(lambda s, f: s + f, load_field(sum_ref, row), far)
        total = with_edges(links_ref, 0, row, rows, total, outer_ref, inner_ref)
        store_field(
            partial_ref, row, combine(lambda p, s: p + inside * (eps * s), load_field(base_ref, row), total)
        )


def last_kernel(rows, eps_ref, coefs_ref, links_ref, near_ref, partial_ref, out_hbm, out_ref, sems):
    _, _, odd_plane, _ = place(rows)
    copies = []
    for row in range(rows):
        inside, eps = coefs_ref[row + 1], eps_ref[...]
        near = z_term(links_ref, 0, row, load_field(near_ref, row), ~odd_plane)
        store_field(out_ref, row, combine(lambda p, s: p + inside * (eps * s), load_field(partial_ref, row), near))
        copies.append(pltpu.make_async_copy(out_ref.at[row], out_hbm.at[row], sems.at[row]))
        copies[-1].start()
    for copy in copies:
        copy.wait()


def call(kernel, name, operands, out_shapes, matvecs, space=pltpu.VMEM, scratch=(), out_space=pltpu.VMEM):
    out_spec = pl.BlockSpec(memory_space=out_space)
    return pl.pallas_call(
        kernel,
        name=name,
        out_shape=out_shapes,
        in_specs=[pl.BlockSpec(memory_space=space)] * len(operands),
        out_specs=jax.tree.map(lambda _: out_spec, out_shapes),
        scratch_shapes=scratch,
        cost_estimate=pl.CostEstimate(flops=matvecs * 72 * 1024, bytes_accessed=4096 * 18 * matvecs, transcendentals=0),
        compiler_params=pltpu.CompilerParams(vmem_limit_bytes=16 * 2**20),
    )(*operands)


def body(adjoint, flowed, source_slice, band_width, flow_steps):
    rows = adjoint.shape[0]
    per_plane = BAND // rows
    count = lax.axis_size("gz")
    links = jnp.transpose(flowed, (0, 1, 2, 4, 5, 3, 6)).reshape(-1, flowed.shape[-1])
    whole = jax.ShapeDtypeStruct(adjoint.shape, jnp.float32)
    one_row = jax.ShapeDtypeStruct((1,) + adjoint.shape[1:], jnp.float32)
    coefs_shape = jax.ShapeDtypeStruct((rows + 2,) + adjoint.shape[3:], jnp.float32)

    def in_plane(i, by):
        return i - i % per_plane + (i + by) % per_plane

    def in_line(i, by):
        return (i + by * per_plane) % count

    far_pairs = [(i, in_line(i, 1 if i // per_plane % 2 else -1)) for i in range(count)]
    near_pairs = [(i, in_line(i, -1 if i // per_plane % 2 else 1)) for i in range(count)]
    outer_pairs = [(i, in_plane(i, 1 if i % 2 else -1)) for i in range(count)]
    inner_pairs = [(i, in_plane(i, -1 if i % 2 else 1)) for i in range(count)]

    up_pairs = [(i, in_line(i, 1)) for i in range(count)]
    down_pairs = [(i, in_line(i, -1)) for i in range(count)]

    def sent_on(far, near, outer, inner, far_first):
        near = lax.ppermute(near, "gz", near_pairs)
        far = lax.ppermute(far, "gz", far_pairs)
        outer = lax.ppermute(outer, "gz", outer_pairs)
        inner = lax.ppermute(inner, "gz", inner_pairs)
        return (far, near, outer, inner) if far_first else (near, far, outer, inner)

    def shifted_on(up, down, outer, inner):
        below = lax.ppermute(up, "gz", up_pairs)
        above = lax.ppermute(down, "gz", down_pairs)
        outer = lax.ppermute(outer, "gz", outer_pairs)
        inner = lax.ppermute(inner, "gz", inner_pairs)
        return below, above, outer, inner

    def local(link_set, field):
        return call(functools.partial(local_kernel, rows, link_set), f"local_{link_set}", (field, links), whole, 22)

    sent = (whole, whole, one_row, one_row)
    copied = SETS * MUS * ENTRIES - (2 * MUS + 2) * ENTRIES // 8 * 8
    sending = call(
        functools.partial(begin_kernel, rows), "begin",
        tuple(pltpu.with_memory_space_constraint(a, pltpu.HBM) for a in (adjoint, links)), sent, 5, pltpu.HBM,
        [
            pltpu.VMEM(adjoint.shape, jnp.float32),
            pltpu.VMEM((rows, copied, flowed.shape[-1]), jnp.float32),
            pltpu.SemaphoreType.DMA((rows + 1,)),
        ],
    )
    arrived = shifted_on(*sending)
    coefs = call(
        functools.partial(taper_kernel, rows), "tapers", (source_slice, band_width), coefs_shape, 1, pltpu.SMEM
    )
    eps_shape = jax.ShapeDtypeStruct(adjoint.shape[3:], jnp.float32)
    eps = call(eps_kernel, "eps", (flow_steps,), eps_shape, 1, pltpu.SMEM)
    total, start = call(
        functools.partial(start_kernel, rows, 2), "start", (coefs, adjoint, links), (whole, whole), 22
    )
    third, *sending = call(
        functools.partial(third_kernel, rows), "third", (coefs, links, total) + arrived, (whole,) + sent, 10
    )
    near, far, outer, inner = sent_on(*sending, far_first=False)
    total = call(
        functools.partial(waiting_kernel, rows), "waiting", (links, local(1, third), near, outer, inner), whole, 5
    )
    mixed, *sending, base = call(
        functools.partial(second_kernel, rows), "second", (eps, coefs, links, total, far, start, third),
        (whole,) + sent + (whole,), 10,
    )
    far, near, outer, inner = sent_on(*sending, far_first=True)
    partial = call(
        functools.partial(partial_kernel, rows), "partial",
        (eps, coefs, links, local(0, mixed), far, outer, inner, base), whole, 5,
    )
    return call(
        functools.partial(last_kernel, rows), "last", (eps, coefs, links, near, partial), whole, 4,
        scratch=[pltpu.VMEM(adjoint.shape, jnp.float32), pltpu.SemaphoreType.DMA((rows,))], out_space=pltpu.HBM,
    )


def solution(mesh):
    in_specs = (
        P(("cfg", "gz"), None, None, None, None),
        P(("cfg", "gz"), None, None, None, None, None, None),
        P("cfg"),
        P("cfg"),
        P("cfg"),
    )
    out_specs = P(("cfg", "gz"), None, None, None, None)
    return jax.shard_map(body, mesh=mesh, in_specs=in_specs, out_specs=out_specs, check_vma=False)
```
